128 devices in a mesh: expert: 64 (over y, x, z), wshard: 2 (over core).
Axes of the slice: x: 4, y: 4, z: 4, core: 2. Of those that a mesh axis runs over, the one named last changes fastest.
Arguments:
- tokens: bfloat16 [16384, 768], P(('expert', 'wshard')), may hold values from -6 to 6
- lengths: int32 [32], replicated, may hold values from 1 to 1024, 16384 in all
- routes: int32 [16384, 1], P(('expert', 'wshard')), may hold values from 0 to 127; in each aligned block of 128 rows (0 to 127, 128 to 255, ...) at most 2 rows name the same one
- attn_gain: bfloat16 [768], P('wshard'), may hold values from 0.5 to 1.5
- query_weight: bfloat16 [768, 768], P('wshard'), may hold values from -0.21875 to 0.21875
- key_weight: bfloat16 [768, 768], P('wshard'), may hold values from -0.21875 to 0.21875
- value_weight: bfloat16 [768, 768], P('wshard'), may hold values from -0.21875 to 0.21875
- output_weight: bfloat16 [768, 768], P('wshard'), may hold values from -2.5 to 2.5
- bias_table: bfloat16 [32, 12], P('wshard'), may hold values from -6 to 6
- mix_gain: bfloat16 [768], P('wshard'), may hold values from 0.5 to 1.5
- router_weight: bfloat16 [768, 128], P('wshard'), may hold values from -0.109375 to 0.109375
- expert_in: bfloat16 [128, 768, 3072], P(('expert', 'wshard')), may hold values from -0.21875 to 0.21875
- expert_out: bfloat16 [128, 3072, 768], P(('expert', 'wshard')), may hold values from -14 to 14
- cotangent: bfloat16 [16384, 768], P(('expert', 'wshard')), may hold values from -6 to 6
Outputs:
- layer_out: bfloat16 [16384, 768], P(('expert', 'wshard'))
- tokens_grad: bfloat16 [16384, 768], P(('expert', 'wshard'))
- attn_gain_grad: float32 [768], P('wshard')
- query_grad: float32 [768, 768], P('wshard')
- key_grad: float32 [768, 768], P('wshard')
- value_grad: float32 [768, 768], P('wshard')
- output_grad: float32 [768, 768], P('wshard')
- bias_grad: float32 [32, 12], P('wshard')
- mix_gain_grad: float32 [768], P('wshard')
- router_grad: float32 [768, 128], P('wshard')
- expert_in_grad: bfloat16 [128, 768, 3072], P(('expert', 'wshard'))
- expert_out_grad: bfloat16 [128, 3072, 768], P(('expert', 'wshard'))
The draws below stay inside these ranges and needn't reach their ends.
Inputs may be any that keep to these rules, and one draw needn't show every extreme that they name: `routes`: among the rows of one device (128 aligned rows) no expert is named more than 2 times, a bound that some block reaches. The lengths sum to 16384, and the longest is exactly 1024.
All inputs are finite; a program needn't handle non-finite values.
Results may differ from the reference program's by a relative error of at most 0.018.
Values may be sent and summed in bfloat16 or wider, within the bound.
A program may use at most 192 MiB of HBM per device.

```python
import math
import jax
import jax.numpy as jnp
import numpy as np
from jax import lax

D = 768
HEADS = 12
HEAD = 64
FF = 3072
NB = 32
TOK_DEV = 128
SPAN_DEV = 8
MAXLEN = 1024
EXPERTS = 128
CAP = 2
TOKENS = 16384
SEQS = 32


def shard_levels(key, shape, shards, smallest, top_value):
    level = 1.0
    for dim, parts in shards:
        draws = jax.random.uniform(jax.random.fold_in(jax.random.fold_in(key, 6), dim), (parts,), jnp.float32, smallest / len(shards), top_value / len(shards))
        level = level * jnp.repeat(jnp.exp(draws), shape[dim] // parts).reshape((-1,) + (1,) * (len(shape) - 1 - dim))
    return level


def length_profile(number_of, total, bound, slope):
    weights = [(1 << 20) // math.isqrt(rank ** slope) + 1 for rank in range(2, number_of + 1)]
    spare, holding = total - bound - (number_of - 1), [1] * (number_of - 1)
    while spare > 0:
        candidates = [i for i in range(number_of - 1) if holding[i] < bound]
        mass, left = sum([weights[i] for i in candidates]), spare
        for i in candidates:
            more = min(bound - holding[i], max(1, left * weights[i] // mass), spare)
            holding[i] = holding[i] + more
            spare = spare - more
    return np.array([bound] + holding)


def ragged_sizes(stream_key, amount, total, limit, lean):
    if amount == 2:
        one = jax.random.randint(stream_key, (), max(1, total - limit), min(limit, total - 1) + 1)
        return jnp.stack([one, total - one])
    sizes = jnp.asarray(length_profile(amount, total, limit, lean), jnp.int32)
    couples = (amount - 1) // 2
    donor, receiver = sizes[1:1 + 2 * couples:2], sizes[2:2 + 2 * couples:2]
    room = jnp.minimum(donor - 1, limit - receiver)
    moved = jax.random.randint(jax.random.fold_in(stream_key, 1), (couples,), 0, 1 << 20) % (room + 1)
    sizes = sizes.at[1:1 + 2 * couples:2].set(donor - moved).at[2:2 + 2 * couples:2].set(receiver + moved)
    return sizes[jax.random.permutation(jax.random.fold_in(stream_key, 2), amount)]


def shared_out(own_key, own, number, rows, count, top, bound, skew):
    sequence = jax.random.permutation(own_key, count)
    crowded, common = load_shares(count, rows * top, bound, skew, True), load_shares(count, rows * top, bound, skew, False)
    places = jnp.arange(count)

    def named(tallies, offset_by):
        used = int((tallies > 0).sum())
        fixed = max(1, used // 4)
        shifted = fixed + (places - fixed + offset_by * (used - fixed)) % max(1, count - fixed)
        return jnp.zeros((count,), jnp.int32).at[sequence[jnp.where(places < fixed, places, shifted)]].set(jnp.asarray(tallies, jnp.int32))

    tallies = jnp.where(number % 4 == 0, named(crowded, number // 4), named(common, number - number // 4 - 1))
    mixed = jax.random.permutation(jax.random.fold_in(own, 3), count)
    giver, taker = mixed[0:count // 2 * 2:2], mixed[1:count // 2 * 2:2]
    room = jnp.minimum(tallies[giver] - 1, bound - tallies[taker]) // 2
    room = jnp.where((giver == sequence[0]) | (taker == sequence[0]) | (tallies[taker] == 0), 0, jnp.maximum(room, 0))
    shifted = jax.random.randint(jax.random.fold_in(own, 4), (count // 2,), 0, 1 << 20) % (room + 1)
    tallies = tallies.at[giver].add(-shifted).at[taker].add(shifted)
    members = jnp.searchsorted(jnp.cumsum(tallies), jnp.arange(rows * top), side="right").astype(jnp.int32)
    grid = members.reshape(top, rows).T
    grid = grid[jax.random.permutation(jax.random.fold_in(own, 1), rows)]
    offset_by = jax.random.randint(jax.random.fold_in(own, 2), (rows, 1), 0, top)
    return jnp.take_along_axis(grid, (jnp.arange(top)[None, :] + offset_by) % top, axis=1)


def load_shares(count, total, limit, slope, full):
    weights = [(1 << 20) // math.isqrt(grade ** slope) + 1 for grade in range(1, count + 1)]
    largest = limit if full else min(limit, max(-(-total // count), total * weights[0] // sum(weights)))
    least = 1 if total - largest >= count - 1 else 0
    counts, rest = [largest] + [least] * (count - 1), total - largest - least * (count - 1)
    while rest > 0:
        candidates = [i for i in range(1, count) if counts[i] < largest] or [i for i in range(1, count) if counts[i] < limit]
        pool, budget = sum([weights[i] for i in candidates]), rest
        for i in candidates:
            extra = min(limit - counts[i], max(1, budget * weights[i] // pool), rest)
            counts[i] = counts[i] + extra
            rest = rest - extra
    return np.array(counts)


def gaussian(own_key, extent, spread, limit, cuts=(), kind=jnp.bfloat16):
    array = jax.random.normal(own_key, extent, jnp.float32) * spread
    if len(cuts) > 0:
        array = shard_levels(own_key, extent, cuts, -0.22, 0.18) * array
    return jnp.clip(array, min=-limit, max=limit).astype(kind)


def setup_inputs(seed: int = 0) -> dict:
    seeds = jax.random.split(jax.random.key(seed), 15)
    tokens = gaussian(seeds[0], (TOKENS, D), 1.0, 6.0, ((0, 128),))
    lengths = ragged_sizes(seeds[1], SEQS, TOKENS, MAXLEN, 2).astype(jnp.int32)
    routes_keys = jax.random.split(jax.random.fold_in(seeds[2], 1), TOKENS // TOK_DEV)
    routes_turns = jax.random.permutation(jax.random.fold_in(seeds[2], 3), TOKENS // TOK_DEV)
    routes = jax.vmap(lambda own, number: shared_out(jax.random.fold_in(seeds[2], 2), own, number, TOK_DEV, EXPERTS, 1, CAP, 2))(routes_keys, routes_turns).reshape((TOKENS, 1))
    attn_gain = jnp.clip(1.0 + 0.1 * jax.random.normal(seeds[3], (D,), jnp.float32), 0.5, 1.5).astype(jnp.bfloat16)
    query_weight = gaussian(seeds[4], (D, D), D ** -0.5, 0.21875, ((0, 2),))
    key_weight = gaussian(seeds[5], (D, D), D ** -0.5, 0.21875, ((0, 2),))
    value_weight = gaussian(seeds[6], (D, D), D ** -0.5, 0.21875, ((0, 2),))
    output_weight = gaussian(seeds[7], (D, D), (max(1, D // 128)) ** -0.5, 2.5, ((0, 2),))
    bias_table = gaussian(seeds[8], (NB, HEADS), 1.0, 6.0, ((0, 2),))
    mix_gain = jnp.clip(1.0 + 0.1 * jax.random.normal(seeds[9], (D,), jnp.float32), 0.5, 1.5).astype(jnp.bfloat16)
    router_weight = gaussian(seeds[10], (D, EXPERTS), (9 * D // 2) ** -0.5, 0.109375, ((0, 2),))
    expert_in = gaussian(seeds[11], (EXPERTS, D, FF), D ** -0.5, 0.21875, ((0, 128),))
    expert_out = gaussian(seeds[12], (EXPERTS, FF, D), (EXPERTS * FF ** -0.5), 14.0, ((0, 128),))
    cotangent = gaussian(seeds[13], (TOKENS, D), 1.0, 6.0, ((0, 128),))
    return {"tokens": tokens, "lengths": lengths, "routes": routes, "attn_gain": attn_gain, "query_weight": query_weight, "key_weight": key_weight, "value_weight": value_weight, "output_weight": output_weight, "bias_table": bias_table, "mix_gain": mix_gain, "router_weight": router_weight, "expert_in": expert_in, "expert_out": expert_out, "cotangent": cotangent}


@jax.custom_vjp
def low(v):
    return lax.optimization_barrier(v.astype(jnp.bfloat16)).astype(jnp.float32)

@jax.custom_vjp
def low_back(v):
    return v

def low_keep(v):
    return (low(v), None)

def low_pass(kept, grad):
    return (grad,)

def back_keep(v):
    return (v, None)

def back_low(kept, grad):
    return (low(grad),)
low.defvjp(low_keep, low_pass)
low_back.defvjp(back_keep, back_low)
epsilon = 1e-06
far_edges = (12, 16, 23, 32, 46, 64, 91)

def rms_scale(values, gain):
    return values * lax.rsqrt(lax.optimization_barrier(jnp.mean(values * values, axis=-1, keepdims=True)) + epsilon) * gain

def bucket_of(relative):
    distance = jnp.abs(relative)
    far_bucket = 8 + sum(((distance >= edge).astype(jnp.int32) for edge in far_edges))
    near_far = jnp.where(distance < 8, distance, far_bucket)
    return near_far + 16 * (relative > 0).astype(jnp.int32)

def segment_ids(positions, seq_ends, total_rows):
    counted = lax.optimization_barrier(jnp.sum((seq_ends[None, :] <= positions[:, None]).astype(jnp.int32), axis=1))
    return jnp.where((positions >= 0) & (positions < total_rows), counted, -1)

def matmul(left, right):
    return jnp.dot(left, right, precision=lax.Precision.HIGHEST)

def reference(tokens, lengths, routes, attn_gain, query_weight, key_weight, value_weight, output_weight, bias_table, mix_gain, router_weight, expert_in, expert_out, cotangent):
    highest = lax.Precision.HIGHEST
    block_count = TOKENS // TOK_DEV
    window_rows = (2 * SPAN_DEV + 1) * TOK_DEV
    margin = SPAN_DEV * TOK_DEV
    seq_ends = jnp.cumsum(lengths).astype(jnp.int32)
    route_ids = routes[:, 0].astype(jnp.int32)
    chosen = route_ids[:, None] == jnp.arange(EXPERTS, dtype=jnp.int32)[None, :]
    running = jnp.cumsum(chosen.astype(jnp.int32).reshape(block_count, TOK_DEV, EXPERTS), axis=1).reshape(TOKENS, EXPERTS)
    slot_rank = lax.optimization_barrier(jnp.sum(jnp.where(chosen, running, 0), axis=1)) - 1
    owner_block = jnp.arange(TOKENS, dtype=jnp.int32) // TOK_DEV
    slot_index = ((route_ids * block_count + owner_block) * CAP + slot_rank).astype(jnp.int32)
    source_rows = jnp.full((EXPERTS * block_count * CAP,), TOKENS, jnp.int32)
    source_rows = source_rows.at[slot_index].set(jnp.arange(TOKENS, dtype=jnp.int32)).reshape(EXPERTS, block_count * CAP)

    def forward(inputs, gain_one, weight_query, weight_key, weight_value, weight_output, table_full, gain_two, weight_router, weight_in, weight_out):
        normed = low(rms_scale(inputs, gain_one))
        query_rows = low(low_back(matmul(normed, weight_query)))
        key_rows = low(low_back(matmul(normed, weight_key)))
        value_rows = low(low_back(matmul(normed, weight_value)))
        key_padded = jnp.pad(key_rows, ((margin, margin), (0, 0)))
        value_padded = jnp.pad(value_rows, ((margin, margin), (0, 0)))
        table_rows = table_full.T

        def attend_block(block_index):
            start = block_index * TOK_DEV
            query_block = lax.dynamic_slice_in_dim(query_rows, start, TOK_DEV, 0).reshape(TOK_DEV, HEADS, HEAD)
            key_block = lax.dynamic_slice_in_dim(key_padded, start, window_rows, 0).reshape(window_rows, HEADS, HEAD)
            value_block = lax.dynamic_slice_in_dim(value_padded, start, window_rows, 0).reshape(window_rows, HEADS, HEAD)
            query_pos = start + jnp.arange(TOK_DEV, dtype=jnp.int32)
            key_pos = start - margin + jnp.arange(window_rows, dtype=jnp.int32)
            raw = jnp.einsum('qhe,khe->hqk', query_block, key_block, precision=highest) * HEAD ** (-0.5)
            buckets = bucket_of(key_pos[None, :] - query_pos[:, None])
            raw = low_back(raw + jnp.take(table_rows, buckets, axis=1))
            allowed = segment_ids(query_pos, seq_ends, TOKENS)[:, None] == segment_ids(key_pos, seq_ends, TOKENS)[None, :]
            probs = low(jax.nn.softmax(jnp.where(allowed[None], raw, -1000000000.0), axis=-1))
            head_rows = jnp.einsum('hqk,khe->qhe', probs, value_block, precision=highest)
            return low(low_back(head_rows)).reshape(TOK_DEV, D)
        attended = lax.map(jax.checkpoint(attend_block), jnp.arange(block_count, dtype=jnp.int32)).reshape(TOKENS, D)
        hidden = inputs + low_back(matmul(attended, weight_output))
        mixed = low(rms_scale(hidden, gain_two))
        logits = low_back(matmul(mixed, weight_router))
        router = jax.nn.softmax(logits, axis=-1)
        gate_value = lax.optimization_barrier(jnp.sum(jnp.where(chosen, router, 0.0), axis=1))
        padded_rows = jnp.concatenate([mixed, jnp.zeros((1, D), mixed.dtype)], axis=0)
        expert_rows = padded_rows[source_rows]

        def expert_block(pieces):
            rows_in, block_in, block_out = pieces
            pre_act = low_back(matmul(rows_in, block_in))
            act_rows = low(jax.nn.gelu(pre_act, approximate=False))
            return low(low_back(matmul(act_rows, block_out)))
        made = lax.map(jax.checkpoint(expert_block), (expert_rows, weight_in, weight_out))
        returned = made.reshape(EXPERTS * block_count * CAP, D)[slot_index]
        return hidden + gate_value[:, None] * returned
    primals = tuple((array_in.astype(jnp.float32) for array_in in (tokens, attn_gain, query_weight, key_weight, value_weight, output_weight, bias_table, mix_gain, router_weight, expert_in, expert_out)))
    result, pullback = jax.vjp(forward, *primals)
    grads = pullback(cotangent.astype(jnp.float32))
    return (result.astype(jnp.bfloat16), grads[0].astype(jnp.bfloat16), grads[1], grads[2], grads[3], grads[4], grads[5], grads[6], grads[7], grads[8], grads[9].astype(jnp.bfloat16), grads[10].astype(jnp.bfloat16))
```

```python
import jax
import jax.numpy as jnp
from jax import lax
from jax.experimental import pallas as pl
from jax.experimental.pallas import tpu as pltpu
from jax.sharding import PartitionSpec as P

MESH = pl.DeviceIdType.MESH
BF = jnp.bfloat16
F32 = jnp.float32
EPSILON = 1e-06
FAR_EDGES = (12, 16, 23, 32, 46, 64, 91)

D = 768
HALF = 384
HEAD = 64
TOK = 128
CHIP = 256
REACH = 4
SLOTS = 2 * REACH + 1
WIN = SLOTS * CHIP
MID = REACH * CHIP
TOTAL = 16384
EXPERTS = 128
NB = 32
FF = 3072
NEAR = 3 * CHIP
LOOP = 1024
VMEM_BYTES = 56 * 1024 * 1024

NT = (((1,), (1,)), ((), ()))
TN = (((0,), (0,)), ((), ()))
NN = (((1,), (0,)), ((), ()))


def mm(left, right, dims=NN):
    return lax.dot_general(left, right, dims, preferred_element_type=F32)


def bucket_of(relative):
    distance = jnp.abs(relative)
    far_bucket = 8 + sum(((distance >= edge).astype(jnp.int32) for edge in FAR_EDGES))
    near_far = jnp.where(distance < 8, distance, far_bucket)
    return near_far + 16 * (relative > 0).astype(jnp.int32)


def tile(ref, rows, start, width):
    return ref[rows, pl.ds(pl.multiple_of(start, 128), width)]


def window_kernel(tok, wq, wk, wv, wo, router, misc, qkv, normed, wqkv, wo_full, router_full, misc_full, win, send, recv, fsend, frecv, wsend, wrecv, local):
    e = lax.axis_index("expert")
    j = lax.axis_index("wshard")
    jp = 1 - j
    chips = lax.axis_size("expert")
    offsets = [m for k in range(1, REACH + 1) for m in (k, -k)]
    barrier = pltpu.get_barrier_semaphore()
    for m in offsets:
        pl.semaphore_signal(barrier, inc=1, device_id=(lax.rem(e + m + chips, chips), j), device_id_type=MESH)
    pl.semaphore_signal(barrier, inc=1, device_id=(e, jp), device_id_type=MESH)
    pl.semaphore_wait(barrier, len(offsets) + 1)

    def rows_of(slot, core):
        return win.at[pl.ds(pl.multiple_of(slot * CHIP + core * TOK, TOK), TOK), :]

    def remote(src, dst, ssem, rsem, chip, core):
        return pltpu.make_async_remote_copy(src_ref=src, dst_ref=dst, send_sem=ssem, recv_sem=rsem, device_id=(chip, core), device_id_type=MESH)

    copies = []
    for n, m in enumerate(offsets):
        copies.append(remote(tok, rows_of(REACH - m, j), send.at[n], recv.at[n], lax.rem(e + m + chips, chips), j))
    for c in copies:
        c.start()
    mine = pltpu.make_async_copy(tok, rows_of(REACH, j), local.at[0])
    mine.start()
    weights = []
    kept = []
    for n, w in enumerate((wq, wk, wv)):
        rows = pl.ds(pl.multiple_of(j * HALF, HALF), HALF)
        there = w.at[:, pl.ds(pl.multiple_of(jp * HALF, 128), HALF)]
        here = w.at[:, pl.ds(pl.multiple_of(j * HALF, 128), HALF)]
        dst = wqkv.at[rows, n * HALF : (n + 1) * HALF]
        weights.append(remote(there, dst, wsend.at[n], wrecv.at[n], e, jp))
        kept.append(pltpu.make_async_copy(here, dst, local.at[1 + n]))
    for n, (src, dst, size) in enumerate(((misc, misc_full, 24), (router, router_full, HALF), (wo, wo_full, HALF))):
        rows = pl.ds(pl.multiple_of(j * size, 8), size)
        weights.append(remote(src, dst.at[rows, :], wsend.at[3 + n], wrecv.at[3 + n], e, jp))
        kept.append(pltpu.make_async_copy(src, dst.at[rows, :], local.at[4 + n]))
    swap = remote(tok, rows_of(REACH, j), fsend.at[8], frecv.at[8], e, jp)
    weights[3].start()
    for c in weights[:3]:
        c.start()
    swap.start()
    for c in weights[4:]:
        c.start()
    for c in kept:
        c.start()
    mine.wait()
    for c in kept[:4]:
        c.wait()
    for c in weights[:4]:
        c.wait_recv()
    gain = jnp.concatenate([misc_full[16:17, :], misc_full[40:41, :]], axis=1)

    def project(slot):
        rows = slice(slot * CHIP, (slot + 1) * CHIP)
        x = win[rows, :].astype(F32)
        y = (x * lax.rsqrt(jnp.mean(x * x, axis=-1, keepdims=True) + EPSILON) * gain).astype(BF)
        if slot == REACH:
            normed[...] = y
        qkv[rows, :] = mm(y, wqkv[...]).astype(BF)

    def passed(n):
        return remote(rows_of(REACH - offsets[n], j), rows_of(REACH - offsets[n], j), fsend.at[n], frecv.at[n], e, jp)

    swap.wait_recv()
    project(REACH)
    for n in range(len(offsets) + 1):
        if n < len(offsets):
            copies[n].wait_recv()
            passed(n).start()
        if n > 0:
            passed(n - 1).wait_recv()
            project(REACH - offsets[n - 1])
    for c in kept[4:]:
        c.wait()
    for c in weights[4:]:
        c.wait_recv()
    for c in weights:
        c.wait_send()
    for c in copies:
        c.wait_send()
    swap.wait_send()
    for n in range(len(offsets)):
        passed(n).wait_send()


def window(tokens, wq, wk, wv, wo, router, misc):
    any_spec = pl.BlockSpec(memory_space=pl.ANY)
    vm = pl.BlockSpec(memory_space=pltpu.VMEM)
    return pl.pallas_call(
        window_kernel,
        name="window",
        out_shape=(
            jax.ShapeDtypeStruct((WIN, 3 * HALF), BF),
            jax.ShapeDtypeStruct((CHIP, D), BF),
            jax.ShapeDtypeStruct((D, 3 * HALF), BF),
            jax.ShapeDtypeStruct((D, D), BF),
            jax.ShapeDtypeStruct((D, EXPERTS), BF),
            jax.ShapeDtypeStruct((48, HALF), F32),
        ),
        in_specs=[any_spec] * 7,
        out_specs=(vm, vm, vm, any_spec, any_spec, vm),
        scratch_shapes=[
            pltpu.VMEM((WIN, D), BF),
            pltpu.SemaphoreType.DMA((8,)),
            pltpu.SemaphoreType.DMA((8,)),
            pltpu.SemaphoreType.DMA((9,)),
            pltpu.SemaphoreType.DMA((9,)),
            pltpu.SemaphoreType.DMA((6,)),
            pltpu.SemaphoreType.DMA((6,)),
            pltpu.SemaphoreType.DMA((7,)),
        ],
        compiler_params=pltpu.CompilerParams(collective_id=1, has_side_effects=True, vmem_limit_bytes=VMEM_BYTES),
    )(tokens, wq, wk, wv, wo, router, misc)


def prepare(lengths, misc, mask, diag, ways):
    e = lax.axis_index("expert")
    row_pos = (e - REACH) * CHIP + lax.broadcasted_iota(jnp.int32, (8, WIN), 1)
    col_pos = e * CHIP + lax.broadcasted_iota(jnp.int32, (CHIP, 128), 0)

    def count(n, state):
        end, rows, cols = state
        end = end + lengths[n]
        return end, rows + (row_pos >= end).astype(jnp.int32), cols + (col_pos >= end).astype(jnp.int32)

    zero = jnp.zeros((8, WIN), jnp.int32)
    _, rows, cols = lax.fori_loop(0, 32, count, (jnp.int32(0), zero, jnp.zeros((CHIP, 128), jnp.int32)))
    rows = jnp.where((row_pos >= 0) & (row_pos < TOTAL), rows, -1)
    for c in range(SLOTS):
        part = rows[0:1, c * CHIP : (c + 1) * CHIP]
        mask[:, c * CHIP : (c + 1) * CHIP] = jnp.where(cols[:, 0:1] == part, 0.0, -1e9).astype(F32)
    table = jnp.concatenate([misc[0:16, 0:128], misc[24:40, 0:128]], axis=0).astype(BF)
    for n, sign in enumerate(ways):
        hot = diagonal_buckets(sign)
        diag[n * 16 : (n + 1) * 16, :] = mm(table, hot.astype(BF), TN)[0:16]


def diagonal_buckets(sign):
    m = lax.broadcasted_iota(jnp.int32, (NB, LOOP), 1)
    r = jnp.where(m < NEAR, m, m - LOOP) - CHIP
    b = lax.broadcasted_iota(jnp.int32, (NB, LOOP), 0)
    return (bucket_of(sign * r) == b).astype(F32)


def biased(raw, c, mask, near, left, right):
    s = raw + mask[:, c * CHIP : (c + 1) * CHIP]
    if c < REACH - 1:
        return s + left
    if c > REACH + 1:
        return s + right
    lower = (c - REACH + 1) * CHIP
    return s + near[:, lower : lower + CHIP]


def near_tile(diag, row):
    line = diag[pl.ds(row, 1), :]
    spread = pltpu.roll(jnp.broadcast_to(line, (CHIP, LOOP)), 0, 1, stride=1, stride_axis=0)
    return spread[:, 0:NEAR], line[:, 0:1], line[:, NEAR - 1 : NEAR]


def chunk(c):
    return slice(c * CHIP, (c + 1) * CHIP)


def forward_kernel(lengths, qkv, misc, att, stat, mask, diag, scores, lse_cols):
    j = lax.axis_index("wshard")
    prepare(lengths, misc, mask, diag, (1,))
    lane = lax.broadcasted_iota(jnp.int32, (CHIP, 128), 1)
    lse_cols[...] = jnp.zeros((CHIP, 128), F32)

    def pair(p, carry):
        q = tile(qkv, slice(MID, MID + CHIP), p * 128, 128).astype(F32) * 0.125
        outs = []
        for hh in range(2):
            own = (lane // HEAD) == hh
            qm = jnp.where(own, q, 0.0).astype(BF)
            near, left, right = near_tile(diag, j * 6 + 2 * p + hh)
            top = None
            for c in range(SLOTS):
                k = tile(qkv, chunk(c), HALF + p * 128, 128)
                s = biased(mm(qm, k, NT), c, mask, near, left, right)
                scores[:, chunk(c)] = s
                top = s if top is None else jnp.maximum(top, s)
            top = jnp.max(top, axis=1, keepdims=True)
            total = jnp.zeros((CHIP, CHIP), F32)
            out = jnp.zeros((CHIP, 128), F32)
            for c in range(SLOTS):
                x = jnp.exp(scores[:, chunk(c)] - top)
                total = total + x
                out = out + mm(x.astype(BF), tile(qkv, chunk(c), 2 * HALF + p * 128, 128))
            total = jnp.sum(total, axis=1, keepdims=True)
            outs.append(out / total)
            lse_cols[...] = jnp.where(lane == 2 * p + hh, top + jnp.log(total), lse_cols[...])
        att[:, pl.ds(pl.multiple_of(p * 128, 128), 128)] = jnp.where(lane < HEAD, outs[0], outs[1]).astype(BF)
        return carry

    lax.fori_loop(0, 3, pair, 0)
    stat[...] = lse_cols[...].T[0:8, :]


def attention(lengths, qkv, misc):
    vm = pl.BlockSpec(memory_space=pltpu.VMEM)
    return pl.pallas_call(
        forward_kernel,
        name="attention",
        out_shape=(jax.ShapeDtypeStruct((CHIP, HALF), BF), jax.ShapeDtypeStruct((8, CHIP), F32)),
        in_specs=[pl.BlockSpec(memory_space=pltpu.SMEM), vm, vm],
        out_specs=(vm, vm),
        scratch_shapes=[
            pltpu.VMEM((CHIP, WIN), F32),
            pltpu.VMEM((16, LOOP), F32),
            pltpu.VMEM((CHIP, WIN), F32),
            pltpu.VMEM((CHIP, 128), F32),
        ],
        compiler_params=pltpu.CompilerParams(vmem_limit_bytes=VMEM_BYTES),
    )(lengths, qkv, misc)


def backward_kernel(lengths, qkv, dout, stat, misc, dqkv, bias, mask, diag, keys):
    j = lax.axis_index("wshard")
    prepare(lengths, misc, mask, diag, (1, -1))
    lane = lax.broadcasted_iota(jnp.int32, (CHIP, 128), 1)
    line = lax.broadcasted_iota(jnp.int32, (NB, 128), 1)
    row32 = lax.broadcasted_iota(jnp.int32, (NB, 128), 0)
    hot = diagonal_buckets(1)
    mid = slice(MID, MID + CHIP)
    cols = jnp.concatenate([stat[REACH], jnp.zeros((112, CHIP), F32)], axis=0).T
    bias[...] = jnp.zeros((NB, 128), F32)

    def pair(p, carry):
        q = tile(qkv, mid, p * 128, 128).astype(F32) * 0.125
        k_own = tile(qkv, mid, HALF + p * 128, 128)
        v_own = tile(qkv, mid, 2 * HALF + p * 128, 128)
        do = tile(dout, mid, p * 128, 128)
        dqs, dks, dvs = [], [], []
        for hh in range(2):
            h = 2 * p + hh
            own = (lane // HEAD) == hh
            spare = (1 - hh) * HEAD
            qm = jnp.where(own, q, 0.0).astype(BF)
            dom = jnp.where(own, do, jnp.zeros_like(do))
            lse = jnp.sum(jnp.where(lane == h, cols, 0.0), axis=1, keepdims=True)
            delta = jnp.sum(jnp.where(lane == h + 8, cols, 0.0), axis=1, keepdims=True)
            near, left, right = near_tile(diag, j * 6 + h)
            dq = jnp.zeros((CHIP, 128), F32)
            tiles = []
            for c in range(SLOTS):
                k = tile(qkv, chunk(c), HALF + p * 128, 128)
                v = tile(qkv, chunk(c), 2 * HALF + p * 128, 128)
                s = biased(mm(qm, k, NT), c, mask, near, left, right)
                ds = jnp.exp(s - lse) * (mm(dom, v, NT) - delta)
                low = ds.astype(BF)
                if c < REACH - 1:
                    other = jnp.where(lane == spare, 1.0, 0.0).astype(BF)
                elif c > REACH + 1:
                    other = jnp.where(lane == spare + 1, 1.0, 0.0).astype(BF)
                else:
                    other = jnp.zeros((CHIP, 128), BF)
                    tiles.append(ds)
                dq = dq + mm(low, jnp.where(own, k, other))
            dqs.append(dq * 0.125)
            fold = jnp.concatenate(tiles + [jnp.zeros((CHIP, CHIP), F32)], axis=1)
            rows = CHIP
            while rows > 8:
                rows //= 2
                fold = fold[0:rows] + pltpu.roll(fold[rows : 2 * rows], LOOP - rows, 1)
            summed = fold[0:1]
            for n in range(1, 8):
                summed = summed + pltpu.roll(fold[n : n + 1], LOOP - n, 1)
            by_bucket = jnp.sum(hot * summed, axis=1, keepdims=True)
            far = jnp.sum(dq, axis=0, keepdims=True)
            far_left = far[:, spare : spare + 1]
            far_right = far[:, spare + 1 : spare + 2]
            by_bucket = by_bucket + jnp.where(row32 == 15, far_left, 0.0) + jnp.where(row32 == 31, far_right, 0.0)
            bias[...] = jnp.where(line == j * 6 + h, by_bucket, bias[...])
            km = jnp.where(own, k_own, jnp.zeros_like(k_own))
            vm = jnp.where(own, v_own, jnp.zeros_like(v_own))
            near, left, right = near_tile(diag, 16 + j * 6 + h)
            dk = jnp.zeros((CHIP, 128), F32)
            dv = jnp.zeros((CHIP, 128), F32)
            for c in range(SLOTS):
                qc = (tile(qkv, chunk(c), p * 128, 128).astype(F32) * 0.125).astype(BF)
                dc = tile(dout, chunk(c), p * 128, 128)
                s = biased(mm(km, qc, NT), c, mask, near, left, right)
                lse_row = stat[c, pl.ds(h, 1), :]
                delta_row = stat[c, pl.ds(h + 8, 1), :]
                prob = jnp.exp(s - lse_row)
                ds = prob * (mm(vm, dc, NT) - delta_row)
                dv = dv + mm(prob.astype(BF), dc)
                dk = dk + mm(ds.astype(BF), qc)
            dks.append(dk)
            dvs.append(dv)
        for n, both in enumerate((dqs, dks, dvs)):
            dqkv[:, pl.ds(pl.multiple_of(n * HALF + p * 128, 128), 128)] = jnp.where(lane < HEAD, both[0], both[1]).astype(BF)
        return carry

    lax.fori_loop(0, 3, pair, 0)


def attention_back(lengths, qkv, dout, stat, misc):
    vm = pl.BlockSpec(memory_space=pltpu.VMEM)
    return pl.pallas_call(
        backward_kernel,
        name="attention_back",
        out_shape=(jax.ShapeDtypeStruct((CHIP, 3 * HALF), BF), jax.ShapeDtypeStruct((NB, 128), F32)),
        in_specs=[pl.BlockSpec(memory_space=pltpu.SMEM), vm, vm, vm, vm],
        out_specs=(vm, vm),
        scratch_shapes=[
            pltpu.VMEM((CHIP, WIN), F32),
            pltpu.VMEM((32, LOOP), F32),
            pltpu.VMEM((8, 128), F32),
        ],
        compiler_params=pltpu.CompilerParams(vmem_limit_bytes=VMEM_BYTES),
    )(lengths, qkv, dout, stat, misc)


def spread_kernel(dout, stat, dout_win, stat_win, send, recv, local):
    e = lax.axis_index("expert")
    j = lax.axis_index("wshard")
    chips = lax.axis_size("expert")
    offsets = [m for k in range(1, REACH + 1) for m in (k, -k)]
    barrier = pltpu.get_barrier_semaphore()
    for m in offsets:
        pl.semaphore_signal(barrier, inc=1, device_id=(lax.rem(e + m + chips, chips), j), device_id_type=MESH)
    pl.semaphore_wait(barrier, len(offsets))
    copies = []
    for n, m in enumerate(offsets):
        slot = REACH - m
        for i, (src, dst) in enumerate(((dout, dout_win.at[slot * CHIP : (slot + 1) * CHIP, :]), (stat, stat_win.at[slot]))):
            copies.append(
                pltpu.make_async_remote_copy(
                    src_ref=src,
                    dst_ref=dst,
                    send_sem=send.at[2 * n + i],
                    recv_sem=recv.at[2 * n + i],
                    device_id=(lax.rem(e + m + chips, chips), j),
                    device_id_type=MESH,
                )
            )
    for c in copies:
        c.start()
    kept = [
        pltpu.make_async_copy(dout, dout_win.at[MID : MID + CHIP, :], local.at[0]),
        pltpu.make_async_copy(stat, stat_win.at[REACH], local.at[1]),
    ]
    for c in kept:
        c.start()
    for c in kept + copies:
        c.wait()


def spread(dout, stat):
    any_spec = pl.BlockSpec(memory_space=pl.ANY)
    return pl.pallas_call(
        spread_kernel,
        name="spread",
        out_shape=(jax.ShapeDtypeStruct((WIN, HALF), BF), jax.ShapeDtypeStruct((SLOTS, 16, CHIP), F32)),
        in_specs=[any_spec] * 2,
        out_specs=(any_spec, any_spec),
        scratch_shapes=[
            pltpu.SemaphoreType.DMA((16,)),
            pltpu.SemaphoreType.DMA((16,)),
            pltpu.SemaphoreType.DMA((2,)),
        ],
        compiler_params=pltpu.CompilerParams(collective_id=2, has_side_effects=True),
    )(dout, stat)


FF_TILE = 512


def expert_kernel(x, g, w_in, w_out, made, back, d_in, d_out, made_sum, back_sum):
    step = pl.program_id(0)

    @pl.when(step == 0)
    def _():
        made_sum[...] = jnp.zeros_like(made_sum)
        back_sum[...] = jnp.zeros_like(back_sum)

    pre = mm(x[...], w_in[0])
    half_erf = 0.5 * lax.erf(pre * (0.5**0.5)) + 0.5
    act = (pre * half_erf).astype(BF)
    slope = half_erf + pre * jnp.exp(-0.5 * pre * pre) * (0.5 * 0.7978845608028654)
    act_grad = mm(g[...], w_out[0], NT)
    pre_grad = (act_grad * slope).astype(BF)
    made_sum[...] += mm(act, w_out[0])
    back_sum[...] += mm(pre_grad, w_in[0], NT)
    d_out[0] = mm(act, g[...], TN).astype(BF)
    d_in[0] = mm(x[...], pre_grad, TN).astype(BF)

    @pl.when(step == pl.num_programs(0) - 1)
    def _():
        made[...] = made_sum[...].astype(BF)
        back[...] = back_sum[...].astype(BF)


def expert(x, g, w_in, w_out):
    rows = x.shape[0]
    whole = pl.BlockSpec((rows, D), lambda f: (0, 0))
    by_in = pl.BlockSpec((1, D, FF_TILE), lambda f: (0, 0, f))
    by_out = pl.BlockSpec((1, FF_TILE, D), lambda f: (0, f, 0))
    return pl.pallas_call(
        expert_kernel,
        name="expert",
        grid=(FF // FF_TILE,),
        out_shape=(
            jax.ShapeDtypeStruct((rows, D), BF),
            jax.ShapeDtypeStruct((rows, D), BF),
            jax.ShapeDtypeStruct((1, D, FF), BF),
            jax.ShapeDtypeStruct((1, FF, D), BF),
        ),
        in_specs=[whole, whole, by_in, by_out],
        out_specs=(whole, whole, by_in, by_out),
        scratch_shapes=[pltpu.VMEM((rows, D), F32), pltpu.VMEM((rows, D), F32)],
        compiler_params=pltpu.CompilerParams(vmem_limit_bytes=VMEM_BYTES, dimension_semantics=("arbitrary",)),
    )(x, g, w_in, w_out)


ORDERS = ("zxy", "xyz", "yzx")
UNITS = (4, 3, 4)


def halves(i):
    while i[0] < i[1]:
        unit, place = divmod(i[0], 64)
        n = min(64 - place, i[1] - i[0])
        yield unit, place, n
        i = (i[0] + n, i[1])


def qkv_places(c):
    if c == 8:
        return [(2, None, 0, 24, 0)]
    done, found = 0, []
    for unit, place, n in halves((24 * c, 24 * c + 24)):
        found.append((0, unit, place, n, done) if unit < 2 else (1, None, place, n, done))
        done += n
    return found


def out_places(c):
    done, found = 0, []
    for unit, place, n in halves((24 * c, 24 * c + 24)):
        found.append(((1, 2), (2, 0), (2, 3))[unit] + (place, n, done))
        done += n
    return found


def tail_kernel(dqkv, normed, wqkv, tok, hidden_grad, att, branch, mixed, logit_grad, mix_grad, bias, misc, tokens_grad, q_sum, k_sum, v_sum, out_sum, router_sum, bias_sum, gain_sum, part_a, part_b, part_c, in1a, in1b, in1c, in2a, in2b, in2c, in3a, in3b, in3c, red1a, red1b, red1c, red2a, red2b, red2c, red3a, red3b, red3c, all_a, all_b, all_c, half_out, half_in, rs_send, rs_recv, ag_send, ag_recv, core_send, core_recv):
    e = lax.axis_index("expert")
    j = lax.axis_index("wshard")
    jp = 1 - j
    parts, into = (part_a, part_b, part_c), ((in1a, in1b, in1c), (in2a, in2b, in2c), (in3a, in3b, in3c))
    reds, alls = ((red1a, red1b, red1c), (red2a, red2b, red2c), (red3a, red3b, red3c)), (all_a, all_b, all_c)
    stride = {"y": 16, "x": 4, "z": 1}
    coord = {a: lax.rem(e // s, 4) for a, s in stride.items()}

    def peer(axis, d):
        c = coord[axis]
        return e + (lax.rem(c + d, 4) - c) * stride[axis]

    barrier = pltpu.get_barrier_semaphore()
    for axis in "zxy":
        for d in (1, 2, 3):
            pl.semaphore_signal(barrier, inc=1, device_id=(peer(axis, d), j), device_id_type=MESH)
    pl.semaphore_signal(barrier, inc=1, device_id=(e, jp), device_id_type=MESH)
    pl.semaphore_wait(barrier, 10)

    def remote(src, dst, ssem, rsem, chip, core):
        return pltpu.make_async_remote_copy(src_ref=src, dst_ref=dst, send_sem=ssem, recv_sem=rsem, device_id=(chip, core), device_id_type=MESH)

    there = pl.ds(pl.multiple_of(jp * TOK, TOK), TOK)
    here = pl.ds(pl.multiple_of(j * TOK, TOK), TOK)
    half_out[...] = mm(dqkv[there, :], wqkv[...], NT).astype(BF)
    trade = remote(half_out, half_in, core_send.at[0], core_recv.at[0], e, jp)
    trade.start()

    def reduce_copies(n, phase):
        src = parts[n] if phase == 0 else reds[phase - 1][n]
        axis, size = ORDERS[n][phase], (16, 4, 1)[phase]
        copies = []
        for d in (1, 2, 3):
            place = lax.rem(coord[axis] + d, 4) * size
            copies.append(remote(src.at[:, pl.ds(place, size)], into[phase][n].at[d - 1], rs_send.at[n, phase, d - 1], rs_recv.at[n, phase, d - 1], peer(axis, d), j))
        return copies

    def gather_copies(n, phase):
        size = (1, 4, 16)[phase]
        one, two, three = (coord[a] for a in ORDERS[n])
        place = (one * 16 + two * 4 + three, one * 16 + two * 4, one * 16)[phase]
        ref = alls[n].at[:, pl.ds(place, size)]
        axis = ORDERS[n][2 - phase]
        return [remote(ref, ref, ag_send.at[n, phase, d - 1], ag_recv.at[n, phase, d - 1], peer(axis, d), j) for d in (1, 2, 3)]

    def fill(ref, unit, place, value):
        ref[unit, place : place + value.shape[0]] = value

    def tiles(value):
        return value.astype(BF).reshape(value.shape[0] // 16, 16, 128)

    for third in range(3):
        grad = mm(normed[...], dqkv[:, third * HALF : (third + 1) * HALF], TN)
        for c in range(3 * third, 3 * third + 3):
            cut = tiles(grad[:, (c % 3) * 128 : (c % 3 + 1) * 128])
            for h in range(2):
                for n, unit, place, count, first in qkv_places(c):
                    unit = (2 * h + unit if n == 0 else h if n == 1 else 1 + h)
                    fill(parts[n], unit, place, cut[24 * h + first : 24 * h + first + count])
        if third == 1:
            started = {(0, 0): reduce_copies(0, 0)}
            for c in started[0, 0]:
                c.start()
    grad = mm(att[...], branch[...], TN)
    for c in range(6):
        cut = tiles(grad[:, c * 128 : (c + 1) * 128])
        for n, unit, place, count, first in out_places(c):
            fill(parts[n], unit, place, cut[first : first + count])
    started[1, 0] = reduce_copies(1, 0)
    for c in started[1, 0]:
        c.start()
    grad = tiles(mm(mixed[...], logit_grad[...], TN))
    for h in range(2):
        fill(part_c, 1 + h, 24, grad[24 * h : 24 * h + 24])
        part_c[1 + h, 50:64] = jnp.zeros((14, 16, 128), BF)
    fill(part_c, 1, 48, tiles(bias[0:16, :]))
    fill(part_c, 2, 48, tiles(bias[16:32, :]))
    part_c[3, 16:64] = jnp.zeros((48, 16, 128), BF)

    own_half = mm(dqkv[here, :], wqkv[...], NT)
    trade.wait_recv()
    grad = own_half + half_in[...].astype(F32)
    x = tok[...].astype(F32)
    gain = jnp.concatenate([misc[16:17, :], misc[40:41, :]], axis=1)
    r = lax.rsqrt(jnp.mean(x * x, axis=-1, keepdims=True) + EPSILON)
    w = grad * gain
    tokens_grad[...] = (hidden_grad[...] + r * w - x * (r * r * r * jnp.mean(w * x, axis=-1, keepdims=True))).astype(BF)
    attn_gain = jnp.sum(grad * x * r, axis=0, keepdims=True)
    for h in range(2):
        lines = [v[:, h * HALF + 128 * n : h * HALF + 128 * n + 128] for v in (attn_gain, mix_grad[0:1, :]) for n in range(3)]
        fill(part_c, 1 + h, 49, tiles(jnp.concatenate(lines + [jnp.zeros((10, 128), F32)], axis=0)))
    started[2, 0] = reduce_copies(2, 0)
    for c in started[2, 0]:
        c.start()

    for phase in range(3):
        for n in range(3):
            for c in started[n, phase]:
                c.wait_recv()
            size = (16, 4, 1)[phase]
            src = parts[n] if phase == 0 else reds[phase - 1][n]
            place = coord[ORDERS[n][phase]] * size
            for u in range(UNITS[n]):
                total = src[u, pl.ds(place, size)].astype(F32)
                for d in range(3):
                    total = total + into[phase][n][d, u].astype(F32)
                reds[phase][n][u] = total.astype(BF)
            if phase < 2:
                started[n, phase + 1] = reduce_copies(n, phase + 1)
                for c in started[n, phase + 1]:
                    c.start()

    spots = [lax.rem(e // stride[o[0]], 4) * 16 + lax.rem(e // stride[o[1]], 4) * 4 + lax.rem(e // stride[o[2]], 4) for o in ORDERS]
    swaps = [
        remote(red3a.at[pl.ds(2 * jp, 2)], all_a.at[2:4, pl.ds(spots[0], 1)], core_send.at[1], core_recv.at[1], e, jp),
        remote(red3b.at[pl.ds(jp, 1)], all_b.at[1:2, pl.ds(spots[1], 1)], core_send.at[2], core_recv.at[2], e, jp),
        remote(red3c.at[pl.ds(1 + jp, 1)], all_c.at[2:3, pl.ds(spots[2], 1)], core_send.at[3], core_recv.at[3], e, jp),
    ]
    for c in swaps:
        c.start()
    all_a[0:2, pl.ds(spots[0], 1)] = red3a[pl.ds(2 * j, 2)]
    all_b[0:1, pl.ds(spots[1], 1)] = red3b[pl.ds(j, 1)]
    all_b[2:3, pl.ds(spots[1], 1)] = red3b[2:3]
    all_c[0:1, pl.ds(spots[2], 1)] = red3c[0:1]
    all_c[1:2, pl.ds(spots[2], 1)] = red3c[pl.ds(1 + j, 1)]
    all_c[3:4, pl.ds(spots[2], 1)] = red3c[3:4]
    gathers = {}
    for n in range(3):
        swaps[n].wait_recv()
        gathers[n, 0] = gather_copies(n, 0)
        for c in gathers[n, 0]:
            c.start()
    for phase in range(2):
        for n in range(3):
            for c in gathers[n, phase]:
                c.wait_recv()
            gathers[n, phase + 1] = gather_copies(n, phase + 1)
            for c in gathers[n, phase + 1]:
                c.start()
    for n in range(3):
        for c in gathers[n, 2]:
            c.wait_recv()

    def rows(value):
        return value.reshape(value.shape[0] * 16, 128)

    sums = (q_sum, k_sum, v_sum)
    for c in range(9):
        for who, core in ((0, j), (1, jp)):
            column = pl.ds(pl.multiple_of(core * HALF + (c % 3) * 128, 128), 128)
            for n, unit, place, count, first in qkv_places(c):
                unit = (2 * who + unit if n == 0 else who if n == 1 else 1 + who)
                sums[c // 3][16 * first : 16 * (first + count), column] = rows(alls[n][unit, place : place + count])
    for c in range(6):
        for n, unit, place, count, first in out_places(c):
            out_sum[16 * first : 16 * (first + count), c * 128 : (c + 1) * 128] = rows(alls[n][unit, place : place + count])
    both = all_c[1, 24:50].astype(F32) + all_c[2, 24:50].astype(F32)
    router_sum[...] = rows(both[0:24])
    bias_sum[...] = both[24]
    gain_sum[...] = both[25]

    trade.wait_send()
    for c in swaps:
        c.wait_send()
    for copies in list(started.values()) + list(gathers.values()):
        for c in copies:
            c.wait_send()


def tail(*operands):
    vm = pl.BlockSpec(memory_space=pltpu.VMEM)

    def tiled(*lead):
        return [pltpu.VMEM(lead[:1] + (u,) + lead[1:] + (16, 128), BF) if len(lead) == 2 else pltpu.VMEM((u,) + lead + (16, 128), BF) for u in UNITS]

    return pl.pallas_call(
        tail_kernel,
        name="tail",
        out_shape=(
            jax.ShapeDtypeStruct((TOK, D), BF),
            jax.ShapeDtypeStruct((HALF, D), BF),
            jax.ShapeDtypeStruct((HALF, D), BF),
            jax.ShapeDtypeStruct((HALF, D), BF),
            jax.ShapeDtypeStruct((HALF, D), BF),
            jax.ShapeDtypeStruct((HALF, EXPERTS), F32),
            jax.ShapeDtypeStruct((16, 128), F32),
            jax.ShapeDtypeStruct((16, 128), F32),
        ),
        in_specs=[vm] * 12,
        out_specs=(vm,) * 8,
        scratch_shapes=[
            *tiled(64),
            *tiled(3, 16),
            *tiled(3, 4),
            *tiled(3, 1),
            *tiled(16),
            *tiled(4),
            *tiled(1),
            *tiled(64),
            pltpu.VMEM((TOK, D), BF),
            pltpu.VMEM((TOK, D), BF),
            pltpu.SemaphoreType.DMA((3, 3, 3)),
            pltpu.SemaphoreType.DMA((3, 3, 3)),
            pltpu.SemaphoreType.DMA((3, 3, 3)),
            pltpu.SemaphoreType.DMA((3, 3, 3)),
            pltpu.SemaphoreType.DMA((4,)),
            pltpu.SemaphoreType.DMA((4,)),
        ],
        compiler_params=pltpu.CompilerParams(collective_id=3, has_side_effects=True, vmem_limit_bytes=VMEM_BYTES),
    )(*operands)


def swapped(value):
    return lax.ppermute(value, "wshard", [(0, 1), (1, 0)])


def part(value, index, size, axis=0):
    return lax.dynamic_slice_in_dim(value, index * size, size, axis)


def rms_scale(values, gain):
    return values * lax.rsqrt(jnp.mean(values * values, axis=-1, keepdims=True) + EPSILON) * gain


def to_all(rows):
    return lax.all_to_all(rows, ("expert", "wshard"), split_axis=0, concat_axis=0, tiled=True)


def per_device(tokens, lengths, routes, attn_gain, query_weight, key_weight, value_weight, output_weight, bias_table, mix_gain, router_weight, expert_in, expert_out, cotangent):
    j = lax.axis_index("wshard")
    jp = 1 - j
    misc = jnp.zeros((24, HALF), F32)
    misc = misc.at[0:16, 0:12].set(bias_table.astype(F32))
    misc = misc.at[16].set(attn_gain.astype(F32)).at[17].set(mix_gain.astype(F32))
    qkv, normed, wqkv, wo_full, router_full, misc_full = window(tokens, query_weight, key_weight, value_weight, output_weight, router_weight, misc)
    gain_second = jnp.concatenate([misc_full[17], misc_full[41]])
    att, lse = attention(lengths, qkv, misc_full)
    got = swapped(part(att, jp, TOK))
    mine = part(att, j, TOK)
    att_row = jnp.where(j == 0, jnp.concatenate([mine, got], axis=1), jnp.concatenate([got, mine], axis=1))
    inputs = tokens.astype(F32)
    hidden = inputs + mm(att_row, wo_full)
    mixed = rms_scale(hidden, gain_second).astype(BF)
    router = jax.nn.softmax(mm(mixed, router_full), axis=-1)
    experts = jnp.arange(EXPERTS, dtype=jnp.int32)
    chosen = routes == experts[None, :]
    chosen_float = chosen.astype(F32)
    gate = jnp.sum(router * chosen_float, axis=1)
    out_grad = cotangent.astype(F32)
    made_grad = (gate[:, None] * out_grad).astype(BF)
    earlier = (jnp.arange(TOK)[:, None] > jnp.arange(TOK)[None, :]) & (routes == routes[:, 0][None, :])
    second = jnp.any(earlier, axis=1)
    place = [(chosen & (second == bool(r))[:, None]).astype(BF) for r in range(2)]
    sent = jnp.stack([mm(place[r], rows, TN).astype(BF) for rows in (mixed, made_grad) for r in range(2)], axis=1)
    arrived = to_all(sent)
    x = arrived[:, 0:2].reshape(2 * EXPERTS, D)
    g = arrived[:, 2:4].reshape(2 * EXPERTS, D)
    made, back, expert_in_grad, expert_out_grad = expert(x, g, expert_in, expert_out)
    home = to_all(jnp.concatenate([made.reshape(EXPERTS, 2, D), back.reshape(EXPERTS, 2, D)], axis=1))
    made_token = mm(place[0], home[:, 0]) + mm(place[1], home[:, 1])
    expert_mixed_grad = mm(place[0], home[:, 2]) + mm(place[1], home[:, 3])
    layer_out = (hidden + gate[:, None] * made_token).astype(BF)
    gate_grad = jnp.sum(out_grad * made_token, axis=1)
    logit_grad = ((gate_grad * gate)[:, None] * (chosen_float - router)).astype(BF)
    mixed_grad = mm(logit_grad, router_full, NT) + expert_mixed_grad
    hidden_part, mix_gain_grad = jax.vjp(rms_scale, hidden, gain_second)[1](mixed_grad)
    hidden_grad = out_grad + hidden_part
    branch_grad = hidden_grad.astype(BF)
    got = swapped(branch_grad)
    branch_chip = jnp.where(j == 0, jnp.concatenate([branch_grad, got]), jnp.concatenate([got, branch_grad]))
    att_grad = mm(branch_chip, output_weight, NT).astype(BF)
    delta = jnp.sum((att_grad.astype(F32) * att.astype(F32)).reshape(CHIP, 6, HEAD), axis=2)
    stat = jnp.concatenate([lse, jnp.pad(delta.T, ((0, 2), (0, 0)))], axis=0)
    dout_win, stat_win = spread(att_grad, stat)
    dqkv, bias_part = attention_back(lengths, qkv, dout_win, stat_win, misc_full)
    mix_row = jnp.broadcast_to(mix_gain_grad[None], (8, D))
    tokens_grad, q_sum, k_sum, v_sum, out_sum, router_sum, bias_sum, gain_sum = tail(
        dqkv, normed, wqkv, tokens, hidden_grad, att, branch_chip, mixed, logit_grad, mix_row, bias_part, misc_full
    )
    return (
        layer_out,
        tokens_grad,
        gain_sum[0:3].reshape(HALF),
        q_sum.astype(F32),
        k_sum.astype(F32),
        v_sum.astype(F32),
        out_sum.astype(F32),
        bias_sum[:, 0:12],
        gain_sum[3:6].reshape(HALF),
        router_sum,
        expert_in_grad,
        expert_out_grad,
    )


def solution(mesh):
    by_token = P(("expert", "wshard"), None)
    by_row = P("wshard", None)
    by_expert = P(("expert", "wshard"), None, None)
    return jax.shard_map(
        per_device,
        mesh=mesh,
        in_specs=(
            by_token,
            P(),
            by_token,
            P("wshard"),
            by_row,
            by_row,
            by_row,
            by_row,
            by_row,
            P("wshard"),
            by_row,
            by_expert,
            by_expert,
            by_token,
        ),
        out_specs=(
            by_token,
            by_token,
            P("wshard"),
            by_row,
            by_row,
            by_row,
            by_row,
            by_row,
            P("wshard"),
            by_row,
            by_expert,
            by_expert,
        ),
        check_vma=False,
    )
```

```python
import functools

import jax
import jax.numpy as jnp
from jax import lax
from jax.experimental import pallas as pl
from jax.experimental.pallas import tpu as pltpu
from jax.sharding import PartitionSpec as P

MESH = pl.DeviceIdType.MESH
BF = jnp.bfloat16
F32 = jnp.float32
EPSILON = 1e-06
FAR_EDGES = (12, 16, 23, 32, 46, 64, 91)

D = 768
HALF = 384
HEAD = 64
TOK = 128
CHIP = 256
REACH = 4
SLOTS = 2 * REACH + 1
WIN = SLOTS * CHIP
MID = REACH * CHIP
TOTAL = 16384
EXPERTS = 128
NB = 32
FF = 3072
NEAR = 3 * CHIP
LOOP = 1024
VMEM_BYTES = 56 * 1024 * 1024

NT = (((1,), (1,)), ((), ()))
TN = (((0,), (0,)), ((), ()))
NN = (((1,), (0,)), ((), ()))


def mm(left, right, dims=NN):
    return lax.dot_general(left, right, dims, preferred_element_type=F32)


def bucket_of(relative):
    distance = jnp.abs(relative)
    far_bucket = 8 + sum(((distance >= edge).astype(jnp.int32) for edge in FAR_EDGES))
    near_far = jnp.where(distance < 8, distance, far_bucket)
    return near_far + 16 * (relative > 0).astype(jnp.int32)


def tile(ref, rows, start, width):
    return ref[rows, pl.ds(pl.multiple_of(start, 128), width)]


OFFSETS = (1, -1, 4, -4, 3, -3, 2, -2)
DIRECT = 6
AXES = {"y": 16, "x": 4, "z": 1}


def remote(src, dst, ssem, rsem, chip, core):
    return pltpu.make_async_remote_copy(src_ref=src, dst_ref=dst, send_sem=ssem, recv_sem=rsem, device_id=(chip, core), device_id_type=MESH)


def chip_at(e, m):
    chips = lax.axis_size("expert")
    return lax.rem(e + m + chips, chips)


def signal(barrier, chip, core):
    pl.semaphore_signal(barrier, inc=1, device_id=(chip, core), device_id_type=MESH)


def chunk(c):
    return slice(c * CHIP, (c + 1) * CHIP)


def both_gains(misc, row):
    return jnp.concatenate([misc[row : row + 1, :], misc[row + 24 : row + 25, :]], axis=1)


def placing(routes_row):
    lane = lax.broadcasted_iota(jnp.int32, (TOK, EXPERTS), 1)
    row = lax.broadcasted_iota(jnp.int32, (TOK, EXPERTS), 0)
    across = jnp.broadcast_to(routes_row[0:1, :], (TOK, TOK))
    down = across.T
    chosen = (down == lane).astype(F32)
    earlier = ((down == across) & (lane < row)).astype(F32)
    second = jnp.max(earlier, axis=1, keepdims=True)
    return chosen, (chosen * (1.0 - second)).astype(BF), (chosen * second).astype(BF)


def prepare(lengths, mask):
    e = lax.axis_index("expert")
    row_pos = (e - REACH) * CHIP + lax.broadcasted_iota(jnp.int32, (8, WIN), 1)
    col_pos = e * CHIP + lax.broadcasted_iota(jnp.int32, (CHIP, 128), 0)

    def count(n, state):
        end, rows, cols = state
        end = end + lengths[n]
        return end, rows + (row_pos >= end).astype(jnp.int32), cols + (col_pos >= end).astype(jnp.int32)

    zero = jnp.zeros((8, WIN), jnp.int32)
    _, rows, cols = lax.fori_loop(0, 32, count, (jnp.int32(0), zero, jnp.zeros((CHIP, 128), jnp.int32)))
    rows = jnp.where((row_pos >= 0) & (row_pos < TOTAL), rows, -1)
    for c in range(SLOTS):
        part = rows[0:1, c * CHIP : (c + 1) * CHIP]
        mask[:, c * CHIP : (c + 1) * CHIP] = jnp.where(cols[:, 0:1] == part, 0.0, -1e9).astype(F32)


def prepare_biases(misc, diag, ways):
    table = jnp.concatenate([misc[0:16, 0:128], misc[24:40, 0:128]], axis=0).astype(BF)
    for n, sign in enumerate(ways):
        hot = diagonal_buckets(sign)
        diag[n * 16 : (n + 1) * 16, :] = mm(table, hot.astype(BF), TN)[0:16]


def diagonal_buckets(sign):
    m = lax.broadcasted_iota(jnp.int32, (NB, LOOP), 1)
    r = jnp.where(m < NEAR, m, m - LOOP) - CHIP
    b = lax.broadcasted_iota(jnp.int32, (NB, LOOP), 0)
    return (bucket_of(sign * r) == b).astype(F32)


def biased(raw, c, mask, near, left, right):
    s = raw + mask[:, c * CHIP : (c + 1) * CHIP]
    if c < REACH - 1:
        return s + left
    if c > REACH + 1:
        return s + right
    lower = (c - REACH + 1) * CHIP
    return s + near[:, lower : lower + CHIP]


def near_tile(diag, row):
    line = diag[pl.ds(row, 1), :]
    spread = pltpu.roll(jnp.broadcast_to(line, (CHIP, LOOP)), 0, 1, stride=1, stride_axis=0)
    return spread[:, 0:NEAR], line[:, 0:1], line[:, NEAR - 1 : NEAR]


def front_kernel(lengths, tok_any, wq, wk, wv, wo_any, router_any, misc_any, tok, wo, routes_row, cot, qkv_any, normed_any, wqkv_any, router_full, misc, att, lse, hidden, mixed, router, sent, qkv, normed, wqkv, win, wo_other, att_other, mask, diag, scores, lse_cols, send, recv, fsend, frecv, wsend, wrecv, local, store):
    e = lax.axis_index("expert")
    j = lax.axis_index("wshard")
    jp = 1 - j
    barrier = pltpu.get_barrier_semaphore()
    for m in OFFSETS:
        signal(barrier, chip_at(e, m), j)
    signal(barrier, e, jp)

    def rows_of(slot, core):
        return win.at[pl.ds(pl.multiple_of(slot * CHIP + core * TOK, TOK), TOK), :]

    weights = []
    kept = []
    for n, w in enumerate((wq, wk, wv)):
        rows = pl.ds(pl.multiple_of(j * HALF, HALF), HALF)
        there = w.at[:, pl.ds(pl.multiple_of(jp * HALF, 128), HALF)]
        here = w.at[:, pl.ds(pl.multiple_of(j * HALF, 128), HALF)]
        dst = wqkv.at[rows, n * HALF : (n + 1) * HALF]
        weights.append(remote(there, dst, wsend.at[n], wrecv.at[n], e, jp))
        kept.append(pltpu.make_async_copy(here, dst, local.at[1 + n]))
    for n, (src, dst, size) in enumerate(((misc_any, misc, 24), (router_any, router_full, HALF))):
        rows = pl.ds(pl.multiple_of(j * size, 8), size)
        weights.append(remote(src, dst.at[rows, :], wsend.at[3 + n], wrecv.at[3 + n], e, jp))
        kept.append(pltpu.make_async_copy(src, dst.at[rows, :], local.at[4 + n]))
    weights.append(remote(wo_any, wo_other, wsend.at[5], wrecv.at[5], e, jp))
    mine = pltpu.make_async_copy(tok_any, rows_of(REACH, j), local.at[0])
    mine.start()
    for c in kept:
        c.start()

    copies = []
    for n, m in enumerate(OFFSETS):
        src = tok_any if n < DIRECT else rows_of(REACH - m // 2, j)
        to = chip_at(e, m if n < DIRECT else m // 2)
        copies.append(remote(src, rows_of(REACH - m, j), send.at[n], recv.at[n], to, j))
    passed = [remote(rows_of(REACH - m, j), rows_of(REACH - m, j), fsend.at[n], frecv.at[n], e, jp) for n, m in enumerate(OFFSETS)]
    swap = remote(tok_any, rows_of(REACH, j), fsend.at[8], frecv.at[8], e, jp)

    pl.semaphore_wait(barrier, len(OFFSETS) + 1)
    for c in copies[:DIRECT]:
        c.start()
    weights[3].start()
    for c in weights[:3]:
        c.start()
    swap.start()
    for c in weights[4:]:
        c.start()
    prepare(lengths, mask)
    mine.wait()
    for c in kept:
        c.wait()
    for c in weights[:4]:
        c.wait_recv()
    prepare_biases(misc, diag, (1,))
    gain = both_gains(misc, 16)

    def project(slot):
        x = win[chunk(slot), :].astype(F32)
        y = (x * lax.rsqrt(jnp.mean(x * x, axis=-1, keepdims=True) + EPSILON) * gain).astype(BF)
        if slot == REACH:
            normed[...] = y
        qkv[chunk(slot), :] = mm(y, wqkv[...]).astype(BF)

    for n in range(2):
        copies[n].wait_recv()
        copies[DIRECT + n].start()
        passed[n].start()
    swap.wait_recv()
    project(REACH)
    for n in range(2, len(OFFSETS) + 2):
        if n < len(OFFSETS):
            copies[n].wait_recv()
            passed[n].start()
        passed[n - 2].wait_recv()
        project(REACH - OFFSETS[n - 2])

    stores = [pltpu.make_async_copy(src, dst, store.at[n]) for n, (src, dst) in enumerate(((qkv, qkv_any), (normed, normed_any), (wqkv, wqkv_any)))]
    for c in stores:
        c.start()
    lane = lax.broadcasted_iota(jnp.int32, (CHIP, 128), 1)
    lse_cols[...] = jnp.zeros((CHIP, 128), F32)

    def pair(p, carry):
        q = tile(qkv, slice(MID, MID + CHIP), p * 128, 128).astype(F32) * 0.125
        outs = []
        for hh in range(2):
            own = (lane // HEAD) == hh
            qm = jnp.where(own, q, 0.0).astype(BF)
            near, left, right = near_tile(diag, j * 6 + 2 * p + hh)
            top = None
            for c in range(SLOTS):
                k = tile(qkv, chunk(c), HALF + p * 128, 128)
                s = biased(mm(qm, k, NT), c, mask, near, left, right)
                scores[:, chunk(c)] = s
                top = s if top is None else jnp.maximum(top, s)
            top = jnp.max(top, axis=1, keepdims=True)
            total = jnp.zeros((CHIP, CHIP), F32)
            out = jnp.zeros((CHIP, 128), F32)
            for c in range(SLOTS):
                x = jnp.exp(scores[:, chunk(c)] - top)
                total = total + x
                out = out + mm(x.astype(BF), tile(qkv, chunk(c), 2 * HALF + p * 128, 128))
            total = jnp.sum(total, axis=1, keepdims=True)
            outs.append(out / total)
            lse_cols[...] = jnp.where(lane == 2 * p + hh, top + jnp.log(total), lse_cols[...])
        att[:, pl.ds(pl.multiple_of(p * 128, 128), 128)] = jnp.where(lane < HEAD, outs[0], outs[1]).astype(BF)
        return carry

    lax.fori_loop(0, 3, pair, 0)
    lse[...] = lse_cols[...].T[0:8, :]

    here = pl.ds(pl.multiple_of(j * TOK, TOK), TOK)
    there = pl.ds(pl.multiple_of(jp * TOK, TOK), TOK)
    trade = remote(att.at[there, :], att_other, wsend.at[6], wrecv.at[6], e, jp)
    trade.start()
    chosen, first, second = placing(routes_row)
    branch = mm(att[here, :], wo[...])
    for c in weights[4:]:
        c.wait_recv()
    trade.wait_recv()
    total = tok[...].astype(F32) + (branch + mm(att_other[...], wo_other[...]))
    hidden[...] = total
    low = (total * lax.rsqrt(jnp.mean(total * total, axis=-1, keepdims=True) + EPSILON) * both_gains(misc, 17)).astype(BF)
    mixed[...] = low
    logits = mm(low, router_full[...])
    powers = jnp.exp(logits - jnp.max(logits, axis=1, keepdims=True))
    probs = powers / jnp.sum(powers, axis=1, keepdims=True)
    router[...] = probs
    gate = jnp.sum(probs * chosen, axis=1, keepdims=True)
    made_grad = (gate * cot[...].astype(F32)).astype(BF)
    for n, (place, rows) in enumerate(((first, low), (second, low), (first, made_grad), (second, made_grad))):
        sent[n] = mm(place, rows, TN).astype(BF)

    trade.wait_send()
    swap.wait_send()
    for c in weights + copies + passed:
        c.wait_send()
    for c in stores:
        c.wait()


def front(lengths, tokens, wq, wk, wv, wo, router, misc, row, cotangent):
    smem = pl.BlockSpec(memory_space=pltpu.SMEM)
    hbm = pl.BlockSpec(memory_space=pl.ANY)
    vm = pl.BlockSpec(memory_space=pltpu.VMEM)
    return pl.pallas_call(
        front_kernel,
        name="front",
        out_shape=(
            jax.ShapeDtypeStruct((WIN, 3 * HALF), BF),
            jax.ShapeDtypeStruct((CHIP, D), BF),
            jax.ShapeDtypeStruct((D, 3 * HALF), BF),
            jax.ShapeDtypeStruct((D, EXPERTS), BF),
            jax.ShapeDtypeStruct((48, HALF), F32),
            jax.ShapeDtypeStruct((CHIP, HALF), BF),
            jax.ShapeDtypeStruct((8, CHIP), F32),
            jax.ShapeDtypeStruct((TOK, D), F32),
            jax.ShapeDtypeStruct((TOK, D), BF),
            jax.ShapeDtypeStruct((TOK, EXPERTS), F32),
            jax.ShapeDtypeStruct((4, EXPERTS, D), BF),
        ),
        in_specs=[smem] + [hbm] * 7 + [vm] * 4,
        out_specs=(hbm,) * 3 + (vm,) * 8,
        scratch_shapes=[
            pltpu.VMEM((WIN, 3 * HALF), BF),
            pltpu.VMEM((CHIP, D), BF),
            pltpu.VMEM((D, 3 * HALF), BF),
            pltpu.VMEM((WIN, D), BF),
            pltpu.VMEM((HALF, D), BF),
            pltpu.VMEM((TOK, HALF), BF),
            pltpu.VMEM((CHIP, WIN), F32),
            pltpu.VMEM((16, LOOP), F32),
            pltpu.VMEM((CHIP, WIN), F32),
            pltpu.VMEM((CHIP, 128), F32),
            pltpu.SemaphoreType.DMA((8,)),
            pltpu.SemaphoreType.DMA((8,)),
            pltpu.SemaphoreType.DMA((9,)),
            pltpu.SemaphoreType.DMA((9,)),
            pltpu.SemaphoreType.DMA((7,)),
            pltpu.SemaphoreType.DMA((7,)),
            pltpu.SemaphoreType.DMA((6,)),
            pltpu.SemaphoreType.DMA((3,)),
        ],
        compiler_params=pltpu.CompilerParams(collective_id=1, has_side_effects=True, vmem_limit_bytes=VMEM_BYTES),
    )(lengths, tokens, wq, wk, wv, wo, router, misc, tokens, wo, row, cotangent)


FF_TILE = 512


def expert_kernel(x, g, w_in, w_out, made_back, d_in, d_out, made_sum, back_sum):
    step = pl.program_id(0)

    @pl.when(step == 0)
    def _():
        made_sum[...] = jnp.zeros_like(made_sum)
        back_sum[...] = jnp.zeros_like(back_sum)

    pre = mm(x[...], w_in[0])
    half_erf = 0.5 * lax.erf(pre * (0.5**0.5)) + 0.5
    act = (pre * half_erf).astype(BF)
    slope = half_erf + pre * jnp.exp(-0.5 * pre * pre) * (0.5 * 0.7978845608028654)
    act_grad = mm(g[...], w_out[0], NT)
    pre_grad = (act_grad * slope).astype(BF)
    made_sum[...] += mm(act, w_out[0])
    back_sum[...] += mm(pre_grad, w_in[0], NT)
    d_out[0] = mm(act, g[...], TN).astype(BF)
    d_in[0] = mm(x[...], pre_grad, TN).astype(BF)

    @pl.when(step == pl.num_programs(0) - 1)
    def _():
        made_back[0 : 2 * EXPERTS, :] = made_sum[...].astype(BF)
        made_back[2 * EXPERTS :, :] = back_sum[...].astype(BF)


def expert(arrived, w_in, w_out):
    rows = 2 * EXPERTS
    forward = pl.BlockSpec((rows, D), lambda f: (0, 0))
    backward = pl.BlockSpec((rows, D), lambda f: (1, 0))
    whole = pl.BlockSpec((2 * rows, D), lambda f: (0, 0))
    by_in = pl.BlockSpec((1, D, FF_TILE), lambda f: (0, 0, f))
    by_out = pl.BlockSpec((1, FF_TILE, D), lambda f: (0, f, 0))
    return pl.pallas_call(
        expert_kernel,
        name="expert",
        grid=(FF // FF_TILE,),
        out_shape=(
            jax.ShapeDtypeStruct((2 * rows, D), BF),
            jax.ShapeDtypeStruct((1, D, FF), BF),
            jax.ShapeDtypeStruct((1, FF, D), BF),
        ),
        in_specs=[forward, backward, by_in, by_out],
        out_specs=(whole, by_in, by_out),
        scratch_shapes=[pltpu.VMEM((rows, D), F32), pltpu.VMEM((rows, D), F32)],
        compiler_params=pltpu.CompilerParams(vmem_limit_bytes=VMEM_BYTES, dimension_semantics=("arbitrary",)),
    )(arrived, arrived, w_in, w_out)


ORDERS = ("zxy", "xyz", "yzx")
RING = 16
PLANE = [(d, f) for d in range(4) for f in range(4) if d + f > 0]


class Sum:
    def __init__(self, e, j, order, part, ring, plane, ring_sum, plane_sum, all_, ring_sems, plane_sems):
        self.e, self.j, self.order = e, j, order
        self.part, self.ring, self.plane, self.ring_sum, self.plane_sum, self.all = part, ring, plane, ring_sum, plane_sum, all_
        self.ring_sems, self.plane_sems = ring_sems, plane_sems
        self.coord = [lax.rem(e // AXES[a], 4) for a in order]

    def peer(self, *steps):
        to = self.e
        for axis, at, d in zip(self.order, self.coord, steps):
            to = to + (lax.rem(at + d, 4) - at) * AXES[axis]
        return to

    def block(self, d, first, count):
        return pl.ds(lax.rem(self.coord[0] + d + 4, 4) * RING + first, count)

    def copy(self, src, dst, sems, n, to):
        return remote(src, dst, sems[0].at[n], sems[1].at[n], to, self.j)

    def reduce_copies(self, which):
        h = RING // 2
        up, down = self.peer(1), self.peer(3)
        pieces = [
            (lambda: self.part.at[:, self.block(2, 0, h)], up),
            (lambda: self.part.at[:, self.block(2, h, h)], down),
            (lambda: self.part.at[:, self.block(1, h, h)], up),
            (lambda: self.part.at[:, self.block(3, 0, h)], down),
            (lambda: self.ring.at[6], up),
            (lambda: self.ring.at[7], down),
        ]
        return [self.copy(pieces[n][0](), self.ring.at[n], self.ring_sems, n, pieces[n][1]) for n in which]

    def gather_copies(self, which):
        h = RING // 2
        up, down = self.peer(1), self.peer(3)
        pieces = [(0, 0, RING, up), (0, 0, RING, down), (-1, 0, h, up), (1, h, h, down)]
        found = []
        for n in which:
            d, first, count, to = pieces[n]
            ref = self.all.at[:, self.block(d, first, count)]
            found.append(self.copy(ref, ref, self.ring_sems, 6 + n, to))
        return found

    def plane_copies(self, back):
        found = []
        for n, (d, f) in enumerate(PLANE):
            to = self.peer(0, d, f)
            if back:
                ref = self.all.at[:, pl.ds(self.coord[0] * RING + self.coord[1] * 4 + self.coord[2], 1)]
                found.append(self.copy(ref, ref, self.plane_sems, 15 + n, to))
            else:
                place = lax.rem(self.coord[1] + d, 4) * 4 + lax.rem(self.coord[2] + f, 4)
                found.append(self.copy(self.ring_sum.at[:, pl.ds(place, 1)], self.plane.at[n], self.plane_sems, n, to))
        return found

    def start_ring(self):
        for c in self.reduce_copies(range(4)):
            c.start()

    def pass_ring(self):
        h = RING // 2
        for n, where in ((0, self.block(1, 0, h)), (1, self.block(3, h, h))):
            came, goes = self.reduce_copies((n, 4 + n))
            came.wait_recv()
            self.ring[6 + n] = (self.part[:, where].astype(F32) + self.ring[n].astype(F32)).astype(BF)
            goes.start()

    def ring_to_plane(self):
        h = RING // 2
        for c in self.reduce_copies(range(2, 6)):
            c.wait_recv()
        for first, others in ((0, (4, 3)), (h, (5, 2))):
            total = self.part[:, self.block(0, first, h)].astype(F32)
            for n in others:
                total = total + self.ring[n].astype(F32)
            self.ring_sum[:, first : first + h] = total.astype(BF)
        for c in self.plane_copies(False):
            c.start()

    def plane_back(self):
        own = self.coord[1] * 4 + self.coord[2]
        total = self.ring_sum[:, pl.ds(own, 1)].astype(F32)
        for n, c in enumerate(self.plane_copies(False)):
            c.wait_recv()
            total = total + self.plane[n].astype(F32)
        self.all[:, pl.ds(self.coord[0] * RING + own, 1)] = total.astype(BF)
        for c in self.plane_copies(True):
            c.start()

    def plane_to_ring(self):
        for c in self.plane_copies(True):
            c.wait_recv()
        for c in self.gather_copies((0, 1)):
            c.start()

    def pass_back(self):
        for n in range(2):
            came, goes = self.gather_copies((n, 2 + n))
            came.wait_recv()
            goes.start()

    def end(self):
        for c in self.gather_copies((2, 3)):
            c.wait_recv()

    def end_sends(self):
        for c in self.reduce_copies(range(6)) + self.plane_copies(False) + self.plane_copies(True) + self.gather_copies(range(4)):
            c.wait_send()


def sum_scratch(units):
    return [
        pltpu.VMEM((units, 64, 16, 128), BF),
        pltpu.VMEM((8, units, RING // 2, 16, 128), BF),
        pltpu.VMEM((15, units, 1, 16, 128), BF),
        pltpu.VMEM((units, RING, 16, 128), BF),
        pltpu.VMEM((units, 1, 16, 128), BF),
        pltpu.VMEM((units, 64, 16, 128), BF),
        pltpu.SemaphoreType.DMA((10,)),
        pltpu.SemaphoreType.DMA((10,)),
        pltpu.SemaphoreType.DMA((30,)),
        pltpu.SemaphoreType.DMA((30,)),
    ]


def sums_of(e, j, scratch):
    found = []
    for n, order in enumerate(ORDERS):
        s = scratch[10 * n : 10 * n + 10]
        found.append(Sum(e, j, order, *s[:6], s[6:8], s[8:10]))
    return found


LATE = (3, 2, 2)
EARLY = (1, 1, 1)
OWN = 216


def spots(units, first, count):
    table = [(n, u) for n in range(3) for u in range(units[n])]
    done = 0
    while done < count:
        unit, place = divmod(first + done, 64)
        n = min(64 - place, count - done)
        yield table[unit] + (place, n, done)
        done += n


def tiles(value):
    return value.astype(BF).reshape(value.shape[0] // 16, 16, 128)


def rows_of_tiles(value):
    return value.reshape(value.shape[0] * 16, 128)


def back_kernel(lengths, home, hidden, mixed, router, routes_row, cot, tok, router_full, misc, wo, att, lse, qkv_any, normed_any, wqkv_any, layer_out, tokens_grad, q_sum, k_sum, v_sum, out_sum, router_sum, bias_sum, gain_sum, qkv, normed, wqkv, mask, diag, dout, stat, cols, dqkv, bias, branch, hidden_grad, half_out, half_in, grads, router_grad, stage, small, send, recv, core_send, core_recv, local, acc, *scratch):
    e = lax.axis_index("expert")
    j = lax.axis_index("wshard")
    jp = 1 - j
    here = pl.ds(pl.multiple_of(j * TOK, TOK), TOK)
    there = pl.ds(pl.multiple_of(jp * TOK, TOK), TOK)
    barrier = pltpu.get_barrier_semaphore()
    early, late = sums_of(e, j, scratch[:30]), sums_of(e, j, scratch[30:])
    for m in OFFSETS:
        signal(barrier, chip_at(e, m), j)
    for n in range(1, 64):
        steps = (n // 16, n // 4 % 4, n % 4)
        if 0 in steps:
            signal(barrier, early[0].peer(*steps), j)
    signal(barrier, e, jp)

    loads = [pltpu.make_async_copy(src, dst, local.at[n]) for n, (src, dst) in enumerate(((qkv_any, qkv), (normed_any, normed), (wqkv_any, wqkv)))]
    for c in loads:
        c.start()

    chosen, first, second = placing(routes_row)
    probs = router[...]
    gate = jnp.sum(probs * chosen, axis=1, keepdims=True)
    made = mm(first, home[0]) + mm(second, home[1])
    expert_back = mm(first, home[2]) + mm(second, home[3])
    total = hidden[...]
    layer_out[...] = (total + gate * made).astype(BF)
    dy = cot[...].astype(F32)
    gate_grad = jnp.sum(dy * made, axis=1, keepdims=True)
    logit_grad = ((gate_grad * gate) * (chosen - probs)).astype(BF)
    mixed_grad = mm(logit_grad, router_full[...], NT) + expert_back
    r = lax.rsqrt(jnp.mean(total * total, axis=-1, keepdims=True) + EPSILON)
    w = mixed_grad * both_gains(misc, 17)
    mix_gain = jnp.sum(mixed_grad * total * r, axis=0, keepdims=True)
    rest = dy + (r * w - total * (r * r * r * jnp.mean(w * total, axis=-1, keepdims=True)))
    hidden_grad[...] = rest
    branch[here, :] = rest.astype(BF)

    pl.semaphore_wait(barrier, len(OFFSETS) + 37)
    trade = remote(branch.at[here, :], branch.at[here, :], core_send.at[0], core_recv.at[0], e, jp)
    trade.start()
    router_grad[...] = tiles(mm(mixed[...], logit_grad, TN))
    router_rows = lambda core: router_grad.at[pl.ds(core * 24, 24)]
    router_trade = remote(router_rows(jp), early[2].part.at[0, 40:64], core_send.at[1], core_recv.at[1], e, jp)
    router_trade.start()
    early[2].part[0, 16:40] = router_grad[pl.ds(j * 24, 24)]
    prepare(lengths, mask)
    prepare_biases(misc, diag, (1, -1))
    trade.wait_recv()

    lane = lax.broadcasted_iota(jnp.int32, (CHIP, 128), 1)
    mid = slice(MID, MID + CHIP)
    att_grad = mm(branch[...], wo[...], NT).astype(BF)
    dout[mid, :] = att_grad
    both = att_grad.astype(F32) * att[...].astype(F32)
    dots = jnp.zeros((CHIP, 128), F32)
    for h in range(6):
        own = (lane // HEAD) == h % 2
        dot = jnp.sum(jnp.where(own, both[:, (h // 2) * 128 : (h // 2) * 128 + 128], 0.0), axis=1, keepdims=True)
        dots = jnp.where(lane == h, dot, dots)
    stat[REACH, 0:8] = lse[...]
    stat[REACH, 8:16] = dots.T[0:8, :]
    cols[...] = jnp.concatenate([stat[REACH], jnp.zeros((112, CHIP), F32)], axis=0).T

    def window_copies(n):
        m = OFFSETS[n]
        slot = REACH if n < DIRECT else REACH - m // 2
        to = chip_at(e, m if n < DIRECT else m // 2)
        return [
            remote(dout.at[chunk(slot), :], dout.at[chunk(REACH - m), :], send.at[n, 0], recv.at[n, 0], to, j),
            remote(stat.at[slot], stat.at[REACH - m], send.at[n, 1], recv.at[n, 1], to, j),
        ]

    for n in range(DIRECT):
        for c in window_copies(n):
            c.start()
    grad = mm(att[...], branch[...], TN)
    for c in range(6):
        cut = tiles(grad[:, c * 128 : (c + 1) * 128])
        for n, unit, place, count, done in spots(EARLY, 24 * c, 24):
            early[n].part[unit, place : place + count] = cut[done : done + count]
    router_trade.wait_recv()
    for s in early:
        s.start_ring()
    for c in loads:
        c.wait()

    def forward_window():
        for n in range(2):
            for c in window_copies(n):
                c.wait_recv()
            for c in window_copies(DIRECT + n):
                c.start()

    def pass_early():
        for s in early:
            s.pass_ring()

    line = lax.broadcasted_iota(jnp.int32, (NB, 128), 1)
    row32 = lax.broadcasted_iota(jnp.int32, (NB, 128), 0)
    hot = diagonal_buckets(1)
    bias[...] = jnp.zeros((NB, 128), F32)

    def by_queries(p, carry):
        q = tile(qkv, mid, p * 128, 128).astype(F32) * 0.125
        do = tile(dout, mid, p * 128, 128)
        found = []
        for hh in range(2):
            h = 2 * p + hh
            own = (lane // HEAD) == hh
            spare = (1 - hh) * HEAD
            qm = jnp.where(own, q, 0.0).astype(BF)
            dom = jnp.where(own, do, jnp.zeros_like(do))
            log_sum = jnp.sum(jnp.where(lane == h, cols[...], 0.0), axis=1, keepdims=True)
            dot = jnp.sum(jnp.where(lane == h + 8, cols[...], 0.0), axis=1, keepdims=True)
            near, left, right = near_tile(diag, j * 6 + h)
            dq = jnp.zeros((CHIP, 128), F32)
            near_grads = []
            for c in range(SLOTS):
                k = tile(qkv, chunk(c), HALF + p * 128, 128)
                v = tile(qkv, chunk(c), 2 * HALF + p * 128, 128)
                s = biased(mm(qm, k, NT), c, mask, near, left, right)
                ds = jnp.exp(s - log_sum) * (mm(dom, v, NT) - dot)
                if c < REACH - 1:
                    other = jnp.where(lane == spare, 1.0, 0.0).astype(BF)
                elif c > REACH + 1:
                    other = jnp.where(lane == spare + 1, 1.0, 0.0).astype(BF)
                else:
                    other = jnp.zeros((CHIP, 128), BF)
                    near_grads.append(ds)
                dq = dq + mm(ds.astype(BF), jnp.where(own, k, other))
            found.append(dq * 0.125)
            fold = jnp.concatenate(near_grads + [jnp.zeros((CHIP, CHIP), F32)], axis=1)
            rows = CHIP
            while rows > 8:
                rows //= 2
                fold = fold[0:rows] + pltpu.roll(fold[rows : 2 * rows], LOOP - rows, 1)
            summed = fold[0:1]
            for n in range(1, 8):
                summed = summed + pltpu.roll(fold[n : n + 1], LOOP - n, 1)
            by_bucket = jnp.sum(hot * summed, axis=1, keepdims=True)
            far = jnp.sum(dq, axis=0, keepdims=True)
            by_bucket = by_bucket + jnp.where(row32 == 15, far[:, spare : spare + 1], 0.0) + jnp.where(row32 == 31, far[:, spare + 1 : spare + 2], 0.0)
            bias[...] = jnp.where(line == j * 6 + h, by_bucket, bias[...])
            if hh == 0:
                pl.when(p == 0)(forward_window)
                pl.when(p == 2)(pass_early)
        dqkv[:, pl.ds(pl.multiple_of(p * 128, 128), 128)] = jnp.where(lane < HEAD, found[0], found[1]).astype(BF)
        return carry

    lax.fori_loop(0, 3, by_queries, 0)

    def by_keys(slots, p, carry):
        k_own = tile(qkv, mid, HALF + p * 128, 128)
        v_own = tile(qkv, mid, 2 * HALF + p * 128, 128)
        found = []
        for hh in range(2):
            h = 2 * p + hh
            own = (lane // HEAD) == hh
            km = jnp.where(own, k_own, jnp.zeros_like(k_own))
            vm = jnp.where(own, v_own, jnp.zeros_like(v_own))
            if REACH in slots:
                near, left, right = near_tile(diag, 16 + j * 6 + h)
            else:
                ends = diag[pl.ds(16 + j * 6 + h, 1), :]
                near, left, right = None, ends[:, 0:1], ends[:, NEAR - 1 : NEAR]
            dk = jnp.zeros((CHIP, 128), F32)
            dv = jnp.zeros((CHIP, 128), F32)
            for c in slots:
                qc = (tile(qkv, chunk(c), p * 128, 128).astype(F32) * 0.125).astype(BF)
                dc = tile(dout, chunk(c), p * 128, 128)
                s = biased(mm(km, qc, NT), c, mask, near, left, right)
                prob = jnp.exp(s - stat[c, pl.ds(h, 1), :])
                ds = prob * (mm(vm, dc, NT) - stat[c, pl.ds(h + 8, 1), :])
                dv = dv + mm(prob.astype(BF), dc)
                dk = dk + mm(ds.astype(BF), qc)
            found.append((dk, dv))
        for n in range(2):
            where = pl.ds(pl.multiple_of(n * HALF + p * 128, 128), 128)
            both = jnp.where(lane < HEAD, found[0][n], found[1][n])
            acc[:, where] = both if REACH in slots else acc[:, where] + both
        return carry

    for n, slots in ((1, (REACH, 3, 5)), (2, (0, 8)), (4, (1, 7)), (6, (2, 6))):
        if n > 1:
            for c in window_copies(n) + window_copies(n + 1):
                c.wait_recv()
        lax.fori_loop(0, 3, functools.partial(by_keys, slots), 0)
        if n == 1:
            for s in early:
                s.ring_to_plane()
        elif n == 4:
            for s in early:
                s.plane_back()
    dqkv[:, HALF:] = acc[...].astype(BF)

    half_out[...] = mm(dqkv[there, :], wqkv[...], NT).astype(BF)
    half_trade = remote(half_out, half_in, core_send.at[2], core_recv.at[2], e, jp)
    half_trade.start()
    whole = tuple(s.part for s in late)
    swaps = []
    for n, unit, place, count, done in spots(LATE, OWN, OWN):
        swaps.append((done + count, remote(stage.at[done : done + count], whole[n].at[unit, place : place + count], core_send.at[4 + len(swaps)], core_recv.at[4 + len(swaps)], e, jp)))
    sent = 0
    for third in range(3):
        grad = mm(normed[...], dqkv[:, third * HALF : (third + 1) * HALF], TN)
        for c in range(3 * third, 3 * third + 3):
            grads[c % 3] = tiles(grad[:, (c % 3) * 128 : (c % 3 + 1) * 128])
            stage[24 * c : 24 * c + 24] = grads[c % 3, pl.ds(24 * jp, 24)]
            for n, unit, place, count, done in spots(LATE, 24 * c, 24):
                whole[n][unit, place : place + count] = grads[c % 3, pl.ds(24 * j + done, count)]
        while sent < len(swaps) and swaps[sent][0] <= 72 * (third + 1):
            swaps[sent][1].start()
            sent += 1
    late[0].start_ring()
    for s in early:
        s.plane_to_ring()

    half = mm(dqkv[here, :], wqkv[...], NT)
    half_trade.wait_recv()
    grad = half + half_in[...].astype(F32)
    x = tok[...].astype(F32)
    r = lax.rsqrt(jnp.mean(x * x, axis=-1, keepdims=True) + EPSILON)
    w = grad * both_gains(misc, 16)
    tokens_grad[...] = (hidden_grad[...] + (r * w - x * (r * r * r * jnp.mean(w * x, axis=-1, keepdims=True)))).astype(BF)
    attn_gain = jnp.sum(grad * x * r, axis=0, keepdims=True)
    for h in range(2):
        lines = [v[:, h * HALF + 128 * n : h * HALF + 128 * n + 128] for v in (attn_gain, mix_gain) for n in range(3)]
        small[2 * h] = bias[16 * h : 16 * h + 16, :].astype(BF)
        small[2 * h + 1] = jnp.concatenate(lines + [jnp.zeros((10, 128), F32)], axis=0).astype(BF)
    last = whole[2]
    last[1, 52:64] = jnp.zeros((12, 16, 128), BF)
    last[1, 48:50] = small[pl.ds(2 * j, 2)]
    small_trade = remote(small.at[pl.ds(2 * jp, 2)], last.at[1, 50:52], core_send.at[3], core_recv.at[3], e, jp)
    small_trade.start()
    late[0].pass_ring()
    for _, c in swaps:
        c.wait_recv()
    late[1].start_ring()
    small_trade.wait_recv()
    late[2].start_ring()
    for s in early:
        s.pass_back()
    for s in late[1:]:
        s.pass_ring()
    for s in late:
        s.ring_to_plane()

    for s in early:
        s.end()
    for c in range(6):
        for n, unit, place, count, done in spots(EARLY, 24 * c, 24):
            out_sum[16 * done : 16 * (done + count), c * 128 : (c + 1) * 128] = rows_of_tiles(early[n].all[unit, place : place + count])
    router_sum[...] = rows_of_tiles(early[2].all[0, 16:40].astype(F32) + early[2].all[0, 40:64].astype(F32))

    for step in ("plane_back", "plane_to_ring", "pass_back", "end"):
        for s in late:
            getattr(s, step)()
    sums = (q_sum, k_sum, v_sum)
    for c in range(9):
        for first_tile, core in ((24 * c, j), (OWN + 24 * c, jp)):
            column = pl.ds(pl.multiple_of(core * HALF + (c % 3) * 128, 128), 128)
            for n, unit, place, count, done in spots(LATE, first_tile, 24):
                sums[c // 3][16 * done : 16 * (done + count), column] = rows_of_tiles(late[n].all[unit, place : place + count])
    smalls = late[2].all[1, 48:50].astype(F32) + late[2].all[1, 50:52].astype(F32)
    bias_sum[...] = smalls[0]
    gain_sum[...] = smalls[1]

    for c in (trade, router_trade, half_trade, small_trade):
        c.wait_send()
    for _, c in swaps:
        c.wait_send()
    for n in range(len(OFFSETS)):
        for c in window_copies(n):
            c.wait_send()
    for s in early + late:
        s.end_sends()


def back(lengths, *operands):
    vm = pl.BlockSpec(memory_space=pltpu.VMEM)
    return pl.pallas_call(
        back_kernel,
        name="back",
        out_shape=(
            jax.ShapeDtypeStruct((TOK, D), BF),
            jax.ShapeDtypeStruct((TOK, D), BF),
            jax.ShapeDtypeStruct((HALF, D), BF),
            jax.ShapeDtypeStruct((HALF, D), BF),
            jax.ShapeDtypeStruct((HALF, D), BF),
            jax.ShapeDtypeStruct((HALF, D), BF),
            jax.ShapeDtypeStruct((HALF, EXPERTS), F32),
            jax.ShapeDtypeStruct((16, 128), F32),
            jax.ShapeDtypeStruct((16, 128), F32),
        ),
        in_specs=[pl.BlockSpec(memory_space=pltpu.SMEM)] + [vm] * 12 + [pl.BlockSpec(memory_space=pl.ANY)] * 3,
        out_specs=(vm,) * 9,
        scratch_shapes=[
            pltpu.VMEM((WIN, 3 * HALF), BF),
            pltpu.VMEM((CHIP, D), BF),
            pltpu.VMEM((D, 3 * HALF), BF),
            pltpu.VMEM((CHIP, WIN), F32),
            pltpu.VMEM((32, LOOP), F32),
            pltpu.VMEM((WIN, HALF), BF),
            pltpu.VMEM((SLOTS, 16, CHIP), F32),
            pltpu.VMEM((CHIP, 128), F32),
            pltpu.VMEM((CHIP, 3 * HALF), BF),
            pltpu.VMEM((NB, 128), F32),
            pltpu.VMEM((CHIP, D), BF),
            pltpu.VMEM((TOK, D), F32),
            pltpu.VMEM((TOK, D), BF),
            pltpu.VMEM((TOK, D), BF),
            pltpu.VMEM((3, 48, 16, 128), BF),
            pltpu.VMEM((48, 16, 128), BF),
            pltpu.VMEM((OWN, 16, 128), BF),
            pltpu.VMEM((4, 16, 128), BF),
            pltpu.SemaphoreType.DMA((8, 2)),
            pltpu.SemaphoreType.DMA((8, 2)),
            pltpu.SemaphoreType.DMA((8,)),
            pltpu.SemaphoreType.DMA((8,)),
            pltpu.SemaphoreType.DMA((3,)),
            pltpu.VMEM((CHIP, 2 * HALF), F32),
            *[s for units in EARLY + LATE for s in sum_scratch(units)],
        ],
        compiler_params=pltpu.CompilerParams(collective_id=2, has_side_effects=True, vmem_limit_bytes=VMEM_BYTES),
    )(lengths, *operands)


def finish_kernel(*refs):
    for src, dst in zip(refs[:8], refs[8:]):
        dst[...] = src[:, 0 : dst.shape[1]].astype(dst.dtype)


def finish(*results):
    vm = pl.BlockSpec(memory_space=pltpu.VMEM)
    kinds = ((TOK, D, BF), (TOK, D, BF)) + ((HALF, D, F32),) * 4 + ((HALF, EXPERTS, F32), (16, 12, F32))
    return pl.pallas_call(
        finish_kernel,
        name="finish",
        out_shape=tuple(jax.ShapeDtypeStruct((rows, columns), kind) for rows, columns, kind in kinds),
        in_specs=[vm] * 8,
        out_specs=(vm,) * 8,
        compiler_params=pltpu.CompilerParams(vmem_limit_bytes=VMEM_BYTES),
    )(*results)


def to_all(rows):
    return lax.all_to_all(rows, ("expert", "wshard"), split_axis=1, concat_axis=1, tiled=True)


def per_device(tokens, lengths, routes, attn_gain, query_weight, key_weight, value_weight, output_weight, bias_table, mix_gain, router_weight, expert_in, expert_out, cotangent):
    misc = jnp.zeros((24, HALF), F32)
    misc = misc.at[0:16, 0:12].set(bias_table.astype(F32))
    misc = misc.at[16].set(attn_gain.astype(F32)).at[17].set(mix_gain.astype(F32))
    row = routes.reshape(1, TOK)
    qkv, normed, wqkv, router_full, misc_full, att, lse, hidden, mixed, router, sent = front(
        lengths, tokens, query_weight, key_weight, value_weight, output_weight, router_weight, misc, row, cotangent
    )

    arrived = to_all(sent).reshape(4 * EXPERTS, D)
    made_back, expert_in_grad, expert_out_grad = expert(arrived, expert_in, expert_out)
    home = to_all(made_back.reshape(4, EXPERTS, D))
    *results, gain_sum = back(lengths, home, hidden, mixed, router, row, cotangent, tokens, router_full, misc_full, output_weight, att, lse, qkv, normed, wqkv)
    layer_out, tokens_grad, query_grad, key_grad, value_grad, output_grad, router_grad, bias_grad = finish(*results)
    return (
        layer_out,
        tokens_grad,
        gain_sum[0:3].reshape(HALF),
        query_grad,
        key_grad,
        value_grad,
        output_grad,
        bias_grad,
        gain_sum[3:6].reshape(HALF),
        router_grad,
        expert_in_grad,
        expert_out_grad,
    )


def solution(mesh):
    by_token = P(("expert", "wshard"), None)
    by_row = P("wshard", None)
    by_expert = P(("expert", "wshard"), None, None)
    return jax.shard_map(
        per_device,
        mesh=mesh,
        in_specs=(
            by_token,
            P(),
            by_token,
            P("wshard"),
            by_row,
            by_row,
            by_row,
            by_row,
            by_row,
            P("wshard"),
            by_row,
            by_expert,
            by_expert,
            by_token,
        ),
        out_specs=(
            by_token,
            by_token,
            P("wshard"),
            by_row,
            by_row,
            by_row,
            by_row,
            by_row,
            P("wshard"),
            by_row,
            by_expert,
            by_expert,
        ),
        check_vma=False,
    )
```

```python
import functools

import jax
import jax.numpy as jnp
from jax import lax
from jax.experimental import pallas as pl
from jax.experimental.pallas import tpu as pltpu
from jax.sharding import PartitionSpec as P

MESH = pl.DeviceIdType.MESH
BF = jnp.bfloat16
F32 = jnp.float32
EPSILON = 1e-06
FAR_EDGES = (12, 16, 23, 32, 46, 64, 91)

D = 768
HALF = 384
HEAD = 64
TOK = 128
CHIP = 256
REACH = 4
SLOTS = 2 * REACH + 1
WIN = SLOTS * CHIP
MID = REACH * CHIP
TOTAL = 16384
EXPERTS = 128
NB = 32
FF = 3072
NEAR = 3 * CHIP
LOOP = 1024
VMEM_BYTES = 56 * 1024 * 1024

NT = (((1,), (1,)), ((), ()))
TN = (((0,), (0,)), ((), ()))
NN = (((1,), (0,)), ((), ()))


def mm(left, right, dims=NN):
    return lax.dot_general(left, right, dims, preferred_element_type=F32)


def bucket_of(relative):
    distance = jnp.abs(relative)
    far_bucket = 8 + sum(((distance >= edge).astype(jnp.int32) for edge in FAR_EDGES))
    near_far = jnp.where(distance < 8, distance, far_bucket)
    return near_far + 16 * (relative > 0).astype(jnp.int32)


def tile(ref, rows, start, width):
    return ref[rows, pl.ds(pl.multiple_of(start, 128), width)]


OFFSETS = (1, -1, 4, -4, 3, -3, 2, -2)
DIRECT = 6
AXES = {"y": 16, "x": 4, "z": 1}


def remote(src, dst, ssem, rsem, chip, core):
    return pltpu.make_async_remote_copy(src_ref=src, dst_ref=dst, send_sem=ssem, recv_sem=rsem, device_id=(chip, core), device_id_type=MESH)


def chip_at(e, m):
    chips = lax.axis_size("expert")
    return lax.rem(e + m + chips, chips)


def signal(barrier, chip, core):
    pl.semaphore_signal(barrier, inc=1, device_id=(chip, core), device_id_type=MESH)


def chunk(c):
    return slice(c * CHIP, (c + 1) * CHIP)


def both_gains(misc, row):
    return jnp.concatenate([misc[row : row + 1, :], misc[row + 24 : row + 25, :]], axis=1)


def placing(routes_row):
    lane = lax.broadcasted_iota(jnp.int32, (TOK, EXPERTS), 1)
    row = lax.broadcasted_iota(jnp.int32, (TOK, EXPERTS), 0)
    across = jnp.broadcast_to(routes_row[0:1, :], (TOK, TOK))
    down = across.T
    chosen = (down == lane).astype(F32)
    earlier = ((down == across) & (lane < row)).astype(F32)
    second = jnp.max(earlier, axis=1, keepdims=True)
    return chosen, (chosen * (1.0 - second)).astype(BF), (chosen * second).astype(BF)


def prepare(lengths, mask):
    e = lax.axis_index("expert")
    row_pos = (e - REACH) * CHIP + lax.broadcasted_iota(jnp.int32, (8, WIN), 1)
    col_pos = e * CHIP + lax.broadcasted_iota(jnp.int32, (CHIP, 128), 0)

    def count(n, state):
        end, rows, cols = state
        end = end + lengths[n]
        return end, rows + (row_pos >= end).astype(jnp.int32), cols + (col_pos >= end).astype(jnp.int32)

    zero = jnp.zeros((8, WIN), jnp.int32)
    _, rows, cols = lax.fori_loop(0, 32, count, (jnp.int32(0), zero, jnp.zeros((CHIP, 128), jnp.int32)))
    rows = jnp.where((row_pos >= 0) & (row_pos < TOTAL), rows, -1)
    for c in range(SLOTS):
        part = rows[0:1, c * CHIP : (c + 1) * CHIP]
        mask[:, c * CHIP : (c + 1) * CHIP] = jnp.where(cols[:, 0:1] == part, 0.0, -1e9).astype(F32)


def prepare_biases(misc, diag, ways):
    table = jnp.concatenate([misc[0:16, 0:128], misc[24:40, 0:128]], axis=0).astype(BF)
    for n, sign in enumerate(ways):
        hot = diagonal_buckets(sign)
        diag[n * 16 : (n + 1) * 16, :] = mm(table, hot.astype(BF), TN)[0:16]


def diagonal_buckets(sign):
    m = lax.broadcasted_iota(jnp.int32, (NB, LOOP), 1)
    r = jnp.where(m < NEAR, m, m - LOOP) - CHIP
    b = lax.broadcasted_iota(jnp.int32, (NB, LOOP), 0)
    return (bucket_of(sign * r) == b).astype(F32)


def biased(raw, c, mask, near, left, right):
    s = raw + mask[:, c * CHIP : (c + 1) * CHIP]
    if c < REACH - 1:
        return s + left
    if c > REACH + 1:
        return s + right
    lower = (c - REACH + 1) * CHIP
    return s + near[:, lower : lower + CHIP]


def near_tile(diag, row):
    line = diag[pl.ds(row, 1), :]
    spread = pltpu.roll(jnp.broadcast_to(line, (8, LOOP)), 0, 1, stride=1, stride_axis=0)
    rows = 8
    while rows < CHIP:
        spread = jnp.concatenate([spread, pltpu.roll(spread, rows, 1)], axis=0)
        rows *= 2
    return spread[:, 0:NEAR], line[:, 0:1], line[:, NEAR - 1 : NEAR]


def front_kernel(lengths, tok_any, wq, wk, wv, wo_any, router_any, gain_one, gain_two, bias_rows, tok, wo, routes_row, cot, qkv_any, normed_any, wqkv_any, router_full, misc, att, lse, hidden, mixed, router, sent, qkv, normed, wqkv, misc_mine, win, wo_other, att_other, mask, diag, scores, lse_cols, send, recv, fsend, frecv, wsend, wrecv, local, store):
    e = lax.axis_index("expert")
    j = lax.axis_index("wshard")
    jp = 1 - j
    barrier = pltpu.get_barrier_semaphore()
    for m in OFFSETS:
        signal(barrier, chip_at(e, m), j)
    signal(barrier, e, jp)

    def rows_of(slot, core):
        return win.at[pl.ds(pl.multiple_of(slot * CHIP + core * TOK, TOK), TOK), :]

    misc_mine[...] = jnp.zeros((24, HALF), F32)
    misc_mine[16:17, :] = gain_one[...].astype(F32).reshape(1, HALF)
    misc_mine[17:18, :] = gain_two[...].astype(F32).reshape(1, HALF)
    misc_mine[0:16, 0:12] = bias_rows[...].astype(F32)
    weights = []
    kept = []
    for n, w in enumerate((wq, wk, wv)):
        rows = pl.ds(pl.multiple_of(j * HALF, HALF), HALF)
        there = w.at[:, pl.ds(pl.multiple_of(jp * HALF, 128), HALF)]
        here = w.at[:, pl.ds(pl.multiple_of(j * HALF, 128), HALF)]
        dst = wqkv.at[rows, n * HALF : (n + 1) * HALF]
        weights.append(remote(there, dst, wsend.at[n], wrecv.at[n], e, jp))
        kept.append(pltpu.make_async_copy(here, dst, local.at[1 + n]))
    for n, (src, dst, size) in enumerate(((misc_mine, misc, 24), (router_any, router_full, HALF))):
        rows = pl.ds(pl.multiple_of(j * size, 8), size)
        weights.append(remote(src, dst.at[rows, :], wsend.at[3 + n], wrecv.at[3 + n], e, jp))
        kept.append(pltpu.make_async_copy(src, dst.at[rows, :], local.at[4 + n]))
    weights.append(remote(wo_any, wo_other, wsend.at[5], wrecv.at[5], e, jp))
    mine = pltpu.make_async_copy(tok_any, rows_of(REACH, j), local.at[0])
    mine.start()
    for c in kept:
        c.start()

    copies = []
    for n, m in enumerate(OFFSETS):
        src = tok_any if n < DIRECT else rows_of(REACH - m // 2, j)
        to = chip_at(e, m if n < DIRECT else m // 2)
        copies.append(remote(src, rows_of(REACH - m, j), send.at[n], recv.at[n], to, j))
    passed = [remote(rows_of(REACH - m, j), rows_of(REACH - m, j), fsend.at[n], frecv.at[n], e, jp) for n, m in enumerate(OFFSETS)]
    swap = remote(tok_any, rows_of(REACH, j), fsend.at[8], frecv.at[8], e, jp)

    pl.semaphore_wait(barrier, len(OFFSETS) + 1)
    for c in copies[:DIRECT]:
        c.start()
    weights[3].start()
    for c in weights[:3]:
        c.start()
    swap.start()
    for c in weights[4:]:
        c.start()
    prepare(lengths, mask)
    mine.wait()
    for c in kept:
        c.wait()
    for c in weights[:4]:
        c.wait_recv()
    prepare_biases(misc, diag, (1,))
    gain = both_gains(misc, 16)

    def project(slot):
        x = win[chunk(slot), :].astype(F32)
        y = (x * lax.rsqrt(jnp.mean(x * x, axis=-1, keepdims=True) + EPSILON) * gain).astype(BF)
        if slot == REACH:
            normed[...] = y
        qkv[chunk(slot), :] = mm(y, wqkv[...]).astype(BF)

    for n in range(2):
        copies[n].wait_recv()
        copies[DIRECT + n].start()
        passed[n].start()
    swap.wait_recv()
    project(REACH)
    for n in range(2, len(OFFSETS) + 2):
        if n < len(OFFSETS):
            copies[n].wait_recv()
            passed[n].start()
        passed[n - 2].wait_recv()
        project(REACH - OFFSETS[n - 2])

    stores = [pltpu.make_async_copy(src, dst, store.at[n]) for n, (src, dst) in enumerate(((qkv, qkv_any), (normed, normed_any), (wqkv, wqkv_any)))]
    for c in stores:
        c.start()
    lane = lax.broadcasted_iota(jnp.int32, (CHIP, 128), 1)
    lse_cols[...] = jnp.zeros((CHIP, 128), F32)

    def pair(p, carry):
        q = tile(qkv, slice(MID, MID + CHIP), p * 128, 128).astype(F32) * 0.125
        outs = []
        for hh in range(2):
            own = (lane // HEAD) == hh
            qm = jnp.where(own, q, 0.0).astype(BF)
            near, left, right = near_tile(diag, j * 6 + 2 * p + hh)
            top = None
            for c in range(SLOTS):
                k = tile(qkv, chunk(c), HALF + p * 128, 128)
                s = biased(mm(qm, k, NT), c, mask, near, left, right)
                scores[:, chunk(c)] = s
                top = s if top is None else jnp.maximum(top, s)
            top = jnp.max(top, axis=1, keepdims=True)
            total = jnp.zeros((CHIP, CHIP), F32)
            out = jnp.zeros((CHIP, 128), F32)
            for c in range(SLOTS):
                x = jnp.exp(scores[:, chunk(c)] - top)
                total = total + x
                out = out + mm(x.astype(BF), tile(qkv, chunk(c), 2 * HALF + p * 128, 128))
            total = jnp.sum(total, axis=1, keepdims=True)
            outs.append(out / total)
            lse_cols[...] = jnp.where(lane == 2 * p + hh, top + jnp.log(total), lse_cols[...])
        att[:, pl.ds(pl.multiple_of(p * 128, 128), 128)] = jnp.where(lane < HEAD, outs[0], outs[1]).astype(BF)
        return carry

    lax.fori_loop(0, 3, pair, 0)
    lse[...] = lse_cols[...].T[0:8, :]

    here = pl.ds(pl.multiple_of(j * TOK, TOK), TOK)
    there = pl.ds(pl.multiple_of(jp * TOK, TOK), TOK)
    trade = remote(att.at[there, :], att_other, wsend.at[6], wrecv.at[6], e, jp)
    trade.start()
    chosen, first, second = placing(routes_row)
    branch = mm(att[here, :], wo[...])
    for c in weights[4:]:
        c.wait_recv()
    trade.wait_recv()
    total = tok[...].astype(F32) + (branch + mm(att_other[...], wo_other[...]))
    hidden[...] = total
    low = (total * lax.rsqrt(jnp.mean(total * total, axis=-1, keepdims=True) + EPSILON) * both_gains(misc, 17)).astype(BF)
    mixed[...] = low
    logits = mm(low, router_full[...])
    powers = jnp.exp(logits - jnp.max(logits, axis=1, keepdims=True))
    probs = powers / jnp.sum(powers, axis=1, keepdims=True)
    router[...] = probs
    gate = jnp.sum(probs * chosen, axis=1, keepdims=True)
    made_grad = (gate * cot[...].astype(F32)).astype(BF)
    for n, (place, rows) in enumerate(((first, low), (second, low), (first, made_grad), (second, made_grad))):
        sent[n] = mm(place, rows, TN).astype(BF)

    trade.wait_send()
    swap.wait_send()
    for c in weights + copies + passed:
        c.wait_send()
    for c in stores:
        c.wait()


def front(lengths, tokens, wq, wk, wv, wo, router, gain_one, gain_two, bias, row, cotangent):
    smem = pl.BlockSpec(memory_space=pltpu.SMEM)
    hbm = pl.BlockSpec(memory_space=pl.ANY)
    vm = pl.BlockSpec(memory_space=pltpu.VMEM)
    return pl.pallas_call(
        front_kernel,
        name="front",
        out_shape=(
            jax.ShapeDtypeStruct((WIN, 3 * HALF), BF),
            jax.ShapeDtypeStruct((CHIP, D), BF),
            jax.ShapeDtypeStruct((D, 3 * HALF), BF),
            jax.ShapeDtypeStruct((D, EXPERTS), BF),
            jax.ShapeDtypeStruct((48, HALF), F32),
            jax.ShapeDtypeStruct((CHIP, HALF), BF),
            jax.ShapeDtypeStruct((8, CHIP), F32),
            jax.ShapeDtypeStruct((TOK, D), F32),
            jax.ShapeDtypeStruct((TOK, D), BF),
            jax.ShapeDtypeStruct((TOK, EXPERTS), F32),
            jax.ShapeDtypeStruct((4, EXPERTS, D), BF),
        ),
        in_specs=[smem] + [hbm] * 6 + [vm] * 7,
        out_specs=(hbm,) * 3 + (vm,) * 8,
        scratch_shapes=[
            pltpu.VMEM((WIN, 3 * HALF), BF),
            pltpu.VMEM((CHIP, D), BF),
            pltpu.VMEM((D, 3 * HALF), BF),
            pltpu.VMEM((24, HALF), F32),
            pltpu.VMEM((WIN, D), BF),
            pltpu.VMEM((HALF, D), BF),
            pltpu.VMEM((TOK, HALF), BF),
            pltpu.VMEM((CHIP, WIN), F32),
            pltpu.VMEM((16, LOOP), F32),
            pltpu.VMEM((CHIP, WIN), F32),
            pltpu.VMEM((CHIP, 128), F32),
            pltpu.SemaphoreType.DMA((8,)),
            pltpu.SemaphoreType.DMA((8,)),
            pltpu.SemaphoreType.DMA((9,)),
            pltpu.SemaphoreType.DMA((9,)),
            pltpu.SemaphoreType.DMA((7,)),
            pltpu.SemaphoreType.DMA((7,)),
            pltpu.SemaphoreType.DMA((6,)),
            pltpu.SemaphoreType.DMA((3,)),
        ],
        compiler_params=pltpu.CompilerParams(collective_id=1, has_side_effects=True, vmem_limit_bytes=VMEM_BYTES),
    )(lengths, tokens, wq, wk, wv, wo, router, gain_one, gain_two, bias, tokens, wo, row, cotangent)


FF_TILE = 512


def expert_kernel(x, g, w_in, w_out, made_back, d_in, d_out, made_sum, back_sum, across):
    step = pl.program_id(0)

    @pl.when(step == 0)
    def _():
        made_sum[...] = jnp.zeros_like(made_sum)
        back_sum[...] = jnp.zeros_like(back_sum)
        across[...] = x[...].T

    pre = mm(x[...], w_in[0])
    half_erf = 0.5 * lax.erf(pre * (0.5**0.5)) + 0.5
    act = (pre * half_erf).astype(BF)
    slope = half_erf + pre * jnp.exp(-0.5 * pre * pre) * (0.5 * 0.7978845608028654)
    act_grad = mm(g[...], w_out[0], NT)
    pre_grad = (act_grad * slope).astype(BF)
    made_sum[...] += mm(act, w_out[0])
    back_sum[...] += mm(pre_grad, w_in[0], NT)
    d_out[0] = mm(act, g[...], TN).astype(BF)
    d_in[0] = mm(across[...], pre_grad).astype(BF)

    @pl.when(step == pl.num_programs(0) - 1)
    def _():
        made_back[0 : 2 * EXPERTS, :] = made_sum[...].astype(BF)
        made_back[2 * EXPERTS :, :] = back_sum[...].astype(BF)


def expert(arrived, w_in, w_out):
    rows = 2 * EXPERTS
    forward = pl.BlockSpec((rows, D), lambda f: (0, 0))
    backward = pl.BlockSpec((rows, D), lambda f: (1, 0))
    whole = pl.BlockSpec((2 * rows, D), lambda f: (0, 0))
    by_in = pl.BlockSpec((1, D, FF_TILE), lambda f: (0, 0, f))
    by_out = pl.BlockSpec((1, FF_TILE, D), lambda f: (0, f, 0))
    return pl.pallas_call(
        expert_kernel,
        name="expert",
        grid=(FF // FF_TILE,),
        out_shape=(
            jax.ShapeDtypeStruct((2 * rows, D), BF),
            jax.ShapeDtypeStruct((1, D, FF), BF),
            jax.ShapeDtypeStruct((1, FF, D), BF),
        ),
        in_specs=[forward, backward, by_in, by_out],
        out_specs=(whole, by_in, by_out),
        scratch_shapes=[pltpu.VMEM((rows, D), F32), pltpu.VMEM((rows, D), F32), pltpu.VMEM((D, rows), BF)],
        compiler_params=pltpu.CompilerParams(vmem_limit_bytes=VMEM_BYTES, dimension_semantics=("arbitrary",)),
    )(arrived, arrived, w_in, w_out)


ORDERS = ("zxy", "xyz", "yzx")
EARLY_ORDERS = ("yxz",)
RING = 16
PLANE = [(d, f) for d in range(4) for f in range(4) if d + f > 0]


class Sum:
    def __init__(self, e, j, order, part, ring, plane, ring_sum, plane_sum, all_, ring_sems, plane_sems):
        self.e, self.j, self.order = e, j, order
        self.part, self.ring, self.plane, self.ring_sum, self.plane_sum, self.all = part, ring, plane, ring_sum, plane_sum, all_
        self.ring_sems, self.plane_sems = ring_sems, plane_sems
        self.coord = [lax.rem(e // AXES[a], 4) for a in order]

    def peer(self, *steps):
        to = self.e
        for axis, at, d in zip(self.order, self.coord, steps):
            to = to + (lax.rem(at + d, 4) - at) * AXES[axis]
        return to

    def block(self, d, first, count):
        return pl.ds(lax.rem(self.coord[0] + d + 4, 4) * RING + first, count)

    def copy(self, src, dst, sems, n, to):
        return remote(src, dst, sems[0].at[n], sems[1].at[n], to, self.j)

    def reduce_copies(self, which):
        h = RING // 2
        up, down = self.peer(1), self.peer(3)
        pieces = [
            (lambda: self.part.at[:, self.block(2, 0, h)], up),
            (lambda: self.part.at[:, self.block(2, h, h)], down),
            (lambda: self.part.at[:, self.block(1, h, h)], up),
            (lambda: self.part.at[:, self.block(3, 0, h)], down),
            (lambda: self.ring.at[6], up),
            (lambda: self.ring.at[7], down),
        ]
        return [self.copy(pieces[n][0](), self.ring.at[n], self.ring_sems, n, pieces[n][1]) for n in which]

    def gather_copies(self, which):
        h = RING // 2
        up, down = self.peer(1), self.peer(3)
        pieces = [(0, 0, RING, up), (0, 0, RING, down), (-1, 0, h, up), (1, h, h, down)]
        found = []
        for n in which:
            d, first, count, to = pieces[n]
            ref = self.all.at[:, self.block(d, first, count)]
            found.append(self.copy(ref, ref, self.ring_sems, 6 + n, to))
        return found

    def plane_copies(self, back):
        found = []
        for n, (d, f) in enumerate(PLANE):
            to = self.peer(0, d, f)
            if back:
                ref = self.all.at[:, pl.ds(self.coord[0] * RING + self.coord[1] * 4 + self.coord[2], 1)]
                found.append(self.copy(ref, ref, self.plane_sems, 15 + n, to))
            else:
                place = lax.rem(self.coord[1] + d, 4) * 4 + lax.rem(self.coord[2] + f, 4)
                found.append(self.copy(self.ring_sum.at[:, pl.ds(place, 1)], self.plane.at[n], self.plane_sems, n, to))
        return found

    def start_ring(self):
        for c in self.reduce_copies(range(4)):
            c.start()

    def pass_ring(self):
        h = RING // 2
        for n, where in ((0, self.block(1, 0, h)), (1, self.block(3, h, h))):
            came, goes = self.reduce_copies((n, 4 + n))
            came.wait_recv()
            self.ring[6 + n] = (self.part[:, where].astype(F32) + self.ring[n].astype(F32)).astype(BF)
            goes.start()

    def ring_to_plane(self):
        h = RING // 2
        for c in self.reduce_copies(range(2, 6)):
            c.wait_recv()
        for first, others in ((0, (4, 3)), (h, (5, 2))):
            total = self.part[:, self.block(0, first, h)].astype(F32)
            for n in others:
                total = total + self.ring[n].astype(F32)
            self.ring_sum[:, first : first + h] = total.astype(BF)
        for c in self.plane_copies(False):
            c.start()

    def plane_back(self):
        own = self.coord[1] * 4 + self.coord[2]
        total = self.ring_sum[:, pl.ds(own, 1)].astype(F32)
        for n, c in enumerate(self.plane_copies(False)):
            c.wait_recv()
            total = total + self.plane[n].astype(F32)
        self.all[:, pl.ds(self.coord[0] * RING + own, 1)] = total.astype(BF)
        for c in self.plane_copies(True):
            c.start()

    def plane_to_ring(self):
        for c in self.plane_copies(True):
            c.wait_recv()
        for c in self.gather_copies((0, 1)):
            c.start()

    def pass_back(self):
        for n in range(2):
            came, goes = self.gather_copies((n, 2 + n))
            came.wait_recv()
            goes.start()

    def end(self):
        for c in self.gather_copies((2, 3)):
            c.wait_recv()

    def end_sends(self):
        for c in self.reduce_copies(range(6)) + self.plane_copies(False) + self.plane_copies(True) + self.gather_copies(range(4)):
            c.wait_send()


def sum_scratch(units):
    return [
        pltpu.VMEM((units, 64, 16, 128), BF),
        pltpu.VMEM((8, units, RING // 2, 16, 128), BF),
        pltpu.VMEM((15, units, 1, 16, 128), BF),
        pltpu.VMEM((units, RING, 16, 128), BF),
        pltpu.VMEM((units, 1, 16, 128), BF),
        pltpu.VMEM((units, 64, 16, 128), BF),
        pltpu.SemaphoreType.DMA((10,)),
        pltpu.SemaphoreType.DMA((10,)),
        pltpu.SemaphoreType.DMA((30,)),
        pltpu.SemaphoreType.DMA((30,)),
    ]


def sums_of(e, j, orders, scratch):
    found = []
    for n, order in enumerate(orders):
        s = scratch[10 * n : 10 * n + 10]
        found.append(Sum(e, j, order, *s[:6], s[6:8], s[8:10]))
    return found


LATE = (3, 2, 2)
EARLY = (3,)
OWN = 216


def spots(units, first, count):
    table = [(n, u) for n in range(len(units)) for u in range(units[n])]
    done = 0
    while done < count:
        unit, place = divmod(first + done, 64)
        n = min(64 - place, count - done)
        yield table[unit] + (place, n, done)
        done += n


def tiles(value):
    return value.astype(BF).reshape(value.shape[0] // 16, 16, 128)


def rows_of_tiles(value):
    return value.reshape(value.shape[0] * 16, 128)


def back_kernel(lengths, home, hidden, mixed, router, routes_row, cot, tok, router_full, misc, wo, att, lse, qkv_any, normed_any, wqkv_any, layer_out, tokens_grad, q_sum, k_sum, v_sum, out_sum, router_sum, bias_sum, gain_sum, qkv, normed, wqkv, mask, diag, dout, stat, cols, dqkv, bias, branch, hidden_grad, half_out, half_in, grads, router_grad, stage, small, send, recv, core_send, core_recv, local, acc, *scratch):
    e = lax.axis_index("expert")
    j = lax.axis_index("wshard")
    jp = 1 - j
    here = pl.ds(pl.multiple_of(j * TOK, TOK), TOK)
    there = pl.ds(pl.multiple_of(jp * TOK, TOK), TOK)
    barrier = pltpu.get_barrier_semaphore()
    early, late = sums_of(e, j, EARLY_ORDERS, scratch[:10]), sums_of(e, j, ORDERS, scratch[10:])
    for m in OFFSETS:
        signal(barrier, chip_at(e, m), j)
    for n in range(1, 64):
        steps = (n // 16, n // 4 % 4, n % 4)
        if 0 in steps:
            signal(barrier, early[0].peer(*steps), j)
    signal(barrier, e, jp)

    loads = [pltpu.make_async_copy(src, dst, local.at[n]) for n, (src, dst) in enumerate(((qkv_any, qkv), (normed_any, normed), (wqkv_any, wqkv)))]
    for c in loads:
        c.start()

    chosen, first, second = placing(routes_row)
    probs = router[...]
    gate = jnp.sum(probs * chosen, axis=1, keepdims=True)
    made = mm(first, home[0]) + mm(second, home[1])
    expert_back = mm(first, home[2]) + mm(second, home[3])
    total = hidden[...]
    layer_out[...] = (total + gate * made).astype(BF)
    dy = cot[...].astype(F32)
    gate_grad = jnp.sum(dy * made, axis=1, keepdims=True)
    logit_grad = ((gate_grad * gate) * (chosen - probs)).astype(BF)
    mixed_grad = mm(logit_grad, router_full[...], NT) + expert_back
    r = lax.rsqrt(jnp.mean(total * total, axis=-1, keepdims=True) + EPSILON)
    w = mixed_grad * both_gains(misc, 17)
    mix_gain = jnp.sum(mixed_grad * total * r, axis=0, keepdims=True)
    rest = dy + (r * w - total * (r * r * r * jnp.mean(w * total, axis=-1, keepdims=True)))
    hidden_grad[...] = rest
    branch[here, :] = rest.astype(BF)

    pl.semaphore_wait(barrier, len(OFFSETS) + 37)
    trade = remote(branch.at[here, :], branch.at[here, :], core_send.at[0], core_recv.at[0], e, jp)
    trade.start()
    router_grad[...] = tiles(mm(mixed[...], logit_grad, TN))
    router_rows = lambda core: router_grad.at[pl.ds(core * 24, 24)]
    router_trade = remote(router_rows(jp), early[0].part.at[2, 40:64], core_send.at[1], core_recv.at[1], e, jp)
    router_trade.start()
    early[0].part[2, 16:40] = router_grad[pl.ds(j * 24, 24)]
    prepare(lengths, mask)
    prepare_biases(misc, diag, (1, -1))
    trade.wait_recv()

    lane = lax.broadcasted_iota(jnp.int32, (CHIP, 128), 1)
    mid = slice(MID, MID + CHIP)
    att_grad = mm(branch[...], wo[...], NT).astype(BF)
    dout[mid, :] = att_grad
    both = att_grad.astype(F32) * att[...].astype(F32)
    dots = jnp.zeros((CHIP, 128), F32)
    for h in range(6):
        own = (lane // HEAD) == h % 2
        dot = jnp.sum(jnp.where(own, both[:, (h // 2) * 128 : (h // 2) * 128 + 128], 0.0), axis=1, keepdims=True)
        dots = jnp.where(lane == h, dot, dots)
    stat[REACH, 0:8] = lse[...]
    stat[REACH, 8:16] = dots.T[0:8, :]
    cols[...] = jnp.concatenate([stat[REACH], jnp.zeros((112, CHIP), F32)], axis=0).T

    def window_copies(n):
        m = OFFSETS[n]
        slot = REACH if n < DIRECT else REACH - m // 2
        to = chip_at(e, m if n < DIRECT else m // 2)
        return [
            remote(dout.at[chunk(slot), :], dout.at[chunk(REACH - m), :], send.at[n, 0], recv.at[n, 0], to, j),
            remote(stat.at[slot], stat.at[REACH - m], send.at[n, 1], recv.at[n, 1], to, j),
        ]

    for n in range(DIRECT):
        for c in window_copies(n):
            c.start()
    grad = mm(att[...], branch[...], TN)
    for c in range(6):
        cut = tiles(grad[:, c * 128 : (c + 1) * 128])
        for n, unit, place, count, done in spots(EARLY, 24 * c, 24):
            early[n].part[unit, place : place + count] = cut[done : done + count]
    router_trade.wait_recv()
    for s in early:
        s.start_ring()
    for c in loads:
        c.wait()

    def forward_window():
        for n in range(2):
            for c in window_copies(n):
                c.wait_recv()
            for c in window_copies(DIRECT + n):
                c.start()

    def pass_early():
        for s in early:
            s.pass_ring()

    line = lax.broadcasted_iota(jnp.int32, (NB, 128), 1)
    row32 = lax.broadcasted_iota(jnp.int32, (NB, 128), 0)
    hot = diagonal_buckets(1)
    bias[...] = jnp.zeros((NB, 128), F32)

    def by_queries(p, carry):
        q = tile(qkv, mid, p * 128, 128).astype(F32) * 0.125
        do = tile(dout, mid, p * 128, 128)
        found = []
        for hh in range(2):
            h = 2 * p + hh
            own = (lane // HEAD) == hh
            spare = (1 - hh) * HEAD
            qm = jnp.where(own, q, 0.0).astype(BF)
            dom = jnp.where(own, do, jnp.zeros_like(do))
            log_sum = jnp.sum(jnp.where(lane == h, cols[...], 0.0), axis=1, keepdims=True)
            dot = jnp.sum(jnp.where(lane == h + 8, cols[...], 0.0), axis=1, keepdims=True)
            near, left, right = near_tile(diag, j * 6 + h)
            dq = jnp.zeros((CHIP, 128), F32)
            near_grads = []
            for c in range(SLOTS):
                k = tile(qkv, chunk(c), HALF + p * 128, 128)
                v = tile(qkv, chunk(c), 2 * HALF + p * 128, 128)
                s = biased(mm(qm, k, NT), c, mask, near, left, right)
                ds = jnp.exp(s - log_sum) * (mm(dom, v, NT) - dot)
                if c < REACH - 1:
                    other = jnp.where(lane == spare, 1.0, 0.0).astype(BF)
                elif c > REACH + 1:
                    other = jnp.where(lane == spare + 1, 1.0, 0.0).astype(BF)
                else:
                    other = jnp.zeros((CHIP, 128), BF)
                    near_grads.append(ds)
                dq = dq + mm(ds.astype(BF), jnp.where(own, k, other))
            found.append(dq * 0.125)
            fold = jnp.concatenate(near_grads + [jnp.zeros((CHIP, CHIP), F32)], axis=1)
            rows = CHIP
            while rows > 8:
                rows //= 2
                fold = fold[0:rows] + pltpu.roll(fold[rows : 2 * rows], LOOP - rows, 1)
            summed = fold[0:1]
            for n in range(1, 8):
                summed = summed + pltpu.roll(fold[n : n + 1], LOOP - n, 1)
            by_bucket = jnp.sum(hot * summed, axis=1, keepdims=True)
            far = jnp.sum(dq, axis=0, keepdims=True)
            by_bucket = by_bucket + jnp.where(row32 == 15, far[:, spare : spare + 1], 0.0) + jnp.where(row32 == 31, far[:, spare + 1 : spare + 2], 0.0)
            bias[...] = jnp.where(line == j * 6 + h, by_bucket, bias[...])
            if hh == 0:
                pl.when(p == 0)(forward_window)
                pl.when(p == 2)(pass_early)
        dqkv[:, pl.ds(pl.multiple_of(p * 128, 128), 128)] = jnp.where(lane < HEAD, found[0], found[1]).astype(BF)
        return carry

    lax.fori_loop(0, 3, by_queries, 0)

    def by_keys(slots, p, carry):
        k_own = tile(qkv, mid, HALF + p * 128, 128)
        v_own = tile(qkv, mid, 2 * HALF + p * 128, 128)
        found = []
        for hh in range(2):
            h = 2 * p + hh
            own = (lane // HEAD) == hh
            km = jnp.where(own, k_own, jnp.zeros_like(k_own))
            vm = jnp.where(own, v_own, jnp.zeros_like(v_own))
            if REACH in slots:
                near, left, right = near_tile(diag, 16 + j * 6 + h)
            else:
                ends = diag[pl.ds(16 + j * 6 + h, 1), :]
                near, left, right = None, ends[:, 0:1], ends[:, NEAR - 1 : NEAR]
            dk = jnp.zeros((CHIP, 128), F32)
            dv = jnp.zeros((CHIP, 128), F32)
            for c in slots:
                qc = (tile(qkv, chunk(c), p * 128, 128).astype(F32) * 0.125).astype(BF)
                dc = tile(dout, chunk(c), p * 128, 128)
                s = biased(mm(km, qc, NT), c, mask, near, left, right)
                prob = jnp.exp(s - stat[c, pl.ds(h, 1), :])
                ds = prob * (mm(vm, dc, NT) - stat[c, pl.ds(h + 8, 1), :])
                dv = dv + mm(prob.astype(BF), dc)
                dk = dk + mm(ds.astype(BF), qc)
            found.append((dk, dv))
        for n in range(2):
            where = pl.ds(pl.multiple_of(n * HALF + p * 128, 128), 128)
            both = jnp.where(lane < HEAD, found[0][n], found[1][n])
            acc[:, where] = both if REACH in slots else acc[:, where] + both
        return carry

    for n, slots in ((1, (REACH, 3, 5)), (2, (0, 8)), (4, (1, 7)), (6, (2, 6))):
        if n > 1:
            for c in window_copies(n) + window_copies(n + 1):
                c.wait_recv()
        lax.fori_loop(0, 3, functools.partial(by_keys, slots), 0)
        if n == 1:
            for s in early:
                s.ring_to_plane()
        elif n == 4:
            for s in early:
                s.plane_back()
    dqkv[:, HALF:] = acc[...].astype(BF)

    half_out[...] = mm(dqkv[there, :], wqkv[...], NT).astype(BF)
    half_trade = remote(half_out, half_in, core_send.at[2], core_recv.at[2], e, jp)
    half_trade.start()
    whole = tuple(s.part for s in late)
    swaps = []
    for n, unit, place, count, done in spots(LATE, OWN, OWN):
        swaps.append((done + count, remote(stage.at[done : done + count], whole[n].at[unit, place : place + count], core_send.at[4 + len(swaps)], core_recv.at[4 + len(swaps)], e, jp)))
    sent = 0
    for third in range(3):
        grad = mm(normed[...], dqkv[:, third * HALF : (third + 1) * HALF], TN)
        for c in range(3 * third, 3 * third + 3):
            grads[c % 3] = tiles(grad[:, (c % 3) * 128 : (c % 3 + 1) * 128])
            stage[24 * c : 24 * c + 24] = grads[c % 3, pl.ds(24 * jp, 24)]
            for n, unit, place, count, done in spots(LATE, 24 * c, 24):
                whole[n][unit, place : place + count] = grads[c % 3, pl.ds(24 * j + done, count)]
        while sent < len(swaps) and swaps[sent][0] <= 72 * (third + 1):
            swaps[sent][1].start()
            sent += 1
    late[0].start_ring()
    for s in early:
        s.plane_to_ring()

    half = mm(dqkv[here, :], wqkv[...], NT)
    half_trade.wait_recv()
    grad = half + half_in[...].astype(F32)
    x = tok[...].astype(F32)
    r = lax.rsqrt(jnp.mean(x * x, axis=-1, keepdims=True) + EPSILON)
    w = grad * both_gains(misc, 16)
    tokens_grad[...] = (hidden_grad[...] + (r * w - x * (r * r * r * jnp.mean(w * x, axis=-1, keepdims=True)))).astype(BF)
    attn_gain = jnp.sum(grad * x * r, axis=0, keepdims=True)
    for h in range(2):
        lines = [v[:, h * HALF + 128 * n : h * HALF + 128 * n + 128] for v in (attn_gain, mix_gain) for n in range(3)]
        small[2 * h] = bias[16 * h : 16 * h + 16, :].astype(BF)
        small[2 * h + 1] = jnp.concatenate(lines + [jnp.zeros((10, 128), F32)], axis=0).astype(BF)
    last = whole[2]
    last[1, 52:64] = jnp.zeros((12, 16, 128), BF)
    last[1, 48:50] = small[pl.ds(2 * j, 2)]
    small_trade = remote(small.at[pl.ds(2 * jp, 2)], last.at[1, 50:52], core_send.at[3], core_recv.at[3], e, jp)
    small_trade.start()
    late[0].pass_ring()
    for _, c in swaps:
        c.wait_recv()
    late[1].start_ring()
    small_trade.wait_recv()
    late[2].start_ring()
    for s in early:
        s.pass_back()
    for s in late[1:]:
        s.pass_ring()
    for s in late:
        s.ring_to_plane()

    for s in early:
        s.end()
    for c in range(6):
        for n, unit, place, count, done in spots(EARLY, 24 * c, 24):
            out_sum[16 * done : 16 * (done + count), c * 128 : (c + 1) * 128] = rows_of_tiles(early[n].all[unit, place : place + count])
    router_sum[...] = rows_of_tiles(early[0].all[2, 16:40].astype(F32) + early[0].all[2, 40:64].astype(F32))

    for step in ("plane_back", "plane_to_ring", "pass_back", "end"):
        for s in late:
            getattr(s, step)()
    sums = (q_sum, k_sum, v_sum)
    for c in range(9):
        for first_tile, core in ((24 * c, j), (OWN + 24 * c, jp)):
            column = pl.ds(pl.multiple_of(core * HALF + (c % 3) * 128, 128), 128)
            for n, unit, place, count, done in spots(LATE, first_tile, 24):
                sums[c // 3][16 * done : 16 * (done + count), column] = rows_of_tiles(late[n].all[unit, place : place + count])
    smalls = late[2].all[1, 48:50].astype(F32) + late[2].all[1, 50:52].astype(F32)
    bias_sum[...] = smalls[0]
    gain_sum[...] = smalls[1]

    for c in (trade, router_trade, half_trade, small_trade):
        c.wait_send()
    for _, c in swaps:
        c.wait_send()
    for n in range(len(OFFSETS)):
        for c in window_copies(n):
            c.wait_send()
    for s in early + late:
        s.end_sends()


def back(lengths, *operands):
    vm = pl.BlockSpec(memory_space=pltpu.VMEM)
    return pl.pallas_call(
        back_kernel,
        name="back",
        out_shape=(
            jax.ShapeDtypeStruct((TOK, D), BF),
            jax.ShapeDtypeStruct((TOK, D), BF),
            jax.ShapeDtypeStruct((HALF, D), BF),
            jax.ShapeDtypeStruct((HALF, D), BF),
            jax.ShapeDtypeStruct((HALF, D), BF),
            jax.ShapeDtypeStruct((HALF, D), BF),
            jax.ShapeDtypeStruct((HALF, EXPERTS), F32),
            jax.ShapeDtypeStruct((16, 128), F32),
            jax.ShapeDtypeStruct((16, 128), F32),
        ),
        in_specs=[pl.BlockSpec(memory_space=pltpu.SMEM)] + [vm] * 12 + [pl.BlockSpec(memory_space=pl.ANY)] * 3,
        out_specs=(vm,) * 9,
        scratch_shapes=[
            pltpu.VMEM((WIN, 3 * HALF), BF),
            pltpu.VMEM((CHIP, D), BF),
            pltpu.VMEM((D, 3 * HALF), BF),
            pltpu.VMEM((CHIP, WIN), F32),
            pltpu.VMEM((32, LOOP), F32),
            pltpu.VMEM((WIN, HALF), BF),
            pltpu.VMEM((SLOTS, 16, CHIP), F32),
            pltpu.VMEM((CHIP, 128), F32),
            pltpu.VMEM((CHIP, 3 * HALF), BF),
            pltpu.VMEM((NB, 128), F32),
            pltpu.VMEM((CHIP, D), BF),
            pltpu.VMEM((TOK, D), F32),
            pltpu.VMEM((TOK, D), BF),
            pltpu.VMEM((TOK, D), BF),
            pltpu.VMEM((3, 48, 16, 128), BF),
            pltpu.VMEM((48, 16, 128), BF),
            pltpu.VMEM((OWN, 16, 128), BF),
            pltpu.VMEM((4, 16, 128), BF),
            pltpu.SemaphoreType.DMA((8, 2)),
            pltpu.SemaphoreType.DMA((8, 2)),
            pltpu.SemaphoreType.DMA((8,)),
            pltpu.SemaphoreType.DMA((8,)),
            pltpu.SemaphoreType.DMA((3,)),
            pltpu.VMEM((CHIP, 2 * HALF), F32),
            *[s for units in EARLY + LATE for s in sum_scratch(units)],
        ],
        compiler_params=pltpu.CompilerParams(collective_id=2, has_side_effects=True, vmem_limit_bytes=VMEM_BYTES),
    )(lengths, *operands)


def finish_kernel(*refs):
    for src, dst in zip(refs[:8], refs[8:]):
        dst[...] = src[:, 0 : dst.shape[1]].astype(dst.dtype)


def finish(*results):
    vm = pl.BlockSpec(memory_space=pltpu.VMEM)
    kinds = ((TOK, D, BF), (TOK, D, BF)) + ((HALF, D, F32),) * 4 + ((HALF, EXPERTS, F32), (16, 12, F32))
    return pl.pallas_call(
        finish_kernel,
        name="finish",
        out_shape=tuple(jax.ShapeDtypeStruct((rows, columns), kind) for rows, columns, kind in kinds),
        in_specs=[vm] * 8,
        out_specs=(vm,) * 8,
        compiler_params=pltpu.CompilerParams(vmem_limit_bytes=VMEM_BYTES),
    )(*results)


def to_all(rows):
    return lax.all_to_all(rows, ("expert", "wshard"), split_axis=1, concat_axis=1, tiled=True)


def per_device(tokens, lengths, routes, attn_gain, query_weight, key_weight, value_weight, output_weight, bias_table, mix_gain, router_weight, expert_in, expert_out, cotangent):
    row = routes.reshape(1, TOK)
    qkv, normed, wqkv, router_full, misc_full, att, lse, hidden, mixed, router, sent = front(
        lengths, tokens, query_weight, key_weight, value_weight, output_weight, router_weight, attn_gain, mix_gain, bias_table, row, cotangent
    )

    arrived = to_all(sent).reshape(4 * EXPERTS, D)
    made_back, expert_in_grad, expert_out_grad = expert(arrived, expert_in, expert_out)
    home = to_all(made_back.reshape(4, EXPERTS, D))
    *results, gain_sum = back(lengths, home, hidden, mixed, router, row, cotangent, tokens, router_full, misc_full, output_weight, att, lse, qkv, normed, wqkv)
    layer_out, tokens_grad, query_grad, key_grad, value_grad, output_grad, router_grad, bias_grad = finish(*results)
    return (
        layer_out,
        tokens_grad,
        gain_sum[0:3].reshape(HALF),
        query_grad,
        key_grad,
        value_grad,
        output_grad,
        bias_grad,
        gain_sum[3:6].reshape(HALF),
        router_grad,
        expert_in_grad,
        expert_out_grad,
    )


def solution(mesh):
    by_token = P(("expert", "wshard"), None)
    by_row = P("wshard", None)
    by_expert = P(("expert", "wshard"), None, None)
    return jax.shard_map(
        per_device,
        mesh=mesh,
        in_specs=(
            by_token,
            P(),
            by_token,
            P("wshard"),
            by_row,
            by_row,
            by_row,
            by_row,
            by_row,
            P("wshard"),
            by_row,
            by_expert,
            by_expert,
            by_token,
        ),
        out_specs=(
            by_token,
            by_token,
            P("wshard"),
            by_row,
            by_row,
            by_row,
            by_row,
            by_row,
            P("wshard"),
            by_row,
            by_expert,
            by_expert,
        ),
        check_vma=False,
    )
```

```python
import functools

import jax
import jax.numpy as jnp
from jax import lax
from jax.experimental import pallas as pl
from jax.experimental.pallas import tpu as pltpu
from jax.sharding import PartitionSpec as P

MESH = pl.DeviceIdType.MESH
BF = jnp.bfloat16
F32 = jnp.float32
EPSILON = 1e-06
FAR_EDGES = (12, 16, 23, 32, 46, 64, 91)

D = 768
HALF = 384
HEAD = 64
TOK = 128
CHIP = 256
REACH = 4
SLOTS = 2 * REACH + 1
WIN = SLOTS * CHIP
MID = REACH * CHIP
TOTAL = 16384
EXPERTS = 128
NB = 32
FF = 3072
NEAR = 3 * TOK
LOOP = 512
VMEM_BYTES = 56 * 1024 * 1024

NT = (((1,), (1,)), ((), ()))
TN = (((0,), (0,)), ((), ()))
NN = (((1,), (0,)), ((), ()))


def mm(left, right, dims=NN):
    return lax.dot_general(left, right, dims, preferred_element_type=F32)


def bucket_of(relative):
    distance = jnp.abs(relative)
    far_bucket = 8 + sum(((distance >= edge).astype(jnp.int32) for edge in FAR_EDGES))
    near_far = jnp.where(distance < 8, distance, far_bucket)
    return near_far + 16 * (relative > 0).astype(jnp.int32)


def tile(ref, rows, start, width):
    return ref[rows, pl.ds(pl.multiple_of(start, 128), width)]


OFFSETS = (1, -1, 4, -4, 3, -3, 2, -2)
DIRECT = 6
AXES = {"y": 16, "x": 4, "z": 1}


def remote(src, dst, ssem, rsem, chip, core):
    return pltpu.make_async_remote_copy(src_ref=src, dst_ref=dst, send_sem=ssem, recv_sem=rsem, device_id=(chip, core), device_id_type=MESH)


def chip_at(e, m):
    chips = lax.axis_size("expert")
    return lax.rem(e + m + chips, chips)


def signal(barrier, chip, core):
    pl.semaphore_signal(barrier, inc=1, device_id=(chip, core), device_id_type=MESH)


def chunk(c):
    return slice(c * CHIP, (c + 1) * CHIP)


def both_gains(misc, row):
    return jnp.concatenate([misc[row : row + 1, :], misc[row + 24 : row + 25, :]], axis=1)


def placing(routes_row):
    lane = lax.broadcasted_iota(jnp.int32, (TOK, EXPERTS), 1)
    row = lax.broadcasted_iota(jnp.int32, (TOK, EXPERTS), 0)
    across = jnp.broadcast_to(routes_row[0:1, :], (TOK, TOK))
    down = across.T
    chosen = (down == lane).astype(F32)
    earlier = ((down == across) & (lane < row)).astype(F32)
    second = jnp.max(earlier, axis=1, keepdims=True)
    return chosen, (chosen * (1.0 - second)).astype(BF), (chosen * second).astype(BF)


def prepare(lengths, mask):
    e = lax.axis_index("expert")
    row_pos = (e - REACH) * CHIP + lax.broadcasted_iota(jnp.int32, (8, WIN), 1)
    col_pos = e * CHIP + lax.broadcasted_iota(jnp.int32, (CHIP, 128), 0)

    def count(n, state):
        end, rows, cols = state
        end = end + lengths[n]
        return end, rows + (row_pos >= end).astype(jnp.int32), cols + (col_pos >= end).astype(jnp.int32)

    zero = jnp.zeros((8, WIN), jnp.int32)
    _, rows, cols = lax.fori_loop(0, 32, count, (jnp.int32(0), zero, jnp.zeros((CHIP, 128), jnp.int32)))
    rows = jnp.where((row_pos >= 0) & (row_pos < TOTAL), rows, -1)
    for c in range(SLOTS):
        part = rows[0:1, c * CHIP : (c + 1) * CHIP]
        mask[:, c * CHIP : (c + 1) * CHIP] = jnp.where(cols[:, 0:1] == part, 0.0, -1e9).astype(F32)


def prepare_biases(misc, diag, ways):
    table = jnp.concatenate([misc[0:16, 0:128], misc[24:40, 0:128]], axis=0).astype(BF)
    for n, sign in enumerate(ways):
        hot = diagonal_buckets(sign)
        diag[n * 16 : (n + 1) * 16, :] = mm(table, hot.astype(BF), TN)[0:16]


def diagonal_buckets(sign):
    m = lax.broadcasted_iota(jnp.int32, (NB, LOOP), 1)
    r = jnp.where(m < NEAR, m, m - LOOP) - TOK
    b = lax.broadcasted_iota(jnp.int32, (NB, LOOP), 0)
    return (bucket_of(sign * r) == b).astype(F32)


def biased(raw, c, mask, near, ends):
    s = raw + mask[:, c * CHIP : (c + 1) * CHIP]
    left, right = ends
    if c < REACH - 1:
        return s + left
    if c > REACH + 1:
        return s + right
    t = [near[:, n * TOK : (n + 1) * TOK] for n in range(3)]
    added = {REACH - 1: (left, t[0], left, left), REACH: (t[1], t[2], t[0], t[1]), REACH + 1: (right, right, t[2], right)}[c]
    return jnp.concatenate(
        [jnp.concatenate([s[i * TOK : (i + 1) * TOK, n * TOK : (n + 1) * TOK] + added[2 * i + n] for n in range(2)], axis=1) for i in range(2)], axis=0
    )


def fill_near(diag, near, j, ways):
    def one(n, carry):
        line = diag[pl.ds(n // 6 * 16 + j * 6 + lax.rem(n, 6), 1), :]
        spread = pltpu.roll(jnp.broadcast_to(line, (8, LOOP)), 0, 1, stride=1, stride_axis=0)
        rows = 8
        while rows < TOK:
            spread = jnp.concatenate([spread, pltpu.roll(spread, rows, 1)], axis=0)
            rows *= 2
        near[n] = spread[:, 0:NEAR]
        return carry

    lax.fori_loop(0, 6 * ways, one, 0)


def far_ends(diag, row):
    line = diag[pl.ds(row, 1), :]
    return line[:, 0:1], line[:, NEAR - 1 : NEAR]


def front_kernel(lengths, tok_any, wq, wk, wv, wo_any, router_any, gain_one, gain_two, bias_rows, tok, wo, routes_row, cot, qkv_any, normed_any, wqkv_any, router_full, misc, att, lse, hidden, mixed, router, sent, qkv, normed, wqkv, misc_mine, win, wo_other, att_other, mask, diag, near, scores, tops, lse_cols, send, recv, fsend, frecv, wsend, wrecv, local, store):
    e = lax.axis_index("expert")
    j = lax.axis_index("wshard")
    jp = 1 - j
    barrier = pltpu.get_barrier_semaphore()
    for m in OFFSETS:
        signal(barrier, chip_at(e, m), j)
    signal(barrier, e, jp)

    def rows_of(slot, core):
        return win.at[pl.ds(pl.multiple_of(slot * CHIP + core * TOK, TOK), TOK), :]

    misc_mine[...] = jnp.zeros((24, HALF), F32)
    misc_mine[16:17, :] = gain_one[...].astype(F32).reshape(1, HALF)
    misc_mine[17:18, :] = gain_two[...].astype(F32).reshape(1, HALF)
    misc_mine[0:16, 0:12] = bias_rows[...].astype(F32)
    weights = []
    kept = []
    for n, w in enumerate((wq, wk, wv)):
        rows = pl.ds(pl.multiple_of(j * HALF, HALF), HALF)
        there = w.at[:, pl.ds(pl.multiple_of(jp * HALF, 128), HALF)]
        here = w.at[:, pl.ds(pl.multiple_of(j * HALF, 128), HALF)]
        dst = wqkv.at[rows, n * HALF : (n + 1) * HALF]
        weights.append(remote(there, dst, wsend.at[n], wrecv.at[n], e, jp))
        kept.append(pltpu.make_async_copy(here, dst, local.at[1 + n]))
    for n, (src, dst, size) in enumerate(((misc_mine, misc, 24), (router_any, router_full, HALF))):
        rows = pl.ds(pl.multiple_of(j * size, 8), size)
        weights.append(remote(src, dst.at[rows, :], wsend.at[3 + n], wrecv.at[3 + n], e, jp))
        kept.append(pltpu.make_async_copy(src, dst.at[rows, :], local.at[4 + n]))
    weights.append(remote(wo_any, wo_other, wsend.at[5], wrecv.at[5], e, jp))
    mine = pltpu.make_async_copy(tok_any, rows_of(REACH, j), local.at[0])
    mine.start()
    for c in kept:
        c.start()

    copies = []
    for n, m in enumerate(OFFSETS):
        src = tok_any if n < DIRECT else rows_of(REACH - m // 2, j)
        to = chip_at(e, m if n < DIRECT else m // 2)
        copies.append(remote(src, rows_of(REACH - m, j), send.at[n], recv.at[n], to, j))
    passed = [remote(rows_of(REACH - m, j), rows_of(REACH - m, j), fsend.at[n], frecv.at[n], e, jp) for n, m in enumerate(OFFSETS)]
    swap = remote(tok_any, rows_of(REACH, j), fsend.at[8], frecv.at[8], e, jp)

    pl.semaphore_wait(barrier, len(OFFSETS) + 1)
    for c in copies[:DIRECT]:
        c.start()
    weights[3].start()
    for c in weights[:3]:
        c.start()
    swap.start()
    for c in weights[4:]:
        c.start()
    prepare(lengths, mask)
    mine.wait()
    for c in kept:
        c.wait()
    for c in weights[:4]:
        c.wait_recv()
    prepare_biases(misc, diag, (1,))
    fill_near(diag, near, j, 1)
    gain = both_gains(misc, 16)

    lane = lax.broadcasted_iota(jnp.int32, (CHIP, 128), 1)

    def project(slot):
        x = win[chunk(slot), :].astype(F32)
        y = (x * lax.rsqrt(jnp.mean(x * x, axis=-1, keepdims=True) + EPSILON) * gain).astype(BF)
        if slot == REACH:
            normed[...] = y
        qkv[chunk(slot), :] = mm(y, wqkv[...]).astype(BF)

        def score(p, carry):
            q = tile(qkv, slice(MID, MID + CHIP), p * 128, 128).astype(F32) * 0.125
            k = tile(qkv, chunk(slot), HALF + p * 128, 128)
            for hh in range(2):
                h = 2 * p + hh
                qm = jnp.where((lane // HEAD) == hh, q, 0.0).astype(BF)
                s = biased(mm(qm, k, NT), slot, mask, near.at[h], far_ends(diag, j * 6 + h))
                scores[h, :, chunk(slot)] = s
                top = jnp.maximum(s[:, 0:128], s[:, 128:256])
                tops[h] = top if slot == REACH else jnp.maximum(tops[h], top)
            return carry

        lax.fori_loop(0, 3, score, 0)

    for n in range(2):
        copies[n].wait_recv()
        copies[DIRECT + n].start()
        passed[n].start()
    swap.wait_recv()
    project(REACH)
    for n in range(2, len(OFFSETS) + 2):
        if n < len(OFFSETS):
            copies[n].wait_recv()
            passed[n].start()
        passed[n - 2].wait_recv()
        project(REACH - OFFSETS[n - 2])

    stores = [pltpu.make_async_copy(src, dst, store.at[n]) for n, (src, dst) in enumerate(((qkv, qkv_any), (normed, normed_any), (wqkv, wqkv_any)))]
    for c in stores:
        c.start()
    lse_cols[...] = jnp.zeros((CHIP, 128), F32)

    def pair(p, carry):
        outs = []
        for hh in range(2):
            h = 2 * p + hh
            top = jnp.max(tops[h], axis=1, keepdims=True)
            total = jnp.zeros((CHIP, CHIP), F32)
            out = jnp.zeros((CHIP, 128), F32)
            for c in range(SLOTS):
                x = jnp.exp(scores[h, :, chunk(c)] - top)
                total = total + x
                out = out + mm(x.astype(BF), tile(qkv, chunk(c), 2 * HALF + p * 128, 128))
            total = jnp.sum(total, axis=1, keepdims=True)
            outs.append(out / total)
            lse_cols[...] = jnp.where(lane == h, top + jnp.log(total), lse_cols[...])
        att[:, pl.ds(pl.multiple_of(p * 128, 128), 128)] = jnp.where(lane < HEAD, outs[0], outs[1]).astype(BF)
        return carry

    lax.fori_loop(0, 3, pair, 0)
    lse[...] = lse_cols[...].T[0:8, :]

    here = pl.ds(pl.multiple_of(j * TOK, TOK), TOK)
    there = pl.ds(pl.multiple_of(jp * TOK, TOK), TOK)
    trade = remote(att.at[there, :], att_other, wsend.at[6], wrecv.at[6], e, jp)
    trade.start()
    chosen, first, second = placing(routes_row)
    branch = mm(att[here, :], wo[...])
    for c in weights[4:]:
        c.wait_recv()
    trade.wait_recv()
    total = tok[...].astype(F32) + (branch + mm(att_other[...], wo_other[...]))
    hidden[...] = total
    low = (total * lax.rsqrt(jnp.mean(total * total, axis=-1, keepdims=True) + EPSILON) * both_gains(misc, 17)).astype(BF)
    mixed[...] = low
    logits = mm(low, router_full[...])
    powers = jnp.exp(logits - jnp.max(logits, axis=1, keepdims=True))
    probs = powers / jnp.sum(powers, axis=1, keepdims=True)
    router[...] = probs
    gate = jnp.sum(probs * chosen, axis=1, keepdims=True)
    made_grad = (gate * cot[...].astype(F32)).astype(BF)
    for n, (place, rows) in enumerate(((first, low), (second, low), (first, made_grad), (second, made_grad))):
        sent[n] = mm(place, rows, TN).astype(BF)

    trade.wait_send()
    swap.wait_send()
    for c in weights + copies + passed:
        c.wait_send()
    for c in stores:
        c.wait()


def front(lengths, tokens, wq, wk, wv, wo, router, gain_one, gain_two, bias, row, cotangent):
    smem = pl.BlockSpec(memory_space=pltpu.SMEM)
    hbm = pl.BlockSpec(memory_space=pl.ANY)
    vm = pl.BlockSpec(memory_space=pltpu.VMEM)
    return pl.pallas_call(
        front_kernel,
        name="front",
        out_shape=(
            jax.ShapeDtypeStruct((WIN, 3 * HALF), BF),
            jax.ShapeDtypeStruct((CHIP, D), BF),
            jax.ShapeDtypeStruct((D, 3 * HALF), BF),
            jax.ShapeDtypeStruct((D, EXPERTS), BF),
            jax.ShapeDtypeStruct((48, HALF), F32),
            jax.ShapeDtypeStruct((CHIP, HALF), BF),
            jax.ShapeDtypeStruct((8, CHIP), F32),
            jax.ShapeDtypeStruct((TOK, D), F32),
            jax.ShapeDtypeStruct((TOK, D), BF),
            jax.ShapeDtypeStruct((TOK, EXPERTS), F32),
            jax.ShapeDtypeStruct((4, EXPERTS, D), BF),
        ),
        in_specs=[smem] + [hbm] * 6 + [vm] * 7,
        out_specs=(hbm,) * 3 + (vm,) * 8,
        scratch_shapes=[
            pltpu.VMEM((WIN, 3 * HALF), BF),
            pltpu.VMEM((CHIP, D), BF),
            pltpu.VMEM((D, 3 * HALF), BF),
            pltpu.VMEM((24, HALF), F32),
            pltpu.VMEM((WIN, D), BF),
            pltpu.VMEM((HALF, D), BF),
            pltpu.VMEM((TOK, HALF), BF),
            pltpu.VMEM((CHIP, WIN), F32),
            pltpu.VMEM((16, LOOP), F32),
            pltpu.VMEM((6, TOK, NEAR), F32),
            pltpu.VMEM((6, CHIP, WIN), F32),
            pltpu.VMEM((6, CHIP, 128), F32),
            pltpu.VMEM((CHIP, 128), F32),
            pltpu.SemaphoreType.DMA((8,)),
            pltpu.SemaphoreType.DMA((8,)),
            pltpu.SemaphoreType.DMA((9,)),
            pltpu.SemaphoreType.DMA((9,)),
            pltpu.SemaphoreType.DMA((7,)),
            pltpu.SemaphoreType.DMA((7,)),
            pltpu.SemaphoreType.DMA((6,)),
            pltpu.SemaphoreType.DMA((3,)),
        ],
        compiler_params=pltpu.CompilerParams(collective_id=1, has_side_effects=True, vmem_limit_bytes=VMEM_BYTES),
    )(lengths, tokens, wq, wk, wv, wo, router, gain_one, gain_two, bias, tokens, wo, row, cotangent)


FF_TILE = 512


def expert_kernel(x, g, w_in, w_out, made_back, d_in, d_out, made_sum, back_sum, across):
    step = pl.program_id(0)

    @pl.when(step == 0)
    def _():
        made_sum[...] = jnp.zeros_like(made_sum)
        back_sum[...] = jnp.zeros_like(back_sum)
        across[...] = x[...].T

    pre = mm(x[...], w_in[0])
    half_erf = 0.5 * lax.erf(pre * (0.5**0.5)) + 0.5
    act = (pre * half_erf).astype(BF)
    slope = half_erf + pre * jnp.exp(-0.5 * pre * pre) * (0.5 * 0.7978845608028654)
    act_grad = mm(g[...], w_out[0], NT)
    pre_grad = (act_grad * slope).astype(BF)
    made_sum[...] += mm(act, w_out[0])
    back_sum[...] += mm(pre_grad, w_in[0], NT)
    d_out[0] = mm(act, g[...], TN).astype(BF)
    d_in[0] = mm(across[...], pre_grad).astype(BF)

    @pl.when(step == pl.num_programs(0) - 1)
    def _():
        made_back[0 : 2 * EXPERTS, :] = made_sum[...].astype(BF)
        made_back[2 * EXPERTS :, :] = back_sum[...].astype(BF)


def expert(arrived, w_in, w_out):
    rows = 2 * EXPERTS
    forward = pl.BlockSpec((rows, D), lambda f: (0, 0))
    backward = pl.BlockSpec((rows, D), lambda f: (1, 0))
    whole = pl.BlockSpec((2 * rows, D), lambda f: (0, 0))
    by_in = pl.BlockSpec((1, D, FF_TILE), lambda f: (0, 0, f))
    by_out = pl.BlockSpec((1, FF_TILE, D), lambda f: (0, f, 0))
    return pl.pallas_call(
        expert_kernel,
        name="expert",
        grid=(FF // FF_TILE,),
        out_shape=(
            jax.ShapeDtypeStruct((2 * rows, D), BF),
            jax.ShapeDtypeStruct((1, D, FF), BF),
            jax.ShapeDtypeStruct((1, FF, D), BF),
        ),
        in_specs=[forward, backward, by_in, by_out],
        out_specs=(whole, by_in, by_out),
        scratch_shapes=[pltpu.VMEM((rows, D), F32), pltpu.VMEM((rows, D), F32), pltpu.VMEM((D, rows), BF)],
        compiler_params=pltpu.CompilerParams(vmem_limit_bytes=VMEM_BYTES, dimension_semantics=("arbitrary",)),
    )(arrived, arrived, w_in, w_out)


ORDERS = ("zxy", "xyz", "yzx")
RING = 16
PLANE = [(d, f) for d in range(4) for f in range(4) if d + f > 0]


class Sum:
    def __init__(self, e, j, order, part, ring, plane, ring_sum, plane_sum, all_, ring_sems, plane_sems):
        self.e, self.j, self.order = e, j, order
        self.part, self.ring, self.plane, self.ring_sum, self.plane_sum, self.all = part, ring, plane, ring_sum, plane_sum, all_
        self.ring_sems, self.plane_sems = ring_sems, plane_sems
        self.coord = [lax.rem(e // AXES[a], 4) for a in order]

    def peer(self, *steps):
        to = self.e
        for axis, at, d in zip(self.order, self.coord, steps):
            to = to + (lax.rem(at + d, 4) - at) * AXES[axis]
        return to

    def block(self, d, first, count):
        return pl.ds(lax.rem(self.coord[0] + d + 4, 4) * RING + first, count)

    def copy(self, src, dst, sems, n, to):
        return remote(src, dst, sems[0].at[n], sems[1].at[n], to, self.j)

    def reduce_copies(self, which):
        h = RING // 2
        up, down = self.peer(1), self.peer(3)
        pieces = [
            (lambda: self.part.at[:, self.block(2, 0, h)], up),
            (lambda: self.part.at[:, self.block(2, h, h)], down),
            (lambda: self.part.at[:, self.block(1, h, h)], up),
            (lambda: self.part.at[:, self.block(3, 0, h)], down),
            (lambda: self.ring.at[6], up),
            (lambda: self.ring.at[7], down),
        ]
        return [self.copy(pieces[n][0](), self.ring.at[n], self.ring_sems, n, pieces[n][1]) for n in which]

    def gather_copies(self, which):
        h = RING // 2
        up, down = self.peer(1), self.peer(3)
        pieces = [(0, 0, RING, up), (0, 0, RING, down), (-1, 0, h, up), (1, h, h, down)]
        found = []
        for n in which:
            d, first, count, to = pieces[n]
            ref = self.all.at[:, self.block(d, first, count)]
            found.append(self.copy(ref, ref, self.ring_sems, 6 + n, to))
        return found

    def plane_copies(self, back):
        found = []
        for n, (d, f) in enumerate(PLANE):
            to = self.peer(0, d, f)
            if back:
                ref = self.all.at[:, pl.ds(self.coord[0] * RING + self.coord[1] * 4 + self.coord[2], 1)]
                found.append(self.copy(ref, ref, self.plane_sems, 15 + n, to))
            else:
                place = lax.rem(self.coord[1] + d, 4) * 4 + lax.rem(self.coord[2] + f, 4)
                found.append(self.copy(self.ring_sum.at[:, pl.ds(place, 1)], self.plane.at[n], self.plane_sems, n, to))
        return found

    def start_ring(self):
        for c in self.reduce_copies(range(4)):
            c.start()

    def pass_ring(self):
        h = RING // 2
        for n, where in ((0, self.block(1, 0, h)), (1, self.block(3, h, h))):
            came, goes = self.reduce_copies((n, 4 + n))
            came.wait_recv()
            self.ring[6 + n] = (self.part[:, where].astype(F32) + self.ring[n].astype(F32)).astype(BF)
            goes.start()

    def ring_to_plane(self):
        h = RING // 2
        for c in self.reduce_copies(range(2, 6)):
            c.wait_recv()
        for first, others in ((0, (4, 3)), (h, (5, 2))):
            total = self.part[:, self.block(0, first, h)].astype(F32)
            for n in others:
                total = total + self.ring[n].astype(F32)
            self.ring_sum[:, first : first + h] = total.astype(BF)
        for c in self.plane_copies(False):
            c.start()

    def plane_back(self):
        own = self.coord[1] * 4 + self.coord[2]
        total = self.ring_sum[:, pl.ds(own, 1)].astype(F32)
        for n, c in enumerate(self.plane_copies(False)):
            c.wait_recv()
            total = total + self.plane[n].astype(F32)
        self.all[:, pl.ds(self.coord[0] * RING + own, 1)] = total.astype(BF)
        for c in self.plane_copies(True):
            c.start()

    def plane_to_ring(self):
        for c in self.plane_copies(True):
            c.wait_recv()
        for c in self.gather_copies((0, 1)):
            c.start()

    def pass_back(self):
        for n in range(2):
            came, goes = self.gather_copies((n, 2 + n))
            came.wait_recv()
            goes.start()

    def end(self):
        for c in self.gather_copies((2, 3)):
            c.wait_recv()

    def end_sends(self):
        for c in self.reduce_copies(range(6)) + self.plane_copies(False) + self.plane_copies(True) + self.gather_copies(range(4)):
            c.wait_send()


def sum_scratch(units):
    return [
        pltpu.VMEM((units, 64, 16, 128), BF),
        pltpu.VMEM((8, units, RING // 2, 16, 128), BF),
        pltpu.VMEM((15, units, 1, 16, 128), BF),
        pltpu.VMEM((units, RING, 16, 128), BF),
        pltpu.VMEM((units, 1, 16, 128), BF),
        pltpu.VMEM((units, 64, 16, 128), BF),
        pltpu.SemaphoreType.DMA((10,)),
        pltpu.SemaphoreType.DMA((10,)),
        pltpu.SemaphoreType.DMA((30,)),
        pltpu.SemaphoreType.DMA((30,)),
    ]


def sums_of(e, j, scratch):
    found = []
    for n, order in enumerate(ORDERS):
        s = scratch[10 * n : 10 * n + 10]
        found.append(Sum(e, j, order, *s[:6], s[6:8], s[8:10]))
    return found


LATE = (3, 2, 2)
EARLY = (1, 1, 1)
OWN = 216


def spots(units, first, count):
    table = [(n, u) for n in range(len(units)) for u in range(units[n])]
    done = 0
    while done < count:
        unit, place = divmod(first + done, 64)
        n = min(64 - place, count - done)
        yield table[unit] + (place, n, done)
        done += n


def tiles(value):
    return value.astype(BF).reshape(value.shape[0] // 16, 16, 128)


def rows_of_tiles(value):
    return value.reshape(value.shape[0] * 16, 128)


def back_kernel(lengths, home, hidden, mixed, router, routes_row, cot, tok, router_full, misc, wo, att, lse, qkv_any, normed_any, wqkv_any, layer_out, tokens_grad, q_sum, k_sum, v_sum, out_sum, router_sum, bias_sum, gain_sum, qkv, normed, wqkv, mask, diag, near, dout, stat, cols, dqkv, bias, branch, hidden_grad, half_out, half_in, grads, router_grad, stage, small, send, recv, core_send, core_recv, local, acc, *scratch):
    e = lax.axis_index("expert")
    j = lax.axis_index("wshard")
    jp = 1 - j
    here = pl.ds(pl.multiple_of(j * TOK, TOK), TOK)
    there = pl.ds(pl.multiple_of(jp * TOK, TOK), TOK)
    barrier = pltpu.get_barrier_semaphore()
    early, late = sums_of(e, j, scratch[:30]), sums_of(e, j, scratch[30:])
    for m in OFFSETS:
        signal(barrier, chip_at(e, m), j)
    for n in range(1, 64):
        steps = (n // 16, n // 4 % 4, n % 4)
        if 0 in steps:
            signal(barrier, early[0].peer(*steps), j)
    signal(barrier, e, jp)

    loads = [pltpu.make_async_copy(src, dst, local.at[n]) for n, (src, dst) in enumerate(((qkv_any, qkv), (normed_any, normed), (wqkv_any, wqkv)))]
    for c in loads:
        c.start()

    chosen, first, second = placing(routes_row)
    probs = router[...]
    gate = jnp.sum(probs * chosen, axis=1, keepdims=True)
    made = mm(first, home[0]) + mm(second, home[1])
    expert_back = mm(first, home[2]) + mm(second, home[3])
    total = hidden[...]
    layer_out[...] = (total + gate * made).astype(BF)
    dy = cot[...].astype(F32)
    gate_grad = jnp.sum(dy * made, axis=1, keepdims=True)
    logit_grad = ((gate_grad * gate) * (chosen - probs)).astype(BF)
    mixed_grad = mm(logit_grad, router_full[...], NT) + expert_back
    r = lax.rsqrt(jnp.mean(total * total, axis=-1, keepdims=True) + EPSILON)
    w = mixed_grad * both_gains(misc, 17)
    mix_gain = jnp.sum(mixed_grad * total * r, axis=0, keepdims=True)
    rest = dy + (r * w - total * (r * r * r * jnp.mean(w * total, axis=-1, keepdims=True)))
    hidden_grad[...] = rest
    branch[here, :] = rest.astype(BF)

    pl.semaphore_wait(barrier, len(OFFSETS) + 37)
    trade = remote(branch.at[here, :], branch.at[here, :], core_send.at[0], core_recv.at[0], e, jp)
    trade.start()
    router_grad[...] = tiles(mm(mixed[...], logit_grad, TN))
    router_rows = lambda core: router_grad.at[pl.ds(core * 24, 24)]
    router_trade = remote(router_rows(jp), early[2].part.at[0, 40:64], core_send.at[1], core_recv.at[1], e, jp)
    router_trade.start()
    early[2].part[0, 16:40] = router_grad[pl.ds(j * 24, 24)]
    prepare(lengths, mask)
    prepare_biases(misc, diag, (1, -1))
    fill_near(diag, near, j, 2)
    trade.wait_recv()

    lane = lax.broadcasted_iota(jnp.int32, (CHIP, 128), 1)
    low = lax.broadcasted_iota(jnp.int32, (CHIP, 128), 0) < TOK
    mid = slice(MID, MID + CHIP)
    att_grad = mm(branch[...], wo[...], NT).astype(BF)
    dout[mid, :] = att_grad
    both = att_grad.astype(F32) * att[...].astype(F32)
    dots = jnp.zeros((CHIP, 128), F32)
    for h in range(6):
        own = (lane // HEAD) == h % 2
        dot = jnp.sum(jnp.where(own, both[:, (h // 2) * 128 : (h // 2) * 128 + 128], 0.0), axis=1, keepdims=True)
        dots = jnp.where(lane == h, dot, dots)
    stat[REACH, 0:8] = lse[...]
    stat[REACH, 8:16] = dots.T[0:8, :]
    cols[...] = jnp.concatenate([stat[REACH], jnp.zeros((112, CHIP), F32)], axis=0).T

    def window_copies(n):
        m = OFFSETS[n]
        slot = REACH if n < DIRECT else REACH - m // 2
        to = chip_at(e, m if n < DIRECT else m // 2)
        return [
            remote(dout.at[chunk(slot), :], dout.at[chunk(REACH - m), :], send.at[n, 0], recv.at[n, 0], to, j),
            remote(stat.at[slot], stat.at[REACH - m], send.at[n, 1], recv.at[n, 1], to, j),
        ]

    for n in range(DIRECT):
        for c in window_copies(n):
            c.start()
    grad = mm(att[...], branch[...], TN)
    for c in range(6):
        cut = tiles(grad[:, c * 128 : (c + 1) * 128])
        for n, unit, place, count, done in spots(EARLY, 24 * c, 24):
            early[n].part[unit, place : place + count] = cut[done : done + count]
    router_trade.wait_recv()
    for s in early:
        s.start_ring()
    for c in loads:
        c.wait()

    def forward_window():
        for n in range(2):
            for c in window_copies(n):
                c.wait_recv()
            for c in window_copies(DIRECT + n):
                c.start()

    line = lax.broadcasted_iota(jnp.int32, (NB, 128), 1)
    row32 = lax.broadcasted_iota(jnp.int32, (NB, 128), 0)
    hot = diagonal_buckets(1)
    bias[...] = jnp.zeros((NB, 128), F32)

    def by_queries(p, carry):
        q = tile(qkv, mid, p * 128, 128).astype(F32) * 0.125
        do = tile(dout, mid, p * 128, 128)
        found = []
        for hh in range(2):
            h = 2 * p + hh
            own = (lane // HEAD) == hh
            spare = (1 - hh) * HEAD
            qm = jnp.where(own, q, 0.0).astype(BF)
            dom = jnp.where(own, do, jnp.zeros_like(do))
            log_sum = jnp.sum(jnp.where(lane == h, cols[...], 0.0), axis=1, keepdims=True)
            dot = jnp.sum(jnp.where(lane == h + 8, cols[...], 0.0), axis=1, keepdims=True)
            ends = far_ends(diag, j * 6 + h)
            dq = jnp.zeros((CHIP, 128), F32)
            near_grads = []
            for c in range(SLOTS):
                k = tile(qkv, chunk(c), HALF + p * 128, 128)
                v = tile(qkv, chunk(c), 2 * HALF + p * 128, 128)
                s = biased(mm(qm, k, NT), c, mask, near.at[h], ends)
                ds = jnp.exp(s - log_sum) * (mm(dom, v, NT) - dot)
                if c < REACH - 1:
                    other = lane == spare
                elif c > REACH + 1:
                    other = lane == spare + 1
                elif c == REACH - 1:
                    other = lane == jnp.where(low, spare, spare + 2)
                elif c == REACH + 1:
                    other = lane == jnp.where(low, spare + 3, spare + 1)
                else:
                    other = lane < 0
                other = jnp.where(other, 1.0, 0.0).astype(BF)
                if abs(c - REACH) < 2:
                    near_grads.append(ds)
                dq = dq + mm(ds.astype(BF), jnp.where(own, k, other))
            found.append(dq * 0.125)
            before, same, after = near_grads
            fold = jnp.concatenate(
                [
                    before[0:TOK, TOK:] + same[TOK:, 0:TOK],
                    same[0:TOK, 0:TOK] + same[TOK:, TOK:],
                    same[0:TOK, TOK:] + after[TOK:, 0:TOK],
                    jnp.zeros((TOK, TOK), F32),
                ],
                axis=1,
            )
            rows = TOK
            while rows > 8:
                rows //= 2
                fold = fold[0:rows] + pltpu.roll(fold[rows : 2 * rows], LOOP - rows, 1)
            summed = fold[0:1]
            for n in range(1, 8):
                summed = summed + pltpu.roll(fold[n : n + 1], LOOP - n, 1)
            by_bucket = jnp.sum(hot * summed, axis=1, keepdims=True)
            far_low = jnp.sum(dq[0:TOK], axis=0, keepdims=True)
            far_high = jnp.sum(dq[TOK:], axis=0, keepdims=True)
            far = far_low + far_high
            far_left = far[:, spare : spare + 1] + far_high[:, spare + 2 : spare + 3]
            far_right = far[:, spare + 1 : spare + 2] + far_low[:, spare + 3 : spare + 4]
            by_bucket = by_bucket + jnp.where(row32 == 15, far_left, 0.0) + jnp.where(row32 == 31, far_right, 0.0)
            bias[...] = jnp.where(line == j * 6 + h, by_bucket, bias[...])
            if hh == 0:
                pl.when(p == 0)(forward_window)
        dqkv[:, pl.ds(pl.multiple_of(p * 128, 128), 128)] = jnp.where(lane < HEAD, found[0], found[1]).astype(BF)
        return carry

    lax.fori_loop(0, 3, by_queries, 0)

    def by_keys(slots, p, carry):
        k_own = tile(qkv, mid, HALF + p * 128, 128)
        v_own = tile(qkv, mid, 2 * HALF + p * 128, 128)
        found = []
        for hh in range(2):
            h = 2 * p + hh
            own = (lane // HEAD) == hh
            km = jnp.where(own, k_own, jnp.zeros_like(k_own))
            vm = jnp.where(own, v_own, jnp.zeros_like(v_own))
            ends = far_ends(diag, 16 + j * 6 + h)
            dk = jnp.zeros((CHIP, 128), F32)
            dv = jnp.zeros((CHIP, 128), F32)
            for c in slots:
                qc = (tile(qkv, chunk(c), p * 128, 128).astype(F32) * 0.125).astype(BF)
                dc = tile(dout, chunk(c), p * 128, 128)
                s = biased(mm(km, qc, NT), c, mask, near.at[6 + h], ends)
                prob = jnp.exp(s - stat[c, pl.ds(h, 1), :])
                ds = prob * (mm(vm, dc, NT) - stat[c, pl.ds(h + 8, 1), :])
                dv = dv + mm(prob.astype(BF), dc)
                dk = dk + mm(ds.astype(BF), qc)
            found.append((dk, dv))
        for n in range(2):
            where = pl.ds(pl.multiple_of(n * HALF + p * 128, 128), 128)
            both = jnp.where(lane < HEAD, found[0][n], found[1][n])
            acc[:, where] = both if REACH in slots else acc[:, where] + both
        return carry

    for n, slots in ((1, (REACH, 3, 5)), (2, (0, 8)), (4, (1, 7)), (6, (2, 6))):
        if n > 1:
            for c in window_copies(n) + window_copies(n + 1):
                c.wait_recv()
        lax.fori_loop(0, 3, functools.partial(by_keys, slots), 0)
        if n == 2:
            for s in early:
                s.pass_ring()
        elif n == 6:
            for s in early:
                s.ring_to_plane()
    dqkv[:, HALF:] = acc[...].astype(BF)

    half_out[...] = mm(dqkv[there, :], wqkv[...], NT).astype(BF)
    half_trade = remote(half_out, half_in, core_send.at[2], core_recv.at[2], e, jp)
    half_trade.start()
    whole = tuple(s.part for s in late)
    swaps = []
    for n, unit, place, count, done in spots(LATE, OWN, OWN):
        swaps.append((done + count, remote(stage.at[done : done + count], whole[n].at[unit, place : place + count], core_send.at[4 + len(swaps)], core_recv.at[4 + len(swaps)], e, jp)))
    sent = 0
    for third in range(3):
        grad = mm(normed[...], dqkv[:, third * HALF : (third + 1) * HALF], TN)
        for c in range(3 * third, 3 * third + 3):
            grads[c % 3] = tiles(grad[:, (c % 3) * 128 : (c % 3 + 1) * 128])
            stage[24 * c : 24 * c + 24] = grads[c % 3, pl.ds(24 * jp, 24)]
            for n, unit, place, count, done in spots(LATE, 24 * c, 24):
                whole[n][unit, place : place + count] = grads[c % 3, pl.ds(24 * j + done, count)]
        while sent < len(swaps) and swaps[sent][0] <= 72 * (third + 1):
            swaps[sent][1].start()
            sent += 1
    late[0].start_ring()
    for s in early:
        s.plane_back()

    half = mm(dqkv[here, :], wqkv[...], NT)
    half_trade.wait_recv()
    grad = half + half_in[...].astype(F32)
    x = tok[...].astype(F32)
    r = lax.rsqrt(jnp.mean(x * x, axis=-1, keepdims=True) + EPSILON)
    w = grad * both_gains(misc, 16)
    tokens_grad[...] = (hidden_grad[...] + (r * w - x * (r * r * r * jnp.mean(w * x, axis=-1, keepdims=True)))).astype(BF)
    attn_gain = jnp.sum(grad * x * r, axis=0, keepdims=True)
    for h in range(2):
        lines = [v[:, h * HALF + 128 * n : h * HALF + 128 * n + 128] for v in (attn_gain, mix_gain) for n in range(3)]
        small[2 * h] = bias[16 * h : 16 * h + 16, :].astype(BF)
        small[2 * h + 1] = jnp.concatenate(lines + [jnp.zeros((10, 128), F32)], axis=0).astype(BF)
    last = whole[2]
    last[1, 52:64] = jnp.zeros((12, 16, 128), BF)
    last[1, 48:50] = small[pl.ds(2 * j, 2)]
    small_trade = remote(small.at[pl.ds(2 * jp, 2)], last.at[1, 50:52], core_send.at[3], core_recv.at[3], e, jp)
    small_trade.start()
    late[0].pass_ring()
    for _, c in swaps:
        c.wait_recv()
    late[1].start_ring()
    small_trade.wait_recv()
    late[2].start_ring()
    for s in early:
        s.plane_to_ring()
    for s in late[1:]:
        s.pass_ring()
    for s in late:
        s.ring_to_plane()
    for s in early:
        s.pass_back()
    for s in late:
        s.plane_back()
    for s in late:
        s.plane_to_ring()

    for s in early:
        s.end()
    for c in range(6):
        for n, unit, place, count, done in spots(EARLY, 24 * c, 24):
            out_sum[16 * done : 16 * (done + count), c * 128 : (c + 1) * 128] = rows_of_tiles(early[n].all[unit, place : place + count])
    router_sum[...] = rows_of_tiles(early[2].all[0, 16:40].astype(F32) + early[2].all[0, 40:64].astype(F32))

    for step in ("pass_back", "end"):
        for s in late:
            getattr(s, step)()
    sums = (q_sum, k_sum, v_sum)
    for c in range(9):
        for first_tile, core in ((24 * c, j), (OWN + 24 * c, jp)):
            column = pl.ds(pl.multiple_of(core * HALF + (c % 3) * 128, 128), 128)
            for n, unit, place, count, done in spots(LATE, first_tile, 24):
                sums[c // 3][16 * done : 16 * (done + count), column] = rows_of_tiles(late[n].all[unit, place : place + count])
    smalls = late[2].all[1, 48:50].astype(F32) + late[2].all[1, 50:52].astype(F32)
    bias_sum[...] = smalls[0]
    gain_sum[...] = smalls[1]

    for c in (trade, router_trade, half_trade, small_trade):
        c.wait_send()
    for _, c in swaps:
        c.wait_send()
    for n in range(len(OFFSETS)):
        for c in window_copies(n):
            c.wait_send()
    for s in early + late:
        s.end_sends()


def back(lengths, *operands):
    vm = pl.BlockSpec(memory_space=pltpu.VMEM)
    return pl.pallas_call(
        back_kernel,
        name="back",
        out_shape=(
            jax.ShapeDtypeStruct((TOK, D), BF),
            jax.ShapeDtypeStruct((TOK, D), BF),
            jax.ShapeDtypeStruct((HALF, D), BF),
            jax.ShapeDtypeStruct((HALF, D), BF),
            jax.ShapeDtypeStruct((HALF, D), BF),
            jax.ShapeDtypeStruct((HALF, D), BF),
            jax.ShapeDtypeStruct((HALF, EXPERTS), F32),
            jax.ShapeDtypeStruct((16, 128), F32),
            jax.ShapeDtypeStruct((16, 128), F32),
        ),
        in_specs=[pl.BlockSpec(memory_space=pltpu.SMEM)] + [vm] * 12 + [pl.BlockSpec(memory_space=pl.ANY)] * 3,
        out_specs=(vm,) * 9,
        scratch_shapes=[
            pltpu.VMEM((WIN, 3 * HALF), BF),
            pltpu.VMEM((CHIP, D), BF),
            pltpu.VMEM((D, 3 * HALF), BF),
            pltpu.VMEM((CHIP, WIN), F32),
            pltpu.VMEM((32, LOOP), F32),
            pltpu.VMEM((12, TOK, NEAR), F32),
            pltpu.VMEM((WIN, HALF), BF),
            pltpu.VMEM((SLOTS, 16, CHIP), F32),
            pltpu.VMEM((CHIP, 128), F32),
            pltpu.VMEM((CHIP, 3 * HALF), BF),
            pltpu.VMEM((NB, 128), F32),
            pltpu.VMEM((CHIP, D), BF),
            pltpu.VMEM((TOK, D), F32),
            pltpu.VMEM((TOK, D), BF),
            pltpu.VMEM((TOK, D), BF),
            pltpu.VMEM((3, 48, 16, 128), BF),
            pltpu.VMEM((48, 16, 128), BF),
            pltpu.VMEM((OWN, 16, 128), BF),
            pltpu.VMEM((4, 16, 128), BF),
            pltpu.SemaphoreType.DMA((8, 2)),
            pltpu.SemaphoreType.DMA((8, 2)),
            pltpu.SemaphoreType.DMA((8,)),
            pltpu.SemaphoreType.DMA((8,)),
            pltpu.SemaphoreType.DMA((3,)),
            pltpu.VMEM((CHIP, 2 * HALF), F32),
            *[s for units in EARLY + LATE for s in sum_scratch(units)],
        ],
        compiler_params=pltpu.CompilerParams(collective_id=2, has_side_effects=True, vmem_limit_bytes=VMEM_BYTES),
    )(lengths, *operands)


def finish_kernel(*refs):
    for src, dst in zip(refs[:8], refs[8:]):
        dst[...] = src[:, 0 : dst.shape[1]].astype(dst.dtype)


def finish(*results):
    vm = pl.BlockSpec(memory_space=pltpu.VMEM)
    kinds = ((TOK, D, BF), (TOK, D, BF)) + ((HALF, D, F32),) * 4 + ((HALF, EXPERTS, F32), (16, 12, F32))
    return pl.pallas_call(
        finish_kernel,
        name="finish",
        out_shape=tuple(jax.ShapeDtypeStruct((rows, columns), kind) for rows, columns, kind in kinds),
        in_specs=[vm] * 8,
        out_specs=(vm,) * 8,
        compiler_params=pltpu.CompilerParams(vmem_limit_bytes=VMEM_BYTES),
    )(*results)


def to_all(rows):
    return lax.all_to_all(rows, ("expert", "wshard"), split_axis=1, concat_axis=1, tiled=True)


def per_device(tokens, lengths, routes, attn_gain, query_weight, key_weight, value_weight, output_weight, bias_table, mix_gain, router_weight, expert_in, expert_out, cotangent):
    row = routes.reshape(1, TOK)
    qkv, normed, wqkv, router_full, misc_full, att, lse, hidden, mixed, router, sent = front(
        lengths, tokens, query_weight, key_weight, value_weight, output_weight, router_weight, attn_gain, mix_gain, bias_table, row, cotangent
    )

    arrived = to_all(sent).reshape(4 * EXPERTS, D)
    made_back, expert_in_grad, expert_out_grad = expert(arrived, expert_in, expert_out)
    home = to_all(made_back.reshape(4, EXPERTS, D))
    *results, gain_sum = back(lengths, home, hidden, mixed, router, row, cotangent, tokens, router_full, misc_full, output_weight, att, lse, qkv, normed, wqkv)
    layer_out, tokens_grad, query_grad, key_grad, value_grad, output_grad, router_grad, bias_grad = finish(*results)
    return (
        layer_out,
        tokens_grad,
        gain_sum[0:3].reshape(HALF),
        query_grad,
        key_grad,
        value_grad,
        output_grad,
        bias_grad,
        gain_sum[3:6].reshape(HALF),
        router_grad,
        expert_in_grad,
        expert_out_grad,
    )


def solution(mesh):
    by_token = P(("expert", "wshard"), None)
    by_row = P("wshard", None)
    by_expert = P(("expert", "wshard"), None, None)
    return jax.shard_map(
        per_device,
        mesh=mesh,
        in_specs=(
            by_token,
            P(),
            by_token,
            P("wshard"),
            by_row,
            by_row,
            by_row,
            by_row,
            by_row,
            P("wshard"),
            by_row,
            by_expert,
            by_expert,
            by_token,
        ),
        out_specs=(
            by_token,
            by_token,
            P("wshard"),
            by_row,
            by_row,
            by_row,
            by_row,
            by_row,
            P("wshard"),
            by_row,
            by_expert,
            by_expert,
        ),
        check_vma=False,
    )
```

```python
import functools

import jax
import jax.numpy as jnp
from jax import lax
from jax.experimental import pallas as pl
from jax.experimental.pallas import tpu as pltpu
from jax.sharding import PartitionSpec as P

MESH = pl.DeviceIdType.MESH
BF = jnp.bfloat16
F32 = jnp.float32
EPSILON = 1e-06
FAR_EDGES = (12, 16, 23, 32, 46, 64, 91)

D = 768
HALF = 384
HEAD = 64
TOK = 128
CHIP = 256
REACH = 4
SLOTS = 2 * REACH + 1
WIN = SLOTS * CHIP
MID = REACH * CHIP
TOTAL = 16384
EXPERTS = 128
NB = 32
FF = 3072
NEAR = 3 * TOK
LOOP = 512
VMEM_BYTES = 56 * 1024 * 1024

NT = (((1,), (1,)), ((), ()))
TN = (((0,), (0,)), ((), ()))
NN = (((1,), (0,)), ((), ()))


def mm(left, right, dims=NN):
    return lax.dot_general(left, right, dims, preferred_element_type=F32)


def bucket_of(relative):
    distance = jnp.abs(relative)
    far_bucket = 8 + sum(((distance >= edge).astype(jnp.int32) for edge in FAR_EDGES))
    near_far = jnp.where(distance < 8, distance, far_bucket)
    return near_far + 16 * (relative > 0).astype(jnp.int32)


def tile(ref, rows, start, width):
    if isinstance(start, int):
        return ref[rows, start : start + width]
    return ref[rows, pl.ds(pl.multiple_of(start, 128), width)]


def each_pair(body):
    for p in range(3):
        body(p)


OFFSETS = (1, -1, 4, -4, 3, -3, 2, -2)
DIRECT = 6
AXES = {"y": 16, "x": 4, "z": 1}


def remote(src, dst, ssem, rsem, chip, core):
    return pltpu.make_async_remote_copy(src_ref=src, dst_ref=dst, send_sem=ssem, recv_sem=rsem, device_id=(chip, core), device_id_type=MESH)


def chip_at(e, m):
    chips = lax.axis_size("expert")
    return lax.rem(e + m + chips, chips)


def signal(barrier, chip, core):
    pl.semaphore_signal(barrier, inc=1, device_id=(chip, core), device_id_type=MESH)


def chunk(c):
    return slice(c * CHIP, (c + 1) * CHIP)


def both_gains(misc, row):
    return jnp.concatenate([misc[row : row + 1, :], misc[row + 24 : row + 25, :]], axis=1)


def placing(routes_row):
    lane = lax.broadcasted_iota(jnp.int32, (TOK, EXPERTS), 1)
    row = lax.broadcasted_iota(jnp.int32, (TOK, EXPERTS), 0)
    across = jnp.broadcast_to(routes_row[0:1, :], (TOK, TOK))
    down = across.T
    chosen = (down == lane).astype(F32)
    earlier = ((down == across) & (lane < row)).astype(F32)
    second = jnp.max(earlier, axis=1, keepdims=True)
    return chosen, (chosen * (1.0 - second)).astype(BF), (chosen * second).astype(BF)


def prepare(lengths, mask):
    e = lax.axis_index("expert")
    row_pos = (e - REACH) * CHIP + lax.broadcasted_iota(jnp.int32, (8, WIN), 1)
    col_pos = e * CHIP + lax.broadcasted_iota(jnp.int32, (CHIP, 128), 0)

    def count(n, state):
        end, rows, cols = state
        end = end + lengths[n]
        return end, rows + (row_pos >= end).astype(jnp.int32), cols + (col_pos >= end).astype(jnp.int32)

    zero = jnp.zeros((8, WIN), jnp.int32)
    _, rows, cols = lax.fori_loop(0, 32, count, (jnp.int32(0), zero, jnp.zeros((CHIP, 128), jnp.int32)))
    rows = jnp.where((row_pos >= 0) & (row_pos < TOTAL), rows, -1)
    for c in range(SLOTS):
        part = rows[0:1, c * CHIP : (c + 1) * CHIP]
        mask[:, c * CHIP : (c + 1) * CHIP] = jnp.where(cols[:, 0:1] == part, 0.0, -1e9).astype(F32)


def prepare_biases(misc, diag, ways):
    table = jnp.concatenate([misc[0:16, 0:128], misc[24:40, 0:128]], axis=0).astype(BF)
    for n, sign in enumerate(ways):
        hot = diagonal_buckets(sign)
        diag[n * 16 : (n + 1) * 16, :] = mm(table, hot.astype(BF), TN)[0:16]


def diagonal_buckets(sign):
    m = lax.broadcasted_iota(jnp.int32, (NB, LOOP), 1)
    r = jnp.where(m < NEAR, m, m - LOOP) - TOK
    b = lax.broadcasted_iota(jnp.int32, (NB, LOOP), 0)
    return (bucket_of(sign * r) == b).astype(F32)


def biased(raw, c, mask, near, ends):
    s = raw + mask[:, c * CHIP : (c + 1) * CHIP]
    left, right = ends
    if c < REACH - 1:
        return s + left
    if c > REACH + 1:
        return s + right
    t = [near[:, n * TOK : (n + 1) * TOK] for n in range(3)]
    added = {REACH - 1: (left, t[0], left, left), REACH: (t[1], t[2], t[0], t[1]), REACH + 1: (right, right, t[2], right)}[c]
    return jnp.concatenate(
        [jnp.concatenate([s[i * TOK : (i + 1) * TOK, n * TOK : (n + 1) * TOK] + added[2 * i + n] for n in range(2)], axis=1) for i in range(2)], axis=0
    )


def fill_near(diag, near, j, ways):
    def one(n, carry):
        line = diag[pl.ds(n // 6 * 16 + j * 6 + lax.rem(n, 6), 1), :]
        spread = pltpu.roll(jnp.broadcast_to(line, (TOK, LOOP)), 0, 1, stride=1, stride_axis=0)
        near[n] = spread[:, 0:NEAR]
        return carry

    lax.fori_loop(0, 6 * ways, one, 0)


def far_ends(diag, row):
    line = diag[pl.ds(row, 1), :]
    return line[:, 0:1], line[:, NEAR - 1 : NEAR]


def front_kernel(lengths, tok_any, wq, wk, wv, wo_any, router_any, gain_one, gain_two, bias_rows, tok, wo, routes_row, cot, qkv_any, normed_any, wqkv_any, router_full, misc, att, lse, hidden, mixed, router, sent, qkv, normed, wqkv, misc_mine, win, wo_other, att_other, mask, diag, near, scores, tops, lse_cols, send, recv, fsend, frecv, wsend, wrecv, local, store):
    e = lax.axis_index("expert")
    j = lax.axis_index("wshard")
    jp = 1 - j
    barrier = pltpu.get_barrier_semaphore()
    for m in OFFSETS:
        signal(barrier, chip_at(e, m), j)
    signal(barrier, e, jp)

    def rows_of(slot, core):
        return win.at[pl.ds(pl.multiple_of(slot * CHIP + core * TOK, TOK), TOK), :]

    misc_mine[...] = jnp.zeros((24, HALF), F32)
    misc_mine[16:17, :] = gain_one[...].astype(F32).reshape(1, HALF)
    misc_mine[17:18, :] = gain_two[...].astype(F32).reshape(1, HALF)
    misc_mine[0:16, 0:12] = bias_rows[...].astype(F32)
    weights = []
    kept = []
    for n, w in enumerate((wq, wk, wv)):
        rows = pl.ds(pl.multiple_of(j * HALF, HALF), HALF)
        there = w.at[:, pl.ds(pl.multiple_of(jp * HALF, 128), HALF)]
        here = w.at[:, pl.ds(pl.multiple_of(j * HALF, 128), HALF)]
        dst = wqkv.at[rows, n * HALF : (n + 1) * HALF]
        weights.append(remote(there, dst, wsend.at[n], wrecv.at[n], e, jp))
        kept.append(pltpu.make_async_copy(here, dst, local.at[1 + n]))
    for n, (src, dst, size) in enumerate(((misc_mine, misc, 24), (router_any, router_full, HALF))):
        rows = pl.ds(pl.multiple_of(j * size, 8), size)
        weights.append(remote(src, dst.at[rows, :], wsend.at[3 + n], wrecv.at[3 + n], e, jp))
        kept.append(pltpu.make_async_copy(src, dst.at[rows, :], local.at[4 + n]))
    weights.append(remote(wo_any, wo_other, wsend.at[5], wrecv.at[5], e, jp))
    mine = pltpu.make_async_copy(tok_any, rows_of(REACH, j), local.at[0])
    mine.start()
    for c in kept:
        c.start()

    copies = []
    for n, m in enumerate(OFFSETS):
        src = tok_any if n < DIRECT else rows_of(REACH - m // 2, j)
        to = chip_at(e, m if n < DIRECT else m // 2)
        copies.append(remote(src, rows_of(REACH - m, j), send.at[n], recv.at[n], to, j))
    passed = [remote(rows_of(REACH - m, j), rows_of(REACH - m, j), fsend.at[n], frecv.at[n], e, jp) for n, m in enumerate(OFFSETS)]
    swap = remote(tok_any, rows_of(REACH, j), fsend.at[8], frecv.at[8], e, jp)

    pl.semaphore_wait(barrier, len(OFFSETS) + 1)
    for c in copies[:DIRECT]:
        c.start()
    weights[3].start()
    for c in weights[:3]:
        c.start()
    swap.start()
    for c in weights[4:]:
        c.start()
    prepare(lengths, mask)
    mine.wait()
    for c in kept:
        c.wait()
    for c in weights[:4]:
        c.wait_recv()
    prepare_biases(misc, diag, (1,))
    fill_near(diag, near, j, 1)
    gain = both_gains(misc, 16)

    lane = lax.broadcasted_iota(jnp.int32, (CHIP, 128), 1)

    def project(slot):
        x = win[chunk(slot), :].astype(F32)
        y = (x * lax.rsqrt(jnp.mean(x * x, axis=-1, keepdims=True) + EPSILON) * gain).astype(BF)
        if slot == REACH:
            normed[...] = y
        qkv[chunk(slot), :] = mm(y, wqkv[...]).astype(BF)

        def score(p, carry):
            q = tile(qkv, slice(MID, MID + CHIP), p * 128, 128).astype(F32) * 0.125
            k = tile(qkv, chunk(slot), HALF + p * 128, 128)
            for hh in range(2):
                h = 2 * p + hh
                qm = jnp.where((lane // HEAD) == hh, q, 0.0).astype(BF)
                s = biased(mm(qm, k, NT), slot, mask, near.at[h], far_ends(diag, j * 6 + h))
                scores[h, :, chunk(slot)] = s
                top = jnp.maximum(s[:, 0:128], s[:, 128:256])
                tops[h] = top if slot == REACH else jnp.maximum(tops[h], top)
            return carry

        lax.fori_loop(0, 3, score, 0)

    for n in range(2):
        copies[n].wait_recv()
        copies[DIRECT + n].start()
        passed[n].start()
    swap.wait_recv()
    project(REACH)
    for n in range(2, len(OFFSETS) + 2):
        if n < len(OFFSETS):
            copies[n].wait_recv()
            passed[n].start()
        passed[n - 2].wait_recv()
        project(REACH - OFFSETS[n - 2])

    stores = [pltpu.make_async_copy(src, dst, store.at[n]) for n, (src, dst) in enumerate(((qkv, qkv_any), (normed, normed_any), (wqkv, wqkv_any)))]
    for c in stores:
        c.start()
    lse_cols[...] = jnp.zeros((CHIP, 128), F32)

    def pair(p):
        outs = []
        for hh in range(2):
            h = 2 * p + hh
            top = jnp.max(tops[h], axis=1, keepdims=True)
            total = jnp.zeros((CHIP, CHIP), F32)
            out = jnp.zeros((CHIP, 128), F32)
            for c in range(SLOTS):
                x = jnp.exp(scores[h, :, chunk(c)] - top)
                total = total + x
                out = out + mm(x.astype(BF), tile(qkv, chunk(c), 2 * HALF + p * 128, 128))
            total = jnp.sum(total, axis=1, keepdims=True)
            outs.append(out / total)
            lse_cols[...] = jnp.where(lane == h, top + jnp.log(total), lse_cols[...])
        att[:, p * 128 : p * 128 + 128] = jnp.where(lane < HEAD, outs[0], outs[1]).astype(BF)

    each_pair(pair)
    lse[...] = lse_cols[...].T[0:8, :]

    here = pl.ds(pl.multiple_of(j * TOK, TOK), TOK)
    there = pl.ds(pl.multiple_of(jp * TOK, TOK), TOK)
    trade = remote(att.at[there, :], att_other, wsend.at[6], wrecv.at[6], e, jp)
    trade.start()
    chosen, first, second = placing(routes_row)
    branch = mm(att[here, :], wo[...])
    for c in weights[4:]:
        c.wait_recv()
    trade.wait_recv()
    total = tok[...].astype(F32) + (branch + mm(att_other[...], wo_other[...]))
    hidden[...] = total
    low = (total * lax.rsqrt(jnp.mean(total * total, axis=-1, keepdims=True) + EPSILON) * both_gains(misc, 17)).astype(BF)
    mixed[...] = low
    logits = mm(low, router_full[...])
    powers = jnp.exp(logits - jnp.max(logits, axis=1, keepdims=True))
    probs = powers / jnp.sum(powers, axis=1, keepdims=True)
    router[...] = probs
    gate = jnp.sum(probs * chosen, axis=1, keepdims=True)
    made_grad = (gate * cot[...].astype(F32)).astype(BF)
    for n, (place, rows) in enumerate(((first, low), (second, low), (first, made_grad), (second, made_grad))):
        sent[n] = mm(place, rows, TN).astype(BF)

    trade.wait_send()
    swap.wait_send()
    for c in weights + copies + passed:
        c.wait_send()
    for c in stores:
        c.wait()


def front(lengths, tokens, wq, wk, wv, wo, router, gain_one, gain_two, bias, row, cotangent):
    smem = pl.BlockSpec(memory_space=pltpu.SMEM)
    hbm = pl.BlockSpec(memory_space=pl.ANY)
    vm = pl.BlockSpec(memory_space=pltpu.VMEM)
    return pl.pallas_call(
        front_kernel,
        name="front",
        out_shape=(
            jax.ShapeDtypeStruct((WIN, 3 * HALF), BF),
            jax.ShapeDtypeStruct((CHIP, D), BF),
            jax.ShapeDtypeStruct((D, 3 * HALF), BF),
            jax.ShapeDtypeStruct((D, EXPERTS), BF),
            jax.ShapeDtypeStruct((48, HALF), F32),
            jax.ShapeDtypeStruct((CHIP, HALF), BF),
            jax.ShapeDtypeStruct((8, CHIP), F32),
            jax.ShapeDtypeStruct((TOK, D), F32),
            jax.ShapeDtypeStruct((TOK, D), BF),
            jax.ShapeDtypeStruct((TOK, EXPERTS), F32),
            jax.ShapeDtypeStruct((4, EXPERTS, D), BF),
        ),
        in_specs=[smem] + [hbm] * 6 + [vm] * 7,
        out_specs=(hbm,) * 3 + (vm,) * 8,
        scratch_shapes=[
            pltpu.VMEM((WIN, 3 * HALF), BF),
            pltpu.VMEM((CHIP, D), BF),
            pltpu.VMEM((D, 3 * HALF), BF),
            pltpu.VMEM((24, HALF), F32),
            pltpu.VMEM((WIN, D), BF),
            pltpu.VMEM((HALF, D), BF),
            pltpu.VMEM((TOK, HALF), BF),
            pltpu.VMEM((CHIP, WIN), F32),
            pltpu.VMEM((16, LOOP), F32),
            pltpu.VMEM((6, TOK, NEAR), F32),
            pltpu.VMEM((6, CHIP, WIN), F32),
            pltpu.VMEM((6, CHIP, 128), F32),
            pltpu.VMEM((CHIP, 128), F32),
            pltpu.SemaphoreType.DMA((8,)),
            pltpu.SemaphoreType.DMA((8,)),
            pltpu.SemaphoreType.DMA((9,)),
            pltpu.SemaphoreType.DMA((9,)),
            pltpu.SemaphoreType.DMA((7,)),
            pltpu.SemaphoreType.DMA((7,)),
            pltpu.SemaphoreType.DMA((6,)),
            pltpu.SemaphoreType.DMA((3,)),
        ],
        compiler_params=pltpu.CompilerParams(collective_id=1, has_side_effects=True, vmem_limit_bytes=VMEM_BYTES),
    )(lengths, tokens, wq, wk, wv, wo, router, gain_one, gain_two, bias, tokens, wo, row, cotangent)


FF_TILE = 512


def expert_kernel(x, g, w_in, w_out, made_back, d_in, d_out, made_sum, back_sum, across):
    step = pl.program_id(0)

    @pl.when(step == 0)
    def _():
        made_sum[...] = jnp.zeros_like(made_sum)
        back_sum[...] = jnp.zeros_like(back_sum)
        across[...] = x[...].T

    pre = mm(x[...], w_in[0])
    half_erf = 0.5 * lax.erf(pre * (0.5**0.5)) + 0.5
    act = (pre * half_erf).astype(BF)
    slope = half_erf + pre * jnp.exp(-0.5 * pre * pre) * (0.5 * 0.7978845608028654)
    act_grad = mm(g[...], w_out[0], NT)
    pre_grad = (act_grad * slope).astype(BF)
    made_sum[...] += mm(act, w_out[0])
    back_sum[...] += mm(pre_grad, w_in[0], NT)
    d_out[0] = mm(act, g[...], TN).astype(BF)
    d_in[0] = mm(across[...], pre_grad).astype(BF)

    @pl.when(step == pl.num_programs(0) - 1)
    def _():
        made_back[0 : 2 * EXPERTS, :] = made_sum[...].astype(BF)
        made_back[2 * EXPERTS :, :] = back_sum[...].astype(BF)


def expert(arrived, w_in, w_out):
    rows = 2 * EXPERTS
    forward = pl.BlockSpec((rows, D), lambda f: (0, 0))
    backward = pl.BlockSpec((rows, D), lambda f: (1, 0))
    whole = pl.BlockSpec((2 * rows, D), lambda f: (0, 0))
    by_in = pl.BlockSpec((1, D, FF_TILE), lambda f: (0, 0, f))
    by_out = pl.BlockSpec((1, FF_TILE, D), lambda f: (0, f, 0))
    return pl.pallas_call(
        expert_kernel,
        name="expert",
        grid=(FF // FF_TILE,),
        out_shape=(
            jax.ShapeDtypeStruct((2 * rows, D), BF),
            jax.ShapeDtypeStruct((1, D, FF), BF),
            jax.ShapeDtypeStruct((1, FF, D), BF),
        ),
        in_specs=[forward, backward, by_in, by_out],
        out_specs=(whole, by_in, by_out),
        scratch_shapes=[pltpu.VMEM((rows, D), F32), pltpu.VMEM((rows, D), F32), pltpu.VMEM((D, rows), BF)],
        compiler_params=pltpu.CompilerParams(vmem_limit_bytes=VMEM_BYTES, dimension_semantics=("arbitrary",)),
    )(arrived, arrived, w_in, w_out)


ORDERS = ("zxy", "xyz", "yzx")
RING = 16
PLANE = [(d, f) for d in range(4) for f in range(4) if d + f > 0]


class Sum:
    def __init__(self, e, j, order, part, ring, plane, ring_sum, plane_sum, all_, ring_sems, plane_sems):
        self.e, self.j, self.order = e, j, order
        self.part, self.ring, self.plane, self.ring_sum, self.plane_sum, self.all = part, ring, plane, ring_sum, plane_sum, all_
        self.ring_sems, self.plane_sems = ring_sems, plane_sems
        self.coord = [lax.rem(e // AXES[a], 4) for a in order]

    def peer(self, *steps):
        to = self.e
        for axis, at, d in zip(self.order, self.coord, steps):
            to = to + (lax.rem(at + d, 4) - at) * AXES[axis]
        return to

    def block(self, d, first, count):
        return pl.ds(lax.rem(self.coord[0] + d + 4, 4) * RING + first, count)

    def copy(self, src, dst, sems, n, to):
        return remote(src, dst, sems[0].at[n], sems[1].at[n], to, self.j)

    def reduce_copies(self, which):
        h = RING // 2
        up, down = self.peer(1), self.peer(3)
        pieces = [
            (lambda: self.part.at[:, self.block(2, 0, h)], up),
            (lambda: self.part.at[:, self.block(2, h, h)], down),
            (lambda: self.part.at[:, self.block(1, h, h)], up),
            (lambda: self.part.at[:, self.block(3, 0, h)], down),
            (lambda: self.ring.at[6], up),
            (lambda: self.ring.at[7], down),
        ]
        return [self.copy(pieces[n][0](), self.ring.at[n], self.ring_sems, n, pieces[n][1]) for n in which]

    def gather_copies(self, which):
        h = RING // 2
        up, down = self.peer(1), self.peer(3)
        pieces = [(0, 0, RING, up), (0, 0, RING, down), (-1, 0, h, up), (1, h, h, down)]
        found = []
        for n in which:
            d, first, count, to = pieces[n]
            ref = self.all.at[:, self.block(d, first, count)]
            found.append(self.copy(ref, ref, self.ring_sems, 6 + n, to))
        return found

    def plane_copies(self, back):
        found = []
        for n, (d, f) in enumerate(PLANE):
            to = self.peer(0, d, f)
            if back:
                ref = self.all.at[:, pl.ds(self.coord[0] * RING + self.coord[1] * 4 + self.coord[2], 1)]
                found.append(self.copy(ref, ref, self.plane_sems, 15 + n, to))
            else:
                place = lax.rem(self.coord[1] + d, 4) * 4 + lax.rem(self.coord[2] + f, 4)
                found.append(self.copy(self.ring_sum.at[:, pl.ds(place, 1)], self.plane.at[n], self.plane_sems, n, to))
        return found

    def start_ring(self):
        for c in self.reduce_copies(range(4)):
            c.start()

    def pass_ring(self):
        h = RING // 2
        for n, where in ((0, self.block(1, 0, h)), (1, self.block(3, h, h))):
            came, goes = self.reduce_copies((n, 4 + n))
            came.wait_recv()
            self.ring[6 + n] = (self.part[:, where].astype(F32) + self.ring[n].astype(F32)).astype(BF)
            goes.start()

    def ring_to_plane(self):
        h = RING // 2
        for c in self.reduce_copies(range(2, 6)):
            c.wait_recv()
        for first, others in ((0, (4, 3)), (h, (5, 2))):
            total = self.part[:, self.block(0, first, h)].astype(F32)
            for n in others:
                total = total + self.ring[n].astype(F32)
            self.ring_sum[:, first : first + h] = total.astype(BF)
        for c in self.plane_copies(False):
            c.start()

    def plane_back(self):
        own = self.coord[1] * 4 + self.coord[2]
        total = self.ring_sum[:, pl.ds(own, 1)].astype(F32)
        for n, c in enumerate(self.plane_copies(False)):
            c.wait_recv()
            total = total + self.plane[n].astype(F32)
        self.all[:, pl.ds(self.coord[0] * RING + own, 1)] = total.astype(BF)
        for c in self.plane_copies(True):
            c.start()

    def plane_to_ring(self):
        for c in self.plane_copies(True):
            c.wait_recv()
        for c in self.gather_copies((0, 1)):
            c.start()

    def pass_back(self):
        for n in range(2):
            came, goes = self.gather_copies((n, 2 + n))
            came.wait_recv()
            goes.start()

    def end(self):
        for c in self.gather_copies((2, 3)):
            c.wait_recv()

    def end_sends(self):
        for c in self.reduce_copies(range(6)) + self.plane_copies(False) + self.plane_copies(True) + self.gather_copies(range(4)):
            c.wait_send()


def sum_scratch(units):
    return [
        pltpu.VMEM((units, 64, 16, 128), BF),
        pltpu.VMEM((8, units, RING // 2, 16, 128), BF),
        pltpu.VMEM((15, units, 1, 16, 128), BF),
        pltpu.VMEM((units, RING, 16, 128), BF),
        pltpu.VMEM((units, 1, 16, 128), BF),
        pltpu.VMEM((units, 64, 16, 128), BF),
        pltpu.SemaphoreType.DMA((10,)),
        pltpu.SemaphoreType.DMA((10,)),
        pltpu.SemaphoreType.DMA((30,)),
        pltpu.SemaphoreType.DMA((30,)),
    ]


def sums_of(e, j, scratch):
    found = []
    for n, order in enumerate(ORDERS):
        s = scratch[10 * n : 10 * n + 10]
        found.append(Sum(e, j, order, *s[:6], s[6:8], s[8:10]))
    return found


UNITS = (4, 3, 3)
MINE = 216
OUT_AT = MINE
ROUTER_AT = OUT_AT + 144
SMALL_AT = ROUTER_AT + 48
OTHER_AT = 640 - MINE


def spots(first, count):
    table = [(n, u) for n in range(3) for u in range(UNITS[n])]
    done = 0
    while done < count:
        unit, place = divmod(first + done, 64)
        n = min(64 - place, count - done)
        yield table[unit] + (place, n, done)
        done += n


def tiles(value):
    return value.astype(BF).reshape(value.shape[0] // 16, 16, 128)


def rows_of_tiles(value):
    return value.reshape(value.shape[0] * 16, 128)


def back_kernel(lengths, home, hidden, mixed, router, routes_row, cot, tok, router_full, misc, wo, att, lse, qkv_any, normed_any, wqkv_any, layer_out, tokens_grad, q_sum, k_sum, v_sum, out_sum, router_sum, bias_sum, gain_sum, qkv, normed, wqkv, mask, diag, near, dout, stat, cols, dqkv, bias, branch, hidden_grad, half_out, half_in, grads, router_grad, stage, small, send, recv, core_send, core_recv, local, acc, *scratch):
    e = lax.axis_index("expert")
    j = lax.axis_index("wshard")
    jp = 1 - j
    here = pl.ds(pl.multiple_of(j * TOK, TOK), TOK)
    there = pl.ds(pl.multiple_of(jp * TOK, TOK), TOK)
    barrier = pltpu.get_barrier_semaphore()
    sums = sums_of(e, j, scratch)
    whole = tuple(s.part for s in sums)

    def run(first, count):
        ((n, unit, place, count, _),) = spots(first, count)
        return n, unit, place, place + count

    for m in OFFSETS:
        signal(barrier, chip_at(e, m), j)
    for n in range(1, 64):
        steps = (n // 16, n // 4 % 4, n % 4)
        if 0 in steps:
            signal(barrier, sums[0].peer(*steps), j)
    signal(barrier, e, jp)

    loads = [pltpu.make_async_copy(src, dst, local.at[n]) for n, (src, dst) in enumerate(((qkv_any, qkv), (normed_any, normed), (wqkv_any, wqkv)))]
    for c in loads:
        c.start()

    chosen, first, second = placing(routes_row)
    probs = router[...]
    gate = jnp.sum(probs * chosen, axis=1, keepdims=True)
    made = mm(first, home[0]) + mm(second, home[1])
    expert_back = mm(first, home[2]) + mm(second, home[3])
    total = hidden[...]
    layer_out[...] = (total + gate * made).astype(BF)
    dy = cot[...].astype(F32)
    gate_grad = jnp.sum(dy * made, axis=1, keepdims=True)
    logit_grad = ((gate_grad * gate) * (chosen - probs)).astype(BF)
    mixed_grad = mm(logit_grad, router_full[...], NT) + expert_back
    r = lax.rsqrt(jnp.mean(total * total, axis=-1, keepdims=True) + EPSILON)
    w = mixed_grad * both_gains(misc, 17)
    mix_gain = jnp.sum(mixed_grad * total * r, axis=0, keepdims=True)
    rest = dy + (r * w - total * (r * r * r * jnp.mean(w * total, axis=-1, keepdims=True)))
    hidden_grad[...] = rest
    branch[here, :] = rest.astype(BF)

    pl.semaphore_wait(barrier, len(OFFSETS) + 37)
    trade = remote(branch.at[here, :], branch.at[here, :], core_send.at[0], core_recv.at[0], e, jp)
    trade.start()
    router_grad[...] = tiles(mm(mixed[...], logit_grad, TN))
    router_rows = lambda core: router_grad.at[pl.ds(core * 24, 24)]
    n, unit, place, end = run(ROUTER_AT + 24, 24)
    router_trade = remote(router_rows(jp), whole[n].at[unit, place:end], core_send.at[1], core_recv.at[1], e, jp)
    router_trade.start()
    n, unit, place, end = run(ROUTER_AT, 24)
    whole[n][unit, place:end] = router_grad[pl.ds(j * 24, 24)]
    prepare(lengths, mask)
    prepare_biases(misc, diag, (1, -1))
    fill_near(diag, near, j, 2)
    trade.wait_recv()

    lane = lax.broadcasted_iota(jnp.int32, (CHIP, 128), 1)
    low = lax.broadcasted_iota(jnp.int32, (CHIP, 128), 0) < TOK
    mid = slice(MID, MID + CHIP)
    att_grad = mm(branch[...], wo[...], NT).astype(BF)
    dout[mid, :] = att_grad
    both = att_grad.astype(F32) * att[...].astype(F32)
    dots = jnp.zeros((CHIP, 128), F32)
    for h in range(6):
        own = (lane // HEAD) == h % 2
        dot = jnp.sum(jnp.where(own, both[:, (h // 2) * 128 : (h // 2) * 128 + 128], 0.0), axis=1, keepdims=True)
        dots = jnp.where(lane == h, dot, dots)
    stat[REACH, 0:8] = lse[...]
    stat[REACH, 8:16] = dots.T[0:8, :]
    cols[...] = jnp.concatenate([stat[REACH], jnp.zeros((112, CHIP), F32)], axis=0).T

    def window_copies(n):
        m = OFFSETS[n]
        slot = REACH if n < DIRECT else REACH - m // 2
        to = chip_at(e, m if n < DIRECT else m // 2)
        return [
            remote(dout.at[chunk(slot), :], dout.at[chunk(REACH - m), :], send.at[n, 0], recv.at[n, 0], to, j),
            remote(stat.at[slot], stat.at[REACH - m], send.at[n, 1], recv.at[n, 1], to, j),
        ]

    for n in range(DIRECT):
        for c in window_copies(n):
            c.start()
    grad = mm(att[...], branch[...], TN)
    for c in range(6):
        cut = tiles(grad[:, c * 128 : (c + 1) * 128])
        for n, unit, place, count, done in spots(OUT_AT + 24 * c, 24):
            whole[n][unit, place : place + count] = cut[done : done + count]
    for c in loads:
        c.wait()

    def forward_window():
        for n in range(2):
            for c in window_copies(n):
                c.wait_recv()
            for c in window_copies(DIRECT + n):
                c.start()

    line = lax.broadcasted_iota(jnp.int32, (NB, 128), 1)
    row32 = lax.broadcasted_iota(jnp.int32, (NB, 128), 0)
    hot = diagonal_buckets(1)
    bias[...] = jnp.zeros((NB, 128), F32)

    def by_queries(p):
        q = tile(qkv, mid, p * 128, 128).astype(F32) * 0.125
        do = tile(dout, mid, p * 128, 128)
        found = []
        for hh in range(2):
            h = 2 * p + hh
            own = (lane // HEAD) == hh
            spare = (1 - hh) * HEAD
            qm = jnp.where(own, q, 0.0).astype(BF)
            dom = jnp.where(own, do, jnp.zeros_like(do))
            log_sum = cols[:, h : h + 1]
            dot = cols[:, h + 8 : h + 9]
            ends = far_ends(diag, j * 6 + h)
            dq = jnp.zeros((CHIP, 128), F32)
            near_grads = []
            for c in range(SLOTS):
                k = tile(qkv, chunk(c), HALF + p * 128, 128)
                v = tile(qkv, chunk(c), 2 * HALF + p * 128, 128)
                s = biased(mm(qm, k, NT), c, mask, near.at[h], ends)
                ds = jnp.exp(s - log_sum) * (mm(dom, v, NT) - dot)
                if c < REACH - 1:
                    other = lane == spare
                elif c > REACH + 1:
                    other = lane == spare + 1
                elif c == REACH - 1:
                    other = lane == jnp.where(low, spare, spare + 2)
                elif c == REACH + 1:
                    other = lane == jnp.where(low, spare + 3, spare + 1)
                else:
                    other = lane < 0
                other = jnp.where(other, 1.0, 0.0).astype(BF)
                if abs(c - REACH) < 2:
                    near_grads.append(ds)
                dq = dq + mm(ds.astype(BF), jnp.where(own, k, other))
            found.append(dq * 0.125)
            before, same, after = near_grads
            fold = jnp.concatenate(
                [
                    before[0:TOK, TOK:] + same[TOK:, 0:TOK],
                    same[0:TOK, 0:TOK] + same[TOK:, TOK:],
                    same[0:TOK, TOK:] + after[TOK:, 0:TOK],
                    jnp.zeros((TOK, TOK), F32),
                ],
                axis=1,
            )
            rows = TOK
            while rows > 8:
                rows //= 2
                fold = fold[0:rows] + pltpu.roll(fold[rows : 2 * rows], LOOP - rows, 1)
            summed = fold[0:1]
            for n in range(1, 8):
                summed = summed + pltpu.roll(fold[n : n + 1], LOOP - n, 1)
            by_bucket = jnp.sum(hot * summed, axis=1, keepdims=True)
            far_low = jnp.sum(dq[0:TOK], axis=0, keepdims=True)
            far_high = jnp.sum(dq[TOK:], axis=0, keepdims=True)
            far = far_low + far_high
            far_left = far[:, spare : spare + 1] + far_high[:, spare + 2 : spare + 3]
            far_right = far[:, spare + 1 : spare + 2] + far_low[:, spare + 3 : spare + 4]
            by_bucket = by_bucket + jnp.where(row32 == 15, far_left, 0.0) + jnp.where(row32 == 31, far_right, 0.0)
            bias[...] = jnp.where(line == j * 6 + h, by_bucket, bias[...])
        dqkv[:, p * 128 : p * 128 + 128] = jnp.where(lane < HEAD, found[0], found[1]).astype(BF)
        if p == 0:
            forward_window()

    each_pair(by_queries)

    def by_keys(slots, p):
        k_own = tile(qkv, mid, HALF + p * 128, 128)
        v_own = tile(qkv, mid, 2 * HALF + p * 128, 128)
        found = []
        for hh in range(2):
            h = 2 * p + hh
            own = (lane // HEAD) == hh
            km = jnp.where(own, k_own, jnp.zeros_like(k_own))
            vm = jnp.where(own, v_own, jnp.zeros_like(v_own))
            ends = far_ends(diag, 16 + j * 6 + h)
            dk = jnp.zeros((CHIP, 128), F32)
            dv = jnp.zeros((CHIP, 128), F32)
            for c in slots:
                qc = (tile(qkv, chunk(c), p * 128, 128).astype(F32) * 0.125).astype(BF)
                dc = tile(dout, chunk(c), p * 128, 128)
                s = biased(mm(km, qc, NT), c, mask, near.at[6 + h], ends)
                prob = jnp.exp(s - stat[c, pl.ds(h, 1), :])
                ds = prob * (mm(vm, dc, NT) - stat[c, pl.ds(h + 8, 1), :])
                dv = dv + mm(prob.astype(BF), dc)
                dk = dk + mm(ds.astype(BF), qc)
            found.append((dk, dv))
        for n in range(2):
            where = slice(n * HALF + p * 128, n * HALF + p * 128 + 128)
            both = jnp.where(lane < HEAD, found[0][n], found[1][n])
            acc[:, where] = both if REACH in slots else acc[:, where] + both

    for n, slots in ((2, (REACH, 3, 5, 0, 8)), (4, (1, 7, 2, 6))):
        for m in (2, 3) if n == 2 else (4, 5, 6, 7):
            for c in window_copies(m):
                c.wait_recv()
        each_pair(functools.partial(by_keys, slots))
    dqkv[:, HALF:] = acc[...].astype(BF)

    half_out[...] = mm(dqkv[there, :], wqkv[...], NT).astype(BF)
    half_trade = remote(half_out, half_in, core_send.at[2], core_recv.at[2], e, jp)
    half_trade.start()
    swaps = []
    for n, unit, place, count, done in spots(OTHER_AT, MINE):
        swaps.append((done + count, remote(stage.at[done : done + count], whole[n].at[unit, place : place + count], core_send.at[4 + len(swaps)], core_recv.at[4 + len(swaps)], e, jp)))
    sent = 0
    for third in range(3):
        grad = mm(normed[...], dqkv[:, third * HALF : (third + 1) * HALF], TN)
        for c in range(3 * third, 3 * third + 3):
            grads[c % 3] = tiles(grad[:, (c % 3) * 128 : (c % 3 + 1) * 128])
            stage[24 * c : 24 * c + 24] = grads[c % 3, pl.ds(24 * jp, 24)]
            for n, unit, place, count, done in spots(24 * c, 24):
                whole[n][unit, place : place + count] = grads[c % 3, pl.ds(24 * j + done, count)]
        while sent < len(swaps) and swaps[sent][0] <= 72 * (third + 1):
            swaps[sent][1].start()
            sent += 1
    sums[0].start_ring()

    half = mm(dqkv[here, :], wqkv[...], NT)
    half_trade.wait_recv()
    grad = half + half_in[...].astype(F32)
    x = tok[...].astype(F32)
    r = lax.rsqrt(jnp.mean(x * x, axis=-1, keepdims=True) + EPSILON)
    w = grad * both_gains(misc, 16)
    tokens_grad[...] = (hidden_grad[...] + (r * w - x * (r * r * r * jnp.mean(w * x, axis=-1, keepdims=True)))).astype(BF)
    attn_gain = jnp.sum(grad * x * r, axis=0, keepdims=True)
    for h in range(2):
        lines = [v[:, h * HALF + 128 * n : h * HALF + 128 * n + 128] for v in (attn_gain, mix_gain) for n in range(3)]
        small[2 * h] = bias[16 * h : 16 * h + 16, :].astype(BF)
        small[2 * h + 1] = jnp.concatenate(lines + [jnp.zeros((10, 128), F32)], axis=0).astype(BF)
    n, unit, place, end = run(SMALL_AT, 4)
    whole[n][unit, place : place + 2] = small[pl.ds(2 * j, 2)]
    whole[n][unit, end : end + 12] = jnp.zeros((12, 16, 128), BF)
    small_trade = remote(small.at[pl.ds(2 * jp, 2)], whole[n].at[unit, place + 2 : end], core_send.at[3], core_recv.at[3], e, jp)
    small_trade.start()
    for _, c in swaps:
        c.wait_recv()
    sums[2].start_ring()
    router_trade.wait_recv()
    small_trade.wait_recv()
    sums[1].start_ring()
    for step in ("pass_ring", "ring_to_plane", "plane_back", "plane_to_ring", "pass_back", "end"):
        for n in (0, 2, 1):
            getattr(sums[n], step)()

    for c in range(6):
        for n, unit, place, count, done in spots(OUT_AT + 24 * c, 24):
            out_sum[16 * done : 16 * (done + count), c * 128 : (c + 1) * 128] = rows_of_tiles(sums[n].all[unit, place : place + count])
    n, unit, place, end = run(ROUTER_AT, 24)
    mine = sums[n].all[unit, place:end].astype(F32)
    n, unit, place, end = run(ROUTER_AT + 24, 24)
    router_sum[...] = rows_of_tiles(mine + sums[n].all[unit, place:end].astype(F32))
    qkv_sums = (q_sum, k_sum, v_sum)
    for c in range(9):
        for first_tile, core in ((24 * c, j), (OTHER_AT + 24 * c, jp)):
            column = pl.ds(pl.multiple_of(core * HALF + (c % 3) * 128, 128), 128)
            for n, unit, place, count, done in spots(first_tile, 24):
                qkv_sums[c // 3][16 * done : 16 * (done + count), column] = rows_of_tiles(sums[n].all[unit, place : place + count])
    n, unit, place, end = run(SMALL_AT, 4)
    smalls = sums[n].all[unit, place : place + 2].astype(F32) + sums[n].all[unit, place + 2 : end].astype(F32)
    bias_sum[...] = smalls[0]
    gain_sum[...] = smalls[1]

    for c in (trade, router_trade, half_trade, small_trade):
        c.wait_send()
    for _, c in swaps:
        c.wait_send()
    for n in range(len(OFFSETS)):
        for c in window_copies(n):
            c.wait_send()
    for s in sums:
        s.end_sends()


def back(lengths, *operands):
    vm = pl.BlockSpec(memory_space=pltpu.VMEM)
    return pl.pallas_call(
        back_kernel,
        name="back",
        out_shape=(
            jax.ShapeDtypeStruct((TOK, D), BF),
            jax.ShapeDtypeStruct((TOK, D), BF),
            jax.ShapeDtypeStruct((HALF, D), BF),
            jax.ShapeDtypeStruct((HALF, D), BF),
            jax.ShapeDtypeStruct((HALF, D), BF),
            jax.ShapeDtypeStruct((HALF, D), BF),
            jax.ShapeDtypeStruct((HALF, EXPERTS), F32),
            jax.ShapeDtypeStruct((16, 128), F32),
            jax.ShapeDtypeStruct((16, 128), F32),
        ),
        in_specs=[pl.BlockSpec(memory_space=pltpu.SMEM)] + [vm] * 12 + [pl.BlockSpec(memory_space=pl.ANY)] * 3,
        out_specs=(vm,) * 9,
        scratch_shapes=[
            pltpu.VMEM((WIN, 3 * HALF), BF),
            pltpu.VMEM((CHIP, D), BF),
            pltpu.VMEM((D, 3 * HALF), BF),
            pltpu.VMEM((CHIP, WIN), F32),
            pltpu.VMEM((32, LOOP), F32),
            pltpu.VMEM((12, TOK, NEAR), F32),
            pltpu.VMEM((WIN, HALF), BF),
            pltpu.VMEM((SLOTS, 16, CHIP), F32),
            pltpu.VMEM((CHIP, 128), F32),
            pltpu.VMEM((CHIP, 3 * HALF), BF),
            pltpu.VMEM((NB, 128), F32),
            pltpu.VMEM((CHIP, D), BF),
            pltpu.VMEM((TOK, D), F32),
            pltpu.VMEM((TOK, D), BF),
            pltpu.VMEM((TOK, D), BF),
            pltpu.VMEM((3, 48, 16, 128), BF),
            pltpu.VMEM((48, 16, 128), BF),
            pltpu.VMEM((MINE, 16, 128), BF),
            pltpu.VMEM((4, 16, 128), BF),
            pltpu.SemaphoreType.DMA((8, 2)),
            pltpu.SemaphoreType.DMA((8, 2)),
            pltpu.SemaphoreType.DMA((8,)),
            pltpu.SemaphoreType.DMA((8,)),
            pltpu.SemaphoreType.DMA((3,)),
            pltpu.VMEM((CHIP, 2 * HALF), F32),
            *[s for units in UNITS for s in sum_scratch(units)],
        ],
        compiler_params=pltpu.CompilerParams(collective_id=2, has_side_effects=True, vmem_limit_bytes=VMEM_BYTES),
    )(lengths, *operands)


def finish_kernel(*refs):
    for src, dst in zip(refs[:8], refs[8:]):
        dst[...] = src[:, 0 : dst.shape[1]].astype(dst.dtype)


def finish(*results):
    vm = pl.BlockSpec(memory_space=pltpu.VMEM)
    kinds = ((TOK, D, BF), (TOK, D, BF)) + ((HALF, D, F32),) * 4 + ((HALF, EXPERTS, F32), (16, 12, F32))
    return pl.pallas_call(
        finish_kernel,
        name="finish",
        out_shape=tuple(jax.ShapeDtypeStruct((rows, columns), kind) for rows, columns, kind in kinds),
        in_specs=[vm] * 8,
        out_specs=(vm,) * 8,
        compiler_params=pltpu.CompilerParams(vmem_limit_bytes=VMEM_BYTES),
    )(*results)


def to_all(rows):
    return lax.all_to_all(rows, ("expert", "wshard"), split_axis=1, concat_axis=1, tiled=True)


def per_device(tokens, lengths, routes, attn_gain, query_weight, key_weight, value_weight, output_weight, bias_table, mix_gain, router_weight, expert_in, expert_out, cotangent):
    row = routes.reshape(1, TOK)
    qkv, normed, wqkv, router_full, misc_full, att, lse, hidden, mixed, router, sent = front(
        lengths, tokens, query_weight, key_weight, value_weight, output_weight, router_weight, attn_gain, mix_gain, bias_table, row, cotangent
    )

    arrived = to_all(sent).reshape(4 * EXPERTS, D)
    made_back, expert_in_grad, expert_out_grad = expert(arrived, expert_in, expert_out)
    home = to_all(made_back.reshape(4, EXPERTS, D))
    *results, gain_sum = back(lengths, home, hidden, mixed, router, row, cotangent, tokens, router_full, misc_full, output_weight, att, lse, qkv, normed, wqkv)
    layer_out, tokens_grad, query_grad, key_grad, value_grad, output_grad, router_grad, bias_grad = finish(*results)
    return (
        layer_out,
        tokens_grad,
        gain_sum[0:3].reshape(HALF),
        query_grad,
        key_grad,
        value_grad,
        output_grad,
        bias_grad,
        gain_sum[3:6].reshape(HALF),
        router_grad,
        expert_in_grad,
        expert_out_grad,
    )


def solution(mesh):
    by_token = P(("expert", "wshard"), None)
    by_row = P("wshard", None)
    by_expert = P(("expert", "wshard"), None, None)
    return jax.shard_map(
        per_device,
        mesh=mesh,
        in_specs=(
            by_token,
            P(),
            by_token,
            P("wshard"),
            by_row,
            by_row,
            by_row,
            by_row,
            by_row,
            P("wshard"),
            by_row,
            by_expert,
            by_expert,
            by_token,
        ),
        out_specs=(
            by_token,
            by_token,
            P("wshard"),
            by_row,
            by_row,
            by_row,
            by_row,
            by_row,
            P("wshard"),
            by_row,
            by_expert,
            by_expert,
        ),
        check_vma=False,
    )
```

```python
import functools

import jax
import jax.numpy as jnp
from jax import lax
from jax.experimental import pallas as pl
from jax.experimental.pallas import tpu as pltpu
from jax.sharding import PartitionSpec as P

MESH = pl.DeviceIdType.MESH
BF = jnp.bfloat16
F32 = jnp.float32
EPSILON = 1e-06
FAR_EDGES = (12, 16, 23, 32, 46, 64, 91)

D = 768
HALF = 384
HEAD = 64
TOK = 128
CHIP = 256
REACH = 4
SLOTS = 2 * REACH + 1
WIN = SLOTS * CHIP
MID = REACH * CHIP
TOTAL = 16384
EXPERTS = 128
NB = 32
FF = 3072
NEAR = 3 * TOK
LOOP = 512
VMEM_BYTES = 56 * 1024 * 1024

NT = (((1,), (1,)), ((), ()))
TN = (((0,), (0,)), ((), ()))
NN = (((1,), (0,)), ((), ()))


def mm(left, right, dims=NN):
    return lax.dot_general(left, right, dims, preferred_element_type=F32)


def bucket_of(relative):
    distance = jnp.abs(relative)
    far_bucket = 8 + sum(((distance >= edge).astype(jnp.int32) for edge in FAR_EDGES))
    near_far = jnp.where(distance < 8, distance, far_bucket)
    return near_far + 16 * (relative > 0).astype(jnp.int32)


def tile(ref, rows, start, width):
    if isinstance(start, int):
        return ref[rows, start : start + width]
    return ref[rows, pl.ds(pl.multiple_of(start, 128), width)]


def each_pair(body):
    for p in range(3):
        body(p)


OFFSETS = (1, -1, 4, -4, 3, -3, 2, -2)
DIRECT = 6
AXES = {"y": 16, "x": 4, "z": 1}


def remote(src, dst, ssem, rsem, chip, core):
    return pltpu.make_async_remote_copy(src_ref=src, dst_ref=dst, send_sem=ssem, recv_sem=rsem, device_id=(chip, core), device_id_type=MESH)


def chip_at(e, m):
    chips = lax.axis_size("expert")
    return lax.rem(e + m + chips, chips)


def signal(barrier, chip, core):
    pl.semaphore_signal(barrier, inc=1, device_id=(chip, core), device_id_type=MESH)


def chunk(c):
    return slice(c * CHIP, (c + 1) * CHIP)


def both_gains(misc, row):
    return jnp.concatenate([misc[row : row + 1, :], misc[row + 24 : row + 25, :]], axis=1)


def placing(routes_row):
    lane = lax.broadcasted_iota(jnp.int32, (TOK, EXPERTS), 1)
    row = lax.broadcasted_iota(jnp.int32, (TOK, EXPERTS), 0)
    across = jnp.broadcast_to(routes_row[0:1, :], (TOK, TOK))
    down = across.T
    chosen = (down == lane).astype(F32)
    earlier = ((down == across) & (lane < row)).astype(F32)
    second = jnp.max(earlier, axis=1, keepdims=True)
    return chosen, (chosen * (1.0 - second)).astype(BF), (chosen * second).astype(BF)


def prepare(lengths, mask):
    e = lax.axis_index("expert")
    row_pos = (e - REACH) * CHIP + lax.broadcasted_iota(jnp.int32, (8, WIN), 1)
    col_pos = e * CHIP + lax.broadcasted_iota(jnp.int32, (CHIP, 128), 0)

    def count(n, state):
        end, rows, cols = state
        end = end + lengths[n]
        return end, rows + (row_pos >= end).astype(jnp.int32), cols + (col_pos >= end).astype(jnp.int32)

    zero = jnp.zeros((8, WIN), jnp.int32)
    _, rows, cols = lax.fori_loop(0, 32, count, (jnp.int32(0), zero, jnp.zeros((CHIP, 128), jnp.int32)))
    rows = jnp.where((row_pos >= 0) & (row_pos < TOTAL), rows, -1)
    for c in range(SLOTS):
        part = rows[0:1, c * CHIP : (c + 1) * CHIP]
        mask[:, c * CHIP : (c + 1) * CHIP] = jnp.where(cols[:, 0:1] == part, 0.0, -1e9).astype(F32)


def prepare_biases(misc, diag, ways):
    table = jnp.concatenate([misc[0:16, 0:128], misc[24:40, 0:128]], axis=0).astype(BF)
    for n, sign in enumerate(ways):
        hot = diagonal_buckets(sign)
        diag[n * 16 : (n + 1) * 16, :] = mm(table, hot.astype(BF), TN)[0:16]


def diagonal_buckets(sign):
    m = lax.broadcasted_iota(jnp.int32, (NB, LOOP), 1)
    r = jnp.where(m < NEAR, m, m - LOOP) - TOK
    b = lax.broadcasted_iota(jnp.int32, (NB, LOOP), 0)
    return (bucket_of(sign * r) == b).astype(F32)


def biased(raw, c, mask, near, ends):
    s = raw + mask[:, c * CHIP : (c + 1) * CHIP]
    left, right = ends
    if c < REACH - 1:
        return s + left
    if c > REACH + 1:
        return s + right
    t = [near[:, n * TOK : (n + 1) * TOK] for n in range(3)]
    added = {REACH - 1: (left, t[0], left, left), REACH: (t[1], t[2], t[0], t[1]), REACH + 1: (right, right, t[2], right)}[c]
    return jnp.concatenate(
        [jnp.concatenate([s[i * TOK : (i + 1) * TOK, n * TOK : (n + 1) * TOK] + added[2 * i + n] for n in range(2)], axis=1) for i in range(2)], axis=0
    )


def fill_near(diag, near, j, ways):
    def one(n, carry):
        line = diag[pl.ds(n // 6 * 16 + j * 6 + lax.rem(n, 6), 1), :]
        spread = pltpu.roll(jnp.broadcast_to(line, (TOK, LOOP)), 0, 1, stride=1, stride_axis=0)
        near[n] = spread[:, 0:NEAR]
        return carry

    lax.fori_loop(0, 6 * ways, one, 0)


def far_ends(diag, row):
    line = diag[pl.ds(row, 1), :]
    return line[:, 0:1], line[:, NEAR - 1 : NEAR]


def front_kernel(lengths, tok_any, wq, wk, wv, wo_any, router_any, gain_one, gain_two, bias_rows, tok, wo, routes_row, cot, qkv_any, normed_any, wqkv_any, router_full, misc, att, lse, hidden, mixed, router, sent, qkv, normed, wqkv, misc_mine, win, wo_other, att_other, mask, diag, near, scores, tops, lse_cols, send, recv, fsend, frecv, wsend, wrecv, local, store):
    e = lax.axis_index("expert")
    j = lax.axis_index("wshard")
    jp = 1 - j
    barrier = pltpu.get_barrier_semaphore()
    for m in OFFSETS:
        signal(barrier, chip_at(e, m), j)
    signal(barrier, e, jp)

    def rows_of(slot, core):
        return win.at[pl.ds(pl.multiple_of(slot * CHIP + core * TOK, TOK), TOK), :]

    misc_mine[...] = jnp.zeros((24, HALF), F32)
    misc_mine[16:17, :] = gain_one[...].astype(F32).reshape(1, HALF)
    misc_mine[17:18, :] = gain_two[...].astype(F32).reshape(1, HALF)
    misc_mine[0:16, 0:12] = bias_rows[...].astype(F32)
    weights = []
    kept = []
    for n, w in enumerate((wq, wk, wv)):
        rows = pl.ds(pl.multiple_of(j * HALF, HALF), HALF)
        there = w.at[:, pl.ds(pl.multiple_of(jp * HALF, 128), HALF)]
        here = w.at[:, pl.ds(pl.multiple_of(j * HALF, 128), HALF)]
        dst = wqkv.at[rows, n * HALF : (n + 1) * HALF]
        weights.append(remote(there, dst, wsend.at[n], wrecv.at[n], e, jp))
        kept.append(pltpu.make_async_copy(here, dst, local.at[1 + n]))
    for n, (src, dst, size) in enumerate(((misc_mine, misc, 24), (router_any, router_full, HALF))):
        rows = pl.ds(pl.multiple_of(j * size, 8), size)
        weights.append(remote(src, dst.at[rows, :], wsend.at[3 + n], wrecv.at[3 + n], e, jp))
        kept.append(pltpu.make_async_copy(src, dst.at[rows, :], local.at[4 + n]))
    weights.append(remote(wo_any, wo_other, wsend.at[5], wrecv.at[5], e, jp))
    mine = pltpu.make_async_copy(tok_any, rows_of(REACH, j), local.at[0])
    mine.start()
    for c in kept:
        c.start()

    copies = []
    for n, m in enumerate(OFFSETS):
        src = tok_any if n < DIRECT else rows_of(REACH - m // 2, j)
        to = chip_at(e, m if n < DIRECT else m // 2)
        copies.append(remote(src, rows_of(REACH - m, j), send.at[n], recv.at[n], to, j))
    passed = [remote(rows_of(REACH - m, j), rows_of(REACH - m, j), fsend.at[n], frecv.at[n], e, jp) for n, m in enumerate(OFFSETS)]
    swap = remote(tok_any, rows_of(REACH, j), fsend.at[8], frecv.at[8], e, jp)

    pl.semaphore_wait(barrier, len(OFFSETS) + 1)
    for c in copies[:DIRECT]:
        c.start()
    weights[3].start()
    for c in weights[:3]:
        c.start()
    swap.start()
    for c in weights[4:]:
        c.start()
    prepare(lengths, mask)
    mine.wait()
    for c in kept:
        c.wait()
    for c in weights[:4]:
        c.wait_recv()
    prepare_biases(misc, diag, (1,))
    fill_near(diag, near, j, 1)
    gain = both_gains(misc, 16)

    lane = lax.broadcasted_iota(jnp.int32, (CHIP, 128), 1)

    def project(slot):
        x = win[chunk(slot), :].astype(F32)
        y = (x * lax.rsqrt(jnp.mean(x * x, axis=-1, keepdims=True) + EPSILON) * gain).astype(BF)
        if slot == REACH:
            normed[...] = y
        qkv[chunk(slot), :] = mm(y, wqkv[...]).astype(BF)

        def score(p, carry):
            q = tile(qkv, slice(MID, MID + CHIP), p * 128, 128).astype(F32) * 0.125
            k = tile(qkv, chunk(slot), HALF + p * 128, 128)
            for hh in range(2):
                h = 2 * p + hh
                qm = jnp.where((lane // HEAD) == hh, q, 0.0).astype(BF)
                s = biased(mm(qm, k, NT), slot, mask, near.at[h], far_ends(diag, j * 6 + h))
                scores[h, :, chunk(slot)] = s
                top = jnp.maximum(s[:, 0:128], s[:, 128:256])
                tops[h] = top if slot == REACH else jnp.maximum(tops[h], top)
            return carry

        lax.fori_loop(0, 3, score, 0)

    for n in range(2):
        copies[n].wait_recv()
        copies[DIRECT + n].start()
        passed[n].start()
    swap.wait_recv()
    project(REACH)
    for n in range(2, len(OFFSETS) + 2):
        if n < len(OFFSETS):
            copies[n].wait_recv()
            passed[n].start()
        passed[n - 2].wait_recv()
        project(REACH - OFFSETS[n - 2])

    stores = [pltpu.make_async_copy(src, dst, store.at[n]) for n, (src, dst) in enumerate(((qkv, qkv_any), (normed, normed_any), (wqkv, wqkv_any)))]
    for c in stores:
        c.start()
    lse_cols[...] = jnp.zeros((CHIP, 128), F32)

    def pair(p):
        outs = []
        for hh in range(2):
            h = 2 * p + hh
            top = jnp.max(tops[h], axis=1, keepdims=True)
            total = jnp.zeros((CHIP, CHIP), F32)
            out = jnp.zeros((CHIP, 128), F32)
            for c in range(SLOTS):
                x = jnp.exp(scores[h, :, chunk(c)] - top)
                total = total + x
                out = out + mm(x.astype(BF), tile(qkv, chunk(c), 2 * HALF + p * 128, 128))
            total = jnp.sum(total, axis=1, keepdims=True)
            outs.append(out / total)
            lse_cols[...] = jnp.where(lane == h, top + jnp.log(total), lse_cols[...])
        att[:, p * 128 : p * 128 + 128] = jnp.where(lane < HEAD, outs[0], outs[1]).astype(BF)

    each_pair(pair)
    lse[...] = lse_cols[...].T[0:8, :]

    here = pl.ds(pl.multiple_of(j * TOK, TOK), TOK)
    there = pl.ds(pl.multiple_of(jp * TOK, TOK), TOK)
    trade = remote(att.at[there, :], att_other, wsend.at[6], wrecv.at[6], e, jp)
    trade.start()
    chosen, first, second = placing(routes_row)
    branch = mm(att[here, :], wo[...])
    for c in weights[4:]:
        c.wait_recv()
    trade.wait_recv()
    total = tok[...].astype(F32) + (branch + mm(att_other[...], wo_other[...]))
    hidden[...] = total
    low = (total * lax.rsqrt(jnp.mean(total * total, axis=-1, keepdims=True) + EPSILON) * both_gains(misc, 17)).astype(BF)
    mixed[...] = low
    logits = mm(low, router_full[...])
    powers = jnp.exp(logits - jnp.max(logits, axis=1, keepdims=True))
    probs = powers / jnp.sum(powers, axis=1, keepdims=True)
    router[...] = probs
    gate = jnp.sum(probs * chosen, axis=1, keepdims=True)
    made_grad = (gate * cot[...].astype(F32)).astype(BF)
    for n, (place, rows) in enumerate(((first, low), (second, low), (first, made_grad), (second, made_grad))):
        sent[n] = mm(place, rows, TN).astype(BF)

    trade.wait_send()
    swap.wait_send()
    for c in weights + copies + passed:
        c.wait_send()
    for c in stores:
        c.wait()


def front(lengths, tokens, wq, wk, wv, wo, router, gain_one, gain_two, bias, row, cotangent):
    smem = pl.BlockSpec(memory_space=pltpu.SMEM)
    hbm = pl.BlockSpec(memory_space=pl.ANY)
    vm = pl.BlockSpec(memory_space=pltpu.VMEM)
    return pl.pallas_call(
        front_kernel,
        name="front",
        out_shape=(
            jax.ShapeDtypeStruct((WIN, 3 * HALF), BF),
            jax.ShapeDtypeStruct((CHIP, D), BF),
            jax.ShapeDtypeStruct((D, 3 * HALF), BF),
            jax.ShapeDtypeStruct((D, EXPERTS), BF),
            jax.ShapeDtypeStruct((48, HALF), F32),
            jax.ShapeDtypeStruct((CHIP, HALF), BF),
            jax.ShapeDtypeStruct((8, CHIP), F32),
            jax.ShapeDtypeStruct((TOK, D), F32),
            jax.ShapeDtypeStruct((TOK, D), BF),
            jax.ShapeDtypeStruct((TOK, EXPERTS), F32),
            jax.ShapeDtypeStruct((4, EXPERTS, D), BF),
        ),
        in_specs=[smem] + [hbm] * 6 + [vm] * 7,
        out_specs=(hbm,) * 3 + (vm,) * 8,
        scratch_shapes=[
            pltpu.VMEM((WIN, 3 * HALF), BF),
            pltpu.VMEM((CHIP, D), BF),
            pltpu.VMEM((D, 3 * HALF), BF),
            pltpu.VMEM((24, HALF), F32),
            pltpu.VMEM((WIN, D), BF),
            pltpu.VMEM((HALF, D), BF),
            pltpu.VMEM((TOK, HALF), BF),
            pltpu.VMEM((CHIP, WIN), F32),
            pltpu.VMEM((16, LOOP), F32),
            pltpu.VMEM((6, TOK, NEAR), F32),
            pltpu.VMEM((6, CHIP, WIN), F32),
            pltpu.VMEM((6, CHIP, 128), F32),
            pltpu.VMEM((CHIP, 128), F32),
            pltpu.SemaphoreType.DMA((8,)),
            pltpu.SemaphoreType.DMA((8,)),
            pltpu.SemaphoreType.DMA((9,)),
            pltpu.SemaphoreType.DMA((9,)),
            pltpu.SemaphoreType.DMA((7,)),
            pltpu.SemaphoreType.DMA((7,)),
            pltpu.SemaphoreType.DMA((6,)),
            pltpu.SemaphoreType.DMA((3,)),
        ],
        compiler_params=pltpu.CompilerParams(collective_id=1, has_side_effects=True, vmem_limit_bytes=VMEM_BYTES),
    )(lengths, tokens, wq, wk, wv, wo, router, gain_one, gain_two, bias, tokens, wo, row, cotangent)


FF_TILE = 768


def expert_kernel(x, g, w_in, w_out, made_back, d_in, d_out, made_sum, back_sum, across):
    step = pl.program_id(0)

    @pl.when(step == 0)
    def _():
        made_sum[...] = jnp.zeros_like(made_sum)
        back_sum[...] = jnp.zeros_like(back_sum)
        across[...] = x[...].T

    pre = mm(x[...], w_in[0])
    half_erf = 0.5 * lax.erf(pre * (0.5**0.5)) + 0.5
    act = (pre * half_erf).astype(BF)
    slope = half_erf + pre * jnp.exp(-0.5 * pre * pre) * (0.5 * 0.7978845608028654)
    act_grad = mm(g[...], w_out[0], NT)
    pre_grad = (act_grad * slope).astype(BF)
    made_sum[...] += mm(act, w_out[0])
    back_sum[...] += mm(pre_grad, w_in[0], NT)
    d_out[0] = mm(act, g[...], TN).astype(BF)
    d_in[0] = mm(across[...], pre_grad).astype(BF)

    @pl.when(step == pl.num_programs(0) - 1)
    def _():
        made_back[0 : 2 * EXPERTS, :] = made_sum[...].astype(BF)
        made_back[2 * EXPERTS :, :] = back_sum[...].astype(BF)


def expert(arrived, w_in, w_out):
    rows = 2 * EXPERTS
    forward = pl.BlockSpec((rows, D), lambda f: (0, 0))
    backward = pl.BlockSpec((rows, D), lambda f: (1, 0))
    whole = pl.BlockSpec((2 * rows, D), lambda f: (0, 0))
    by_in = pl.BlockSpec((1, D, FF_TILE), lambda f: (0, 0, f))
    by_out = pl.BlockSpec((1, FF_TILE, D), lambda f: (0, f, 0))
    return pl.pallas_call(
        expert_kernel,
        name="expert",
        grid=(FF // FF_TILE,),
        out_shape=(
            jax.ShapeDtypeStruct((2 * rows, D), BF),
            jax.ShapeDtypeStruct((1, D, FF), BF),
            jax.ShapeDtypeStruct((1, FF, D), BF),
        ),
        in_specs=[forward, backward, by_in, by_out],
        out_specs=(whole, by_in, by_out),
        scratch_shapes=[pltpu.VMEM((rows, D), F32), pltpu.VMEM((rows, D), F32), pltpu.VMEM((D, rows), BF)],
        compiler_params=pltpu.CompilerParams(vmem_limit_bytes=VMEM_BYTES, dimension_semantics=("arbitrary",)),
    )(arrived, arrived, w_in, w_out)


ORDERS = ("zxy", "xyz", "yzx")
RING = 16
PLANE = [(d, f) for d in range(4) for f in range(4) if d + f > 0]


class Sum:
    def __init__(self, e, j, order, part, ring, plane, ring_sum, plane_sum, all_, ring_sems, plane_sems):
        self.e, self.j, self.order = e, j, order
        self.part, self.ring, self.plane, self.ring_sum, self.plane_sum, self.all = part, ring, plane, ring_sum, plane_sum, all_
        self.ring_sems, self.plane_sems = ring_sems, plane_sems
        self.coord = [lax.rem(e // AXES[a], 4) for a in order]

    def peer(self, *steps):
        to = self.e
        for axis, at, d in zip(self.order, self.coord, steps):
            to = to + (lax.rem(at + d, 4) - at) * AXES[axis]
        return to

    def block(self, d, first, count):
        return pl.ds(lax.rem(self.coord[0] + d + 4, 4) * RING + first, count)

    def copy(self, src, dst, sems, n, to):
        return remote(src, dst, sems[0].at[n], sems[1].at[n], to, self.j)

    def reduce_copies(self, which):
        h = RING // 2
        up, down = self.peer(1), self.peer(3)
        pieces = [
            (lambda: self.part.at[:, self.block(2, 0, h)], up),
            (lambda: self.part.at[:, self.block(2, h, h)], down),
            (lambda: self.part.at[:, self.block(1, h, h)], up),
            (lambda: self.part.at[:, self.block(3, 0, h)], down),
            (lambda: self.ring.at[6], up),
            (lambda: self.ring.at[7], down),
        ]
        return [self.copy(pieces[n][0](), self.ring.at[n], self.ring_sems, n, pieces[n][1]) for n in which]

    def gather_copies(self, which):
        h = RING // 2
        up, down = self.peer(1), self.peer(3)
        pieces = [(0, 0, RING, up), (0, 0, RING, down), (-1, 0, h, up), (1, h, h, down)]
        found = []
        for n in which:
            d, first, count, to = pieces[n]
            ref = self.all.at[:, self.block(d, first, count)]
            found.append(self.copy(ref, ref, self.ring_sems, 6 + n, to))
        return found

    def plane_copies(self, back):
        found = []
        for n, (d, f) in enumerate(PLANE):
            to = self.peer(0, d, f)
            if back:
                ref = self.all.at[:, pl.ds(self.coord[0] * RING + self.coord[1] * 4 + self.coord[2], 1)]
                found.append(self.copy(ref, ref, self.plane_sems, 15 + n, to))
            else:
                place = lax.rem(self.coord[1] + d, 4) * 4 + lax.rem(self.coord[2] + f, 4)
                found.append(self.copy(self.ring_sum.at[:, pl.ds(place, 1)], self.plane.at[n], self.plane_sems, n, to))
        return found

    def start_ring(self):
        for c in self.reduce_copies(range(4)):
            c.start()

    def pass_ring(self):
        h = RING // 2
        for n, where in ((0, self.block(1, 0, h)), (1, self.block(3, h, h))):
            came, goes = self.reduce_copies((n, 4 + n))
            came.wait_recv()
            self.ring[6 + n] = (self.part[:, where].astype(F32) + self.ring[n].astype(F32)).astype(BF)
            goes.start()

    def ring_to_plane(self):
        h = RING // 2
        for c in self.reduce_copies(range(2, 6)):
            c.wait_recv()
        for first, others in ((0, (4, 3)), (h, (5, 2))):
            total = self.part[:, self.block(0, first, h)].astype(F32)
            for n in others:
                total = total + self.ring[n].astype(F32)
            self.ring_sum[:, first : first + h] = total.astype(BF)
        for c in self.plane_copies(False):
            c.start()

    def plane_back(self):
        own = self.coord[1] * 4 + self.coord[2]
        total = self.ring_sum[:, pl.ds(own, 1)].astype(F32)
        for n, c in enumerate(self.plane_copies(False)):
            c.wait_recv()
            total = total + self.plane[n].astype(F32)
        self.all[:, pl.ds(self.coord[0] * RING + own, 1)] = total.astype(BF)
        for c in self.plane_copies(True):
            c.start()

    def plane_to_ring(self):
        for c in self.plane_copies(True):
            c.wait_recv()
        for c in self.gather_copies((0, 1)):
            c.start()

    def pass_back(self):
        for n in range(2):
            came, goes = self.gather_copies((n, 2 + n))
            came.wait_recv()
            goes.start()

    def end(self):
        for c in self.gather_copies((2, 3)):
            c.wait_recv()

    def end_sends(self):
        for c in self.reduce_copies(range(6)) + self.plane_copies(False) + self.plane_copies(True) + self.gather_copies(range(4)):
            c.wait_send()


def sum_scratch(units):
    return [
        pltpu.VMEM((units, 64, 16, 128), BF),
        pltpu.VMEM((8, units, RING // 2, 16, 128), BF),
        pltpu.VMEM((15, units, 1, 16, 128), BF),
        pltpu.VMEM((units, RING, 16, 128), BF),
        pltpu.VMEM((units, 1, 16, 128), BF),
        pltpu.VMEM((units, 64, 16, 128), BF),
        pltpu.SemaphoreType.DMA((10,)),
        pltpu.SemaphoreType.DMA((10,)),
        pltpu.SemaphoreType.DMA((30,)),
        pltpu.SemaphoreType.DMA((30,)),
    ]


def sums_of(e, j, scratch):
    found = []
    for n, order in enumerate(ORDERS):
        s = scratch[10 * n : 10 * n + 10]
        found.append(Sum(e, j, order, *s[:6], s[6:8], s[8:10]))
    return found


UNITS = (4, 3, 3)
MINE = 216
OUT_AT = MINE
ROUTER_AT = OUT_AT + 144
SMALL_AT = ROUTER_AT + 48
OTHER_AT = 640 - MINE


def spots(first, count):
    table = [(n, u) for n in range(3) for u in range(UNITS[n])]
    done = 0
    while done < count:
        unit, place = divmod(first + done, 64)
        n = min(64 - place, count - done)
        yield table[unit] + (place, n, done)
        done += n


def tiles(value):
    return value.astype(BF).reshape(value.shape[0] // 16, 16, 128)


def rows_of_tiles(value):
    return value.reshape(value.shape[0] * 16, 128)


def back_kernel(lengths, home, hidden, mixed, router, routes_row, cot, tok, router_full, misc, wo, att, lse, qkv_any, normed_any, wqkv_any, layer_out, tokens_grad, q_sum, k_sum, v_sum, out_sum, router_sum, bias_sum, gain_sum, qkv, normed, wqkv, mask, diag, near, dout, stat, cols, dqkv, bias, branch, hidden_grad, half_out, half_in, grads, router_grad, stage, small, send, recv, core_send, core_recv, local, acc, *scratch):
    e = lax.axis_index("expert")
    j = lax.axis_index("wshard")
    jp = 1 - j
    here = pl.ds(pl.multiple_of(j * TOK, TOK), TOK)
    there = pl.ds(pl.multiple_of(jp * TOK, TOK), TOK)
    barrier = pltpu.get_barrier_semaphore()
    sums = sums_of(e, j, scratch)
    whole = tuple(s.part for s in sums)

    def run(first, count):
        ((n, unit, place, count, _),) = spots(first, count)
        return n, unit, place, place + count

    for m in OFFSETS:
        signal(barrier, chip_at(e, m), j)
    for n in range(1, 64):
        steps = (n // 16, n // 4 % 4, n % 4)
        if 0 in steps:
            signal(barrier, sums[0].peer(*steps), j)
    signal(barrier, e, jp)

    loads = [pltpu.make_async_copy(src, dst, local.at[n]) for n, (src, dst) in enumerate(((qkv_any, qkv), (normed_any, normed), (wqkv_any, wqkv)))]
    for c in loads:
        c.start()

    chosen, first, second = placing(routes_row)
    probs = router[...]
    gate = jnp.sum(probs * chosen, axis=1, keepdims=True)
    made = mm(first, home[0]) + mm(second, home[1])
    expert_back = mm(first, home[2]) + mm(second, home[3])
    total = hidden[...]
    layer_out[...] = (total + gate * made).astype(BF)
    dy = cot[...].astype(F32)
    gate_grad = jnp.sum(dy * made, axis=1, keepdims=True)
    logit_grad = ((gate_grad * gate) * (chosen - probs)).astype(BF)
    mixed_grad = mm(logit_grad, router_full[...], NT) + expert_back
    r = lax.rsqrt(jnp.mean(total * total, axis=-1, keepdims=True) + EPSILON)
    w = mixed_grad * both_gains(misc, 17)
    mix_gain = jnp.sum(mixed_grad * total * r, axis=0, keepdims=True)
    rest = dy + (r * w - total * (r * r * r * jnp.mean(w * total, axis=-1, keepdims=True)))
    hidden_grad[...] = rest
    branch[here, :] = rest.astype(BF)

    pl.semaphore_wait(barrier, len(OFFSETS) + 37)
    trade = remote(branch.at[here, :], branch.at[here, :], core_send.at[0], core_recv.at[0], e, jp)
    trade.start()
    router_grad[...] = tiles(mm(mixed[...], logit_grad, TN))
    router_rows = lambda core: router_grad.at[pl.ds(core * 24, 24)]
    n, unit, place, end = run(ROUTER_AT + 24, 24)
    router_trade = remote(router_rows(jp), whole[n].at[unit, place:end], core_send.at[1], core_recv.at[1], e, jp)
    router_trade.start()
    n, unit, place, end = run(ROUTER_AT, 24)
    whole[n][unit, place:end] = router_grad[pl.ds(j * 24, 24)]
    prepare(lengths, mask)
    prepare_biases(misc, diag, (1, -1))
    fill_near(diag, near, j, 2)
    trade.wait_recv()

    lane = lax.broadcasted_iota(jnp.int32, (CHIP, 128), 1)
    low = lax.broadcasted_iota(jnp.int32, (CHIP, 128), 0) < TOK
    mid = slice(MID, MID + CHIP)
    att_grad = mm(branch[...], wo[...], NT).astype(BF)
    dout[mid, :] = att_grad
    both = att_grad.astype(F32) * att[...].astype(F32)
    dots = jnp.zeros((CHIP, 128), F32)
    for h in range(6):
        own = (lane // HEAD) == h % 2
        dot = jnp.sum(jnp.where(own, both[:, (h // 2) * 128 : (h // 2) * 128 + 128], 0.0), axis=1, keepdims=True)
        dots = jnp.where(lane == h, dot, dots)
    stat[REACH, 0:8] = lse[...]
    stat[REACH, 8:16] = dots.T[0:8, :]
    cols[...] = jnp.concatenate([stat[REACH], jnp.zeros((112, CHIP), F32)], axis=0).T

    def window_copies(n):
        m = OFFSETS[n]
        slot = REACH if n < DIRECT else REACH - m // 2
        to = chip_at(e, m if n < DIRECT else m // 2)
        return [
            remote(dout.at[chunk(slot), :], dout.at[chunk(REACH - m), :], send.at[n, 0], recv.at[n, 0], to, j),
            remote(stat.at[slot], stat.at[REACH - m], send.at[n, 1], recv.at[n, 1], to, j),
        ]

    for n in range(DIRECT):
        for c in window_copies(n):
            c.start()
    grad = mm(att[...], branch[...], TN)
    for c in range(6):
        cut = tiles(grad[:, c * 128 : (c + 1) * 128])
        for n, unit, place, count, done in spots(OUT_AT + 24 * c, 24):
            whole[n][unit, place : place + count] = cut[done : done + count]
    for c in loads:
        c.wait()

    def forward_window():
        for n in range(2):
            for c in window_copies(n):
                c.wait_recv()
            for c in window_copies(DIRECT + n):
                c.start()

    line = lax.broadcasted_iota(jnp.int32, (NB, 128), 1)
    row32 = lax.broadcasted_iota(jnp.int32, (NB, 128), 0)
    hot = diagonal_buckets(1)
    bias[...] = jnp.zeros((NB, 128), F32)

    def by_queries(p):
        q = tile(qkv, mid, p * 128, 128).astype(F32) * 0.125
        do = tile(dout, mid, p * 128, 128)
        found = []
        for hh in range(2):
            h = 2 * p + hh
            own = (lane // HEAD) == hh
            spare = (1 - hh) * HEAD
            qm = jnp.where(own, q, 0.0).astype(BF)
            dom = jnp.where(own, do, jnp.zeros_like(do))
            log_sum = cols[:, h : h + 1]
            dot = cols[:, h + 8 : h + 9]
            ends = far_ends(diag, j * 6 + h)
            dq = jnp.zeros((CHIP, 128), F32)
            near_grads = []
            for c in range(SLOTS):
                k = tile(qkv, chunk(c), HALF + p * 128, 128)
                v = tile(qkv, chunk(c), 2 * HALF + p * 128, 128)
                s = biased(mm(qm, k, NT), c, mask, near.at[h], ends)
                ds = jnp.exp(s - log_sum) * (mm(dom, v, NT) - dot)
                if c < REACH - 1:
                    other = lane == spare
                elif c > REACH + 1:
                    other = lane == spare + 1
                elif c == REACH - 1:
                    other = lane == jnp.where(low, spare, spare + 2)
                elif c == REACH + 1:
                    other = lane == jnp.where(low, spare + 3, spare + 1)
                else:
                    other = lane < 0
                other = jnp.where(other, 1.0, 0.0).astype(BF)
                if abs(c - REACH) < 2:
                    near_grads.append(ds)
                dq = dq + mm(ds.astype(BF), jnp.where(own, k, other))
            found.append(dq * 0.125)
            before, same, after = near_grads
            fold = jnp.concatenate(
                [
                    before[0:TOK, TOK:] + same[TOK:, 0:TOK],
                    same[0:TOK, 0:TOK] + same[TOK:, TOK:],
                    same[0:TOK, TOK:] + after[TOK:, 0:TOK],
                    jnp.zeros((TOK, TOK), F32),
                ],
                axis=1,
            )
            rows = TOK
            while rows > 8:
                rows //= 2
                fold = fold[0:rows] + pltpu.roll(fold[rows : 2 * rows], LOOP - rows, 1)
            summed = fold[0:1]
            for n in range(1, 8):
                summed = summed + pltpu.roll(fold[n : n + 1], LOOP - n, 1)
            by_bucket = jnp.sum(hot * summed, axis=1, keepdims=True)
            far_low = jnp.sum(dq[0:TOK], axis=0, keepdims=True)
            far_high = jnp.sum(dq[TOK:], axis=0, keepdims=True)
            far = far_low + far_high
            far_left = far[:, spare : spare + 1] + far_high[:, spare + 2 : spare + 3]
            far_right = far[:, spare + 1 : spare + 2] + far_low[:, spare + 3 : spare + 4]
            by_bucket = by_bucket + jnp.where(row32 == 15, far_left, 0.0) + jnp.where(row32 == 31, far_right, 0.0)
            bias[...] = jnp.where(line == j * 6 + h, by_bucket, bias[...])
        dqkv[:, p * 128 : p * 128 + 128] = jnp.where(lane < HEAD, found[0], found[1]).astype(BF)
        if p == 0:
            forward_window()

    each_pair(by_queries)

    def by_keys(slots, p):
        k_own = tile(qkv, mid, HALF + p * 128, 128)
        v_own = tile(qkv, mid, 2 * HALF + p * 128, 128)
        found = []
        for hh in range(2):
            h = 2 * p + hh
            own = (lane // HEAD) == hh
            km = jnp.where(own, k_own, jnp.zeros_like(k_own))
            vm = jnp.where(own, v_own, jnp.zeros_like(v_own))
            ends = far_ends(diag, 16 + j * 6 + h)
            dk = jnp.zeros((CHIP, 128), F32)
            dv = jnp.zeros((CHIP, 128), F32)
            for c in slots:
                qc = (tile(qkv, chunk(c), p * 128, 128).astype(F32) * 0.125).astype(BF)
                dc = tile(dout, chunk(c), p * 128, 128)
                s = biased(mm(km, qc, NT), c, mask, near.at[6 + h], ends)
                prob = jnp.exp(s - stat[c, pl.ds(h, 1), :])
                ds = prob * (mm(vm, dc, NT) - stat[c, pl.ds(h + 8, 1), :])
                dv = dv + mm(prob.astype(BF), dc)
                dk = dk + mm(ds.astype(BF), qc)
            found.append((dk, dv))
        for n in range(2):
            where = slice(n * HALF + p * 128, n * HALF + p * 128 + 128)
            both = jnp.where(lane < HEAD, found[0][n], found[1][n])
            acc[:, where] = both if REACH in slots else acc[:, where] + both

    for n, slots in ((2, (REACH, 3, 5, 0, 8)), (4, (1, 7, 2, 6))):
        for m in (2, 3) if n == 2 else (4, 5, 6, 7):
            for c in window_copies(m):
                c.wait_recv()
        each_pair(functools.partial(by_keys, slots))
    dqkv[:, HALF:] = acc[...].astype(BF)

    half_out[...] = mm(dqkv[there, :], wqkv[...], NT).astype(BF)
    half_trade = remote(half_out, half_in, core_send.at[2], core_recv.at[2], e, jp)
    half_trade.start()
    swaps = []
    for n, unit, place, count, done in spots(OTHER_AT, MINE):
        swaps.append((done + count, remote(stage.at[done : done + count], whole[n].at[unit, place : place + count], core_send.at[4 + len(swaps)], core_recv.at[4 + len(swaps)], e, jp)))
    sent = 0
    for third in range(3):
        grad = mm(normed[...], dqkv[:, third * HALF : (third + 1) * HALF], TN)
        for c in range(3 * third, 3 * third + 3):
            grads[c % 3] = tiles(grad[:, (c % 3) * 128 : (c % 3 + 1) * 128])
            stage[24 * c : 24 * c + 24] = grads[c % 3, pl.ds(24 * jp, 24)]
            for n, unit, place, count, done in spots(24 * c, 24):
                whole[n][unit, place : place + count] = grads[c % 3, pl.ds(24 * j + done, count)]
        while sent < len(swaps) and swaps[sent][0] <= 72 * (third + 1):
            swaps[sent][1].start()
            sent += 1
    sums[0].start_ring()

    half = mm(dqkv[here, :], wqkv[...], NT)
    half_trade.wait_recv()
    grad = half + half_in[...].astype(F32)
    x = tok[...].astype(F32)
    r = lax.rsqrt(jnp.mean(x * x, axis=-1, keepdims=True) + EPSILON)
    w = grad * both_gains(misc, 16)
    tokens_grad[...] = (hidden_grad[...] + (r * w - x * (r * r * r * jnp.mean(w * x, axis=-1, keepdims=True)))).astype(BF)
    attn_gain = jnp.sum(grad * x * r, axis=0, keepdims=True)
    for h in range(2):
        lines = [v[:, h * HALF + 128 * n : h * HALF + 128 * n + 128] for v in (attn_gain, mix_gain) for n in range(3)]
        small[2 * h] = bias[16 * h : 16 * h + 16, :].astype(BF)
        small[2 * h + 1] = jnp.concatenate(lines + [jnp.zeros((10, 128), F32)], axis=0).astype(BF)
    n, unit, place, end = run(SMALL_AT, 4)
    whole[n][unit, place : place + 2] = small[pl.ds(2 * j, 2)]
    whole[n][unit, end : end + 12] = jnp.zeros((12, 16, 128), BF)
    small_trade = remote(small.at[pl.ds(2 * jp, 2)], whole[n].at[unit, place + 2 : end], core_send.at[3], core_recv.at[3], e, jp)
    small_trade.start()
    for _, c in swaps:
        c.wait_recv()
    sums[2].start_ring()
    router_trade.wait_recv()
    small_trade.wait_recv()
    sums[1].start_ring()
    for step in ("pass_ring", "ring_to_plane", "plane_back", "plane_to_ring", "pass_back", "end"):
        for n in (0, 2, 1):
            getattr(sums[n], step)()

    for c in range(6):
        for n, unit, place, count, done in spots(OUT_AT + 24 * c, 24):
            out_sum[16 * done : 16 * (done + count), c * 128 : (c + 1) * 128] = rows_of_tiles(sums[n].all[unit, place : place + count])
    n, unit, place, end = run(ROUTER_AT, 24)
    mine = sums[n].all[unit, place:end].astype(F32)
    n, unit, place, end = run(ROUTER_AT + 24, 24)
    router_sum[...] = rows_of_tiles(mine + sums[n].all[unit, place:end].astype(F32))
    qkv_sums = (q_sum, k_sum, v_sum)
    for c in range(9):
        for first_tile, core in ((24 * c, j), (OTHER_AT + 24 * c, jp)):
            column = pl.ds(pl.multiple_of(core * HALF + (c % 3) * 128, 128), 128)
            for n, unit, place, count, done in spots(first_tile, 24):
                qkv_sums[c // 3][16 * done : 16 * (done + count), column] = rows_of_tiles(sums[n].all[unit, place : place + count])
    n, unit, place, end = run(SMALL_AT, 4)
    smalls = sums[n].all[unit, place : place + 2].astype(F32) + sums[n].all[unit, place + 2 : end].astype(F32)
    bias_sum[...] = smalls[0]
    gain_sum[...] = smalls[1]

    for c in (trade, router_trade, half_trade, small_trade):
        c.wait_send()
    for _, c in swaps:
        c.wait_send()
    for n in range(len(OFFSETS)):
        for c in window_copies(n):
            c.wait_send()
    for s in sums:
        s.end_sends()


def back(lengths, *operands):
    vm = pl.BlockSpec(memory_space=pltpu.VMEM)
    return pl.pallas_call(
        back_kernel,
        name="back",
        out_shape=(
            jax.ShapeDtypeStruct((TOK, D), BF),
            jax.ShapeDtypeStruct((TOK, D), BF),
            jax.ShapeDtypeStruct((HALF, D), BF),
            jax.ShapeDtypeStruct((HALF, D), BF),
            jax.ShapeDtypeStruct((HALF, D), BF),
            jax.ShapeDtypeStruct((HALF, D), BF),
            jax.ShapeDtypeStruct((HALF, EXPERTS), F32),
            jax.ShapeDtypeStruct((16, 128), F32),
            jax.ShapeDtypeStruct((16, 128), F32),
        ),
        in_specs=[pl.BlockSpec(memory_space=pltpu.SMEM)] + [vm] * 12 + [pl.BlockSpec(memory_space=pl.ANY)] * 3,
        out_specs=(vm,) * 9,
        scratch_shapes=[
            pltpu.VMEM((WIN, 3 * HALF), BF),
            pltpu.VMEM((CHIP, D), BF),
            pltpu.VMEM((D, 3 * HALF), BF),
            pltpu.VMEM((CHIP, WIN), F32),
            pltpu.VMEM((32, LOOP), F32),
            pltpu.VMEM((12, TOK, NEAR), F32),
            pltpu.VMEM((WIN, HALF), BF),
            pltpu.VMEM((SLOTS, 16, CHIP), F32),
            pltpu.VMEM((CHIP, 128), F32),
            pltpu.VMEM((CHIP, 3 * HALF), BF),
            pltpu.VMEM((NB, 128), F32),
            pltpu.VMEM((CHIP, D), BF),
            pltpu.VMEM((TOK, D), F32),
            pltpu.VMEM((TOK, D), BF),
            pltpu.VMEM((TOK, D), BF),
            pltpu.VMEM((3, 48, 16, 128), BF),
            pltpu.VMEM((48, 16, 128), BF),
            pltpu.VMEM((MINE, 16, 128), BF),
            pltpu.VMEM((4, 16, 128), BF),
            pltpu.SemaphoreType.DMA((8, 2)),
            pltpu.SemaphoreType.DMA((8, 2)),
            pltpu.SemaphoreType.DMA((8,)),
            pltpu.SemaphoreType.DMA((8,)),
            pltpu.SemaphoreType.DMA((3,)),
            pltpu.VMEM((CHIP, 2 * HALF), F32),
            *[s for units in UNITS for s in sum_scratch(units)],
        ],
        compiler_params=pltpu.CompilerParams(collective_id=2, has_side_effects=True, vmem_limit_bytes=VMEM_BYTES),
    )(lengths, *operands)


def finish_kernel(*refs):
    sums, (*results, first_gain, second_gain) = refs[:9], refs[9:]
    for src, dst in zip(sums, results):
        dst[...] = src[:, 0 : dst.shape[1]].astype(dst.dtype)
    for first, dst in ((0, first_gain), (3, second_gain)):
        dst[...] = jnp.concatenate([sums[8][first + n : first + n + 1, :] for n in range(3)], axis=1).reshape(HALF)


def finish(*results):
    kinds = ((TOK, D, BF), (TOK, D, BF)) + ((HALF, D, F32),) * 4 + ((HALF, EXPERTS, F32), (16, 12, F32))
    shapes = tuple(jax.ShapeDtypeStruct((r, c), kind) for r, c, kind in kinds)
    vm = pl.BlockSpec(memory_space=pltpu.VMEM)
    return pl.pallas_call(
        finish_kernel,
        name="finish",
        out_shape=shapes + (jax.ShapeDtypeStruct((HALF,), F32),) * 2,
        in_specs=[vm] * 9,
        out_specs=(vm,) * 10,
        compiler_params=pltpu.CompilerParams(vmem_limit_bytes=VMEM_BYTES),
    )(*results)


def to_all(rows):
    return lax.all_to_all(rows, ("expert", "wshard"), split_axis=1, concat_axis=1, tiled=True)


def per_device(tokens, lengths, routes, attn_gain, query_weight, key_weight, value_weight, output_weight, bias_table, mix_gain, router_weight, expert_in, expert_out, cotangent):
    row = routes.reshape(1, TOK)
    qkv, normed, wqkv, router_full, misc_full, att, lse, hidden, mixed, router, sent = front(
        lengths, tokens, query_weight, key_weight, value_weight, output_weight, router_weight, attn_gain, mix_gain, bias_table, row, cotangent
    )

    arrived = to_all(sent).reshape(4 * EXPERTS, D)
    made_back, expert_in_grad, expert_out_grad = expert(arrived, expert_in, expert_out)
    home = to_all(made_back.reshape(4, EXPERTS, D))
    results = back(lengths, home, hidden, mixed, router, row, cotangent, tokens, router_full, misc_full, output_weight, att, lse, qkv, normed, wqkv)
    layer_out, tokens_grad, query_grad, key_grad, value_grad, output_grad, router_grad, bias_grad, attn_gain_grad, mix_gain_grad = finish(*results)
    return (
        layer_out,
        tokens_grad,
        attn_gain_grad,
        query_grad,
        key_grad,
        value_grad,
        output_grad,
        bias_grad,
        mix_gain_grad,
        router_grad,
        expert_in_grad,
        expert_out_grad,
    )


def solution(mesh):
    by_token = P(("expert", "wshard"), None)
    by_row = P("wshard", None)
    by_expert = P(("expert", "wshard"), None, None)
    return jax.shard_map(
        per_device,
        mesh=mesh,
        in_specs=(
            by_token,
            P(),
            by_token,
            P("wshard"),
            by_row,
            by_row,
            by_row,
            by_row,
            by_row,
            P("wshard"),
            by_row,
            by_expert,
            by_expert,
            by_token,
        ),
        out_specs=(
            by_token,
            by_token,
            P("wshard"),
            by_row,
            by_row,
            by_row,
            by_row,
            by_row,
            P("wshard"),
            by_row,
            by_expert,
            by_expert,
        ),
        check_vma=False,
    )
```
